32 devices in a mesh: aux: 2 (over core), occ: 16 (over z, y, x).
Axes of the slice: x: 2, y: 2, z: 4, core: 2. Of those that a mesh axis runs over, the one named last changes fastest.
Arguments:
- factors: float32 [2048, 16, 512], P('aux', 'occ'), may hold values from -0.3 to 0.3
- eps_occ: float32 [16], P('occ'), may hold values from -2 to -0.3
- eps_virt: float32 [512], replicated, may hold values from 0.2 to 3
- pair_mask: int32 [16, 4], P('occ'), may hold values 0 or 1
Outputs:
- gradient: float32 [2048, 16, 512], P('aux', 'occ')
The draws below stay inside these ranges and needn't reach their ends.
Inputs may be any that keep to these rules, and one draw needn't show every extreme that they name: `pair_mask`: 1 marks a surviving pair.
All inputs are finite; a program needn't handle non-finite values. No bound on the sum of `pair_mask` on one device may be relied on, other than what follows from the above.
Results may differ from the reference program's by a relative error of at most 0.0003.
Values sent between devices are 32-bit elements; how exact they have to be, the bound alone decides.
No kernel may reach another device: no remote copies, remote signals or barrier semaphores. Data moves between devices by JAX's collectives and lax.ppermute only.
A program may use at most 128 MiB of HBM per device.

```python
import jax
import jax.numpy as jnp
from jax import lax

VIRT = 512
OCC_DEV = 1
OFFSETS = 4
NAUX = 2048
NOCC = 16
N_OCC = 16


def place_ends(result, stream_key, least, largest):
    shape = result.shape
    place = [jax.random.randint(jax.random.fold_in(stream_key, axis), (), 0, shape[axis]) for axis in range(len(shape))]
    result = result.at[tuple(place)].set(least)
    longest = shape.index(max(shape))
    place[longest] = (place[longest] + 1) % shape[longest]
    return result.at[tuple(place)].set(largest)


def levels(rng, shape, shards, smallest, high):
    factor_of, own = 1.0, jax.random.fold_in(rng, 6)
    for axis_at, blocks in shards:
        steps = jnp.exp(jax.random.uniform(jax.random.fold_in(own, axis_at), (blocks,), jnp.float32, smallest / len(shards), high / len(shards)))
        factor_of = factor_of * jnp.repeat(steps, shape[axis_at] // blocks).reshape([-1 if axis == axis_at else 1 for axis in range(len(shape))])
    return factor_of


def scatter_about(stream_key, extent, deviation, bound, shards=(), kind=jnp.bfloat16):
    drawn = jax.random.normal(stream_key, extent, jnp.float32) * deviation
    if len(shards) > 0:
        drawn = levels(stream_key, extent, shards, -0.22, 0.18) * drawn
    return jnp.clip(drawn, min=-bound, max=bound).astype(kind)


def setup_inputs(seed: int = 0) -> dict:
    arg_keys = jax.random.split(jax.random.key(seed), 5)
    factors = scatter_about(arg_keys[0], (NAUX, NOCC, VIRT), 0.05, 0.3, ((0, 2), (1, 16)), jnp.float32)
    eps_occ = jnp.clip(-2.0 + 1.7 * jax.random.uniform(arg_keys[1], (NOCC,), jnp.float32) ** levels(arg_keys[1], (NOCC,), ((0, 16),), -0.2, 0.2), -2.0, -0.3)
    eps_virt = jnp.clip(jax.random.uniform(arg_keys[2], (VIRT,), jnp.float32, 0.2, 3.0), 0.2, 3.0)
    pair_mask = place_ends((jax.random.randint(arg_keys[3], (N_OCC, OFFSETS), 0, 4) < 3).astype(jnp.int32), jax.random.fold_in(arg_keys[3], 1), 0, 1)
    return {"factors": factors, "eps_occ": eps_occ, "eps_virt": eps_virt, "pair_mask": pair_mask}


def reference(factors, eps_occ, eps_virt, pair_mask):
    width = OCC_DEV * VIRT
    blocks = factors.reshape(NAUX, N_OCC, width)
    energies = (eps_virt[None, None, :] - eps_occ.reshape(N_OCC, OCC_DEV)[:, :, None]).reshape(N_OCC, width)

    def group(index):
        resident = lax.dynamic_index_in_dim(blocks, index, 1, keepdims=False)
        total = jnp.zeros((NAUX, width), jnp.float32)
        for offset in range(OFFSETS + 1):
            source = jnp.maximum(index - offset, 0).astype(jnp.int32)
            visitor = lax.dynamic_index_in_dim(blocks, source, 1, keepdims=False)
            if offset == 0:
                live = jnp.array(True)
            else:
                live = (index >= offset) & (pair_mask[index, offset - 1] > 0)
            integrals = lax.dot_general(resident, visitor, (((0,), (0,)), ((), ())), precision=lax.Precision.HIGHEST, preferred_element_type=jnp.float32)
            row_energy = lax.dynamic_index_in_dim(energies, index, 0, keepdims=False)
            col_energy = lax.dynamic_index_in_dim(energies, source, 0, keepdims=False)
            amplitude = -integrals / (row_energy[:, None] + col_energy[None, :])
            added = lax.dot_general(visitor, amplitude, (((1,), (1,)), ((), ())), precision=lax.Precision.HIGHEST, preferred_element_type=jnp.float32)
            total = total + jnp.where(live, added, jnp.zeros_like(added))
        return total

    stacked = lax.map(group, jnp.arange(N_OCC, dtype=jnp.int32))
    return stacked.transpose(1, 0, 2).reshape(NAUX, NOCC, VIRT)
```

```python
import functools

import jax
import jax.numpy as jnp
from jax import lax
from jax.experimental import pallas as pl
from jax.experimental.pallas import tpu as pltpu
from jax.sharding import PartitionSpec as P

LANES = 128
PLANE = 4
CHUNKS = 4
VMEM_LIMIT = 40 * 1024 * 1024
NN = (((1,), (0,)), ((), ()))


def split(value):
    high = value.astype(jnp.bfloat16)
    low = (value - high.astype(jnp.float32)).astype(jnp.bfloat16)
    return high, low


def product(left, right):
    def dot(a, b):
        return lax.dot_general(a, b, NN, preferred_element_type=jnp.float32)

    return dot(left[0], right[0]) + (dot(left[0], right[1]) + dot(left[1], right[0]))


def rows_of(refs, start, count, width):
    lines = width // LANES
    columns = []
    for column in range(lines):
        parts = [ref[pl.ds(start * lines + column, count, stride=lines), :] for ref in refs]
        columns.append(functools.reduce(jnp.add, parts))
    return jnp.concatenate(columns, axis=1)


def call(kernel, inputs, outputs, scratch=(), flops=0, smem=()):
    specs = [pl.BlockSpec(memory_space=pltpu.SMEM)] * len(smem)
    specs += [pl.BlockSpec(memory_space=pltpu.VMEM)] * len(inputs)
    moved = sum(a.size * a.dtype.itemsize for a in (*inputs, *outputs))
    return pl.pallas_call(
        kernel,
        out_shape=outputs,
        in_specs=specs,
        out_specs=[pl.BlockSpec(memory_space=pltpu.VMEM)] * len(outputs),
        scratch_shapes=list(scratch),
        compiler_params=pltpu.CompilerParams(vmem_limit_bytes=VMEM_LIMIT),
        cost_estimate=pl.CostEstimate(flops=flops, bytes_accessed=moved, transcendentals=0),
    )(*smem, *inputs)


def prepare(own, rows, width):
    def kernel(own_ref, high_ref, low_ref, integrals_ref):
        tile = min(256, rows)
        integrals_ref[...] = jnp.zeros_like(integrals_ref)

        def step(at, _):
            start = pl.multiple_of(at * tile, tile)
            block = rows_of([own_ref], start, tile, width)
            turned = split(block.T)
            high_ref[:, pl.ds(start, tile)] = turned[0]
            low_ref[:, pl.ds(start, tile)] = turned[1]
            integrals_ref[...] += product(turned, split(block))
            return 0

        lax.fori_loop(0, rows // tile, step, 0)

    half = jax.ShapeDtypeStruct((width, rows), jnp.bfloat16)
    square = jax.ShapeDtypeStruct((width, width), jnp.float32)
    return call(kernel, [own], [half, half, square], flops=6 * rows * width * width)


def integrate(high, low, slots, first, size, width, before=None):
    count = len(slots)
    chunks = len(slots[0])
    flat = [array for slot in slots for chunk in slot for array in chunk]
    inputs = [high, low] + flat + ([before] if before is not None else [])

    def kernel(*refs):
        high_ref, low_ref = refs[:2]
        given = iter(refs[2 : 2 + len(flat)])
        out_ref = refs[-1]
        for slot in range(count):
            total = None
            for at in range(chunks):
                parts = [next(given) for _ in slots[slot][at]]
                where = pl.ds((first + at) * size, size)
                left = (high_ref[:, where], low_ref[:, where])
                value = product(left, split(rows_of(parts, 0, size, width)))
                total = value if total is None else total + value
            if before is not None:
                total = total + refs[-2][slot]
            out_ref[slot] = total

    out = jax.ShapeDtypeStruct((count, width, width), jnp.float32)
    return call(kernel, inputs, [out], flops=6 * count * chunks * size * width * width)[0]


def contract(partials, slots, signs, row_energy, col_energy, rows, size, width, before=None):
    count = len(slots)
    chunks = len(slots[0])
    lines = width // LANES
    summed = [array for slot in partials for array in slot]
    flat = [array for slot in slots for chunk in slot for array in chunk]
    inputs = [row_energy, col_energy] + summed + flat + ([before] if before is not None else [])

    def kernel(sign_ref, row_ref, col_ref, *refs):
        given = iter(refs)
        sums = [[next(given) for _ in slot] for slot in partials]
        visitors = [[[next(given) for _ in chunk] for chunk in slot] for slot in slots]
        before_ref = next(given) if before is not None else None
        out_ref, high_ref, low_ref = refs[-3:]
        for slot in range(count):
            total = functools.reduce(jnp.add, [ref[...] for ref in sums[slot]])
            energy = row_ref[...] + col_ref[slot : slot + 1, :]
            amplitude = (sign_ref[slot] * total) / energy
            high_ref[slot], low_ref[slot] = split(amplitude.T)
        tile = min(256, size)
        for at in range(chunks):
            for start in range(0, size, tile):
                value = None
                for slot in range(count):
                    block = split(rows_of(visitors[slot][at], start, tile, width))
                    term = product(block, (high_ref[slot], low_ref[slot]))
                    value = term if value is None else value + term
                base = (at * size + start) * lines
                for column in range(lines):
                    lanes = value[:, column * LANES : (column + 1) * LANES]
                    where = pl.ds(base + column, tile, stride=lines)
                    if before_ref is not None:
                        lanes = lanes + before_ref[where, :]
                    out_ref[where, :] = lanes

    out = jax.ShapeDtypeStruct((rows * lines, LANES), jnp.float32)
    held = pltpu.VMEM((count, width, width), jnp.bfloat16)
    flops = 6 * count * rows * width * width
    return call(kernel, inputs, [out], [held, held], flops, [signs])[0]


def on_device(factors, eps_occ, eps_virt, pair_mask):
    rows, occ_rows, virt = factors.shape
    width = occ_rows * virt
    lines = width // LANES
    groups = lax.axis_size("occ")
    shares = lax.axis_size("aux")
    offsets = pair_mask.shape[1]
    size = rows // CHUNKS
    group = lax.axis_index("occ")
    place = group % PLANE

    own = factors.reshape(rows * lines, LANES)
    own_parts = [own[at * size * lines : (at + 1) * size * lines] for at in range(CHUNKS)]

    def swap(block, bit):
        return lax.ppermute(block, "occ", [(g, g ^ bit) for g in range(groups)])

    def up(block):
        return lax.ppermute(block, "occ", [(g, g + PLANE) for g in range(groups - PLANE)])

    def summed(partial):
        if shares == 2:
            return [partial, lax.ppermute(partial, "aux", [(0, 1), (1, 0)])]
        return [lax.psum(partial, "aux")]

    every_eps = lax.all_gather(eps_occ, "occ", tiled=True).reshape(groups, occ_rows)

    def flat_energy(eps_group):
        return (eps_virt[None, :] - eps_group[:, None]).reshape(width)

    row_energy = flat_energy(eps_occ)[:, None]

    def slot_terms(offset):
        source = jnp.maximum(group - offset, 0)
        energy = flat_energy(lax.dynamic_index_in_dim(every_eps, source, 0, keepdims=False))
        flag = lax.dynamic_index_in_dim(pair_mask[0], offset - 1, 0, keepdims=False)
        live = (group >= offset) & (flag > 0)
        return energy, jnp.where(live, -1.0, 0.0).astype(jnp.float32)

    odd_x = place % 2 == 1
    odd_y = place // 2 == 1
    slot_z = slot_terms(PLANE)
    slot_x = slot_terms(jnp.where(odd_x, 1, PLANE - 1))
    slot_y = slot_terms(jnp.int32(PLANE // 2))
    slot_d = slot_terms(jnp.where(odd_x, PLANE - 1, 1))

    from_z, from_x, from_y, from_d = [], [], [], []
    for at in range(CHUNKS):
        from_z.append(up(own_parts[at]))
        from_x.append(swap(jnp.where(odd_x, from_z[at], own_parts[at]), 1))
        from_y.append(swap(jnp.where(odd_y, from_z[at], own_parts[at]), 2))
        from_d.append(swap(from_y[at], 1))

    high, low, own_partial = prepare(own, rows, width)
    own_sum = summed(own_partial)

    def chunks_of(blocks):
        return [[block] for block in blocks]

    def terms(*slots):
        return jnp.stack([s[1] for s in slots]), jnp.stack([s[0] for s in slots])

    partial_z = integrate(high, low, [chunks_of(from_z)], 0, size, width)
    sum_z = [part[0] for part in summed(partial_z)]
    slot_own = (flat_energy(eps_occ), jnp.float32(-1.0))
    signs, col_energy = terms(slot_own, slot_z)
    gradient = contract(
        [own_sum, sum_z], [chunks_of(own_parts), chunks_of(from_z)], signs, row_energy, col_energy, rows, size, width
    )

    last = CHUNKS - 1
    partial = integrate(high, low, [chunks_of(from_x[:last]), chunks_of(from_y[:last])], 0, size, width)
    partial = integrate(high, low, [chunks_of(from_x[last:]), chunks_of(from_y[last:])], last, size, width, partial)
    both = summed(partial)
    signs, col_energy = terms(slot_x, slot_y)
    gradient = contract(
        [[part[slot] for part in both] for slot in range(2)],
        [chunks_of(from_x), chunks_of(from_y)], signs, row_energy, col_energy, rows, size, width, gradient,
    )

    partial = integrate(high, low, [chunks_of(from_d[:last])], 0, size, width)
    partial = integrate(high, low, [chunks_of(from_d[last:])], last, size, width, partial)
    sum_d = [part[0] for part in summed(partial)]
    signs, col_energy = terms(slot_d)
    gradient = contract(
        [sum_d], [chunks_of(from_d)], signs, row_energy, col_energy, rows, size, width, gradient
    )
    return gradient.reshape(rows, occ_rows, virt)


def solution(mesh):
    if mesh.shape["occ"] % PLANE:
        raise ValueError("incomplete plane")
    in_specs = (P("aux", "occ", None), P("occ"), P(), P("occ", None))
    out_specs = P("aux", "occ", None)
    return jax.shard_map(
        on_device, mesh=mesh, in_specs=in_specs, out_specs=out_specs, check_vma=False
    )
```

```python
import functools

import jax
import jax.numpy as jnp
from jax import lax
from jax.experimental import pallas as pl
from jax.experimental.pallas import tpu as pltpu
from jax.sharding import PartitionSpec as P

LANES = 128
SUBLANES = 8
PLANE = 4
CHUNKS = 4
VMEM_LIMIT = 40 * 1024 * 1024
NN = (((1,), (0,)), ((), ()))


def split(value):
    high = value.astype(jnp.bfloat16)
    low = (value - high.astype(jnp.float32)).astype(jnp.bfloat16)
    return high, low


def product(left, right):
    def dot(a, b):
        return lax.dot_general(a, b, NN, preferred_element_type=jnp.float32)

    return dot(left[0], right[0]) + (dot(left[0], right[1]) + dot(left[1], right[0]))


def rows_of(ref, base, start, count, width):
    lines = width // LANES
    first = base + start * lines
    columns = [ref[pl.ds(first + at, count, stride=lines), :] for at in range(lines)]
    return jnp.concatenate(columns, axis=1)


def distinct(slots):
    return list({id(array): array for slot in slots for array, _ in slot}.values())


def call(kernel, inputs, outputs, scratch=(), flops=0, smem=()):
    specs = [pl.BlockSpec(memory_space=pltpu.SMEM)] * len(smem)
    specs += [pl.BlockSpec(memory_space=pltpu.VMEM)] * len(inputs)
    moved = sum(a.size * a.dtype.itemsize for a in (*inputs, *outputs))
    return pl.pallas_call(
        kernel,
        out_shape=outputs,
        in_specs=specs,
        out_specs=[pl.BlockSpec(memory_space=pltpu.VMEM)] * len(outputs),
        scratch_shapes=list(scratch),
        compiler_params=pltpu.CompilerParams(vmem_limit_bytes=VMEM_LIMIT),
        cost_estimate=pl.CostEstimate(flops=flops, bytes_accessed=moved, transcendentals=0),
    )(*smem, *inputs)


def prepare(own, rows, width):
    def kernel(own_ref, high_ref, low_ref, integrals_ref):
        tile = min(256, rows)
        integrals_ref[...] = jnp.zeros_like(integrals_ref)

        def step(at, _):
            start = pl.multiple_of(at * tile, tile)
            block = rows_of(own_ref, 0, start, tile, width)
            turned = split(block.T)
            high_ref[:, pl.ds(start, tile)] = turned[0]
            low_ref[:, pl.ds(start, tile)] = turned[1]
            integrals_ref[...] += product(turned, split(block))
            return 0

        lax.fori_loop(0, rows // tile, step, 0)

    half = jax.ShapeDtypeStruct((width, rows), jnp.bfloat16)
    square = jax.ShapeDtypeStruct((width, width), jnp.float32)
    return call(kernel, [own], [half, half, square], flops=6 * rows * width * width)


def integrate(turned, slots, first, size, width, before=()):
    count = len(slots)
    flat = distinct(slots)
    before = list(before)

    def kernel(high_ref, low_ref, *refs):
        ref_of = {id(array): ref for array, ref in zip(flat, refs)}
        before_refs = refs[len(flat) : len(flat) + len(before)]
        outs = refs[len(flat) + len(before) :]
        for slot in range(count):
            total = before_refs[slot][...] if before else None
            for number, (array, base) in enumerate(slots[slot], first[slot]):
                where = pl.ds(number * size, size)
                left = (high_ref[:, where], low_ref[:, where])
                value = product(left, split(rows_of(ref_of[id(array)], base, 0, size, width)))
                total = value if total is None else total + value
            outs[slot][...] = total

    out = [jax.ShapeDtypeStruct((width, width), jnp.float32)] * count
    flops = 6 * sum(map(len, slots)) * size * width * width
    return call(kernel, [*turned, *flat, *before], out, flops=flops)


def contract(partials, slots, signs, eps_own, eps_virt, size, before=None):
    count = len(slots)
    chunks = len(slots[0])
    virt = eps_virt.shape[1]
    occ_rows = eps_own.shape[0]
    width = occ_rows * virt
    lines = width // LANES
    summed = [array for slot in partials for array in slot]
    flat = distinct(slots)
    inputs = [eps_virt] + summed + flat + ([before] if before is not None else [])

    def kernel(sign_ref, own_ref, virt_ref, *refs):
        given = iter(refs)
        sums = [[next(given) for _ in slot] for slot in partials]
        ref_of = {id(array): next(given) for array in flat}
        before_ref = next(given) if before is not None else None
        out_ref, high_ref, low_ref = refs[-3:]
        virtual = virt_ref[...]
        row = jnp.concatenate([virtual - own_ref[i] for i in range(occ_rows)], axis=1)
        row = jnp.broadcast_to(row, (SUBLANES, width)).T[:, :1]
        for slot in range(count):
            total = functools.reduce(jnp.add, [ref[...] for ref in sums[slot]])
            array, base = slots[slot][0]
            at = base + size * lines
            line = ref_of[id(array)][at : at + 1, :]
            column = jnp.concatenate([virtual - line[:, j : j + 1] for j in range(occ_rows)], axis=1)
            amplitude = (sign_ref[slot] * total) / (row + column)
            high_ref[slot], low_ref[slot] = split(amplitude.T)
        tile = min(256, size)
        for at in range(chunks):
            for start in range(0, size, tile):
                value = None
                for slot in range(count):
                    array, base = slots[slot][at]
                    block = split(rows_of(ref_of[id(array)], base, start, tile, width))
                    term = product(block, (high_ref[slot], low_ref[slot]))
                    value = term if value is None else value + term
                base = (at * size + start) * lines
                for column in range(lines):
                    lanes = value[:, column * LANES : (column + 1) * LANES]
                    where = pl.ds(base + column, tile, stride=lines)
                    if before_ref is not None:
                        lanes = lanes + before_ref[where, :]
                    out_ref[where, :] = lanes

    rows = chunks * size
    out = jax.ShapeDtypeStruct((rows * lines, LANES), jnp.float32)
    held = pltpu.VMEM((count, width, width), jnp.bfloat16)
    flops = 6 * count * rows * width * width
    return call(kernel, inputs, [out], [held, held], flops, [signs, eps_own])[0]


def after(block, *others):
    return lax.optimization_barrier((block, *others))[0]


def on_device(factors, eps_occ, eps_virt, pair_mask):
    rows, occ_rows, virt = factors.shape
    width = occ_rows * virt
    lines = width // LANES
    groups = lax.axis_size("occ")
    shares = lax.axis_size("aux")
    size = rows // CHUNKS
    last = CHUNKS - 1
    group = lax.axis_index("occ")
    place = group % PLANE
    odd_x = place % 2 == 1
    odd_y = place // 2 == 1

    own = factors.reshape(rows * lines, LANES)
    energies = jnp.zeros((SUBLANES * LANES,), jnp.float32).at[:occ_rows].set(eps_occ)
    energies = energies.reshape(SUBLANES, LANES)

    def part(whole, at):
        block = whole[at * size * lines : (at + 1) * size * lines]
        return jnp.concatenate([block, energies]) if at == 0 else block

    def swap(block, bit):
        return lax.ppermute(block, "occ", [(g, g ^ bit) for g in range(groups)])

    def up(block):
        return lax.ppermute(block, "occ", [(g, g + PLANE) for g in range(groups - PLANE)])

    def totals(partial):
        if shares == 2:
            return [partial, lax.ppermute(partial, "aux", [(0, 1), (1, 0)])]
        return [lax.psum(partial, "aux")]

    def sign(offset):
        flag = lax.dynamic_index_in_dim(pair_mask[0], offset - 1, 0, keepdims=False)
        return jnp.where((group >= offset) & (flag > 0), -1.0, 0.0).astype(jnp.float32)

    sign_own = jnp.float32(-1.0)
    sign_z = sign(jnp.int32(PLANE))
    sign_x = sign(jnp.where(odd_x, 1, PLANE - 1))
    sign_y = sign(jnp.int32(PLANE // 2))
    sign_d = sign(jnp.where(odd_x, PLANE - 1, 1))

    def add(partials, slots, signs, before=None):
        return contract(partials, slots, jnp.stack(signs), eps_occ, eps_virt[None, :], size, before)

    from_z, from_x, from_y, from_d = [], [], [], []
    from_z.append(up(part(own, 0)))
    high, low, partial_own = prepare(own, rows, width)
    turned = (high, low)
    sums_own = totals(partial_own)
    ready = [partial_own]
    for at in range(CHUNKS):
        send_x = after(jnp.where(odd_x, from_z[at], part(own, at)), *ready)
        send_y = jnp.where(odd_y, from_z[at], part(own, at))
        from_x.append(swap(send_x, 1))
        from_y.append(swap(send_y, 2))
        if at < last:
            from_z.append(up(part(after(own, from_z[at]), at + 1)))
        ready = [from_x[at]]
        from_d.append(swap(after(from_y[at], from_d[at - 1] if at else from_x[0]), 1))

    cut = size * lines
    slot_own = [(part(own, 0), 0)] + [(own, at * cut) for at in range(1, CHUNKS)]
    slot_z, slot_x, slot_y, slot_d = (
        [(block, 0) for block in blocks] for blocks in (from_z, from_x, from_y, from_d)
    )

    (partial_z,) = integrate(turned, [slot_z], [0], size, width)
    gradient = add([sums_own, totals(partial_z)], [slot_own, slot_z], [sign_own, sign_z])
    turned = after(turned, gradient)
    early = integrate(
        turned, [slot_x[:last], slot_y[:last], slot_d[: last - 1]], [0, 0, 0], size, width
    )
    partial_x, partial_y, partial_d = integrate(
        turned, [slot_x[last:], slot_y[last:], slot_d[last - 1 : last]], [last, last, last - 1], size, width, early
    )
    (partial_d,) = integrate(turned, [slot_d[last:]], [last], size, width, [partial_d])
    gradient = add(
        [totals(partial_x), totals(partial_y), totals(partial_d)],
        [slot_x, slot_y, slot_d], [sign_x, sign_y, sign_d], gradient,
    )
    return gradient.reshape(rows, occ_rows, virt)


def solution(mesh):
    if mesh.shape["occ"] % PLANE:
        raise ValueError("incomplete plane")
    in_specs = (P("aux", "occ", None), P("occ"), P(), P("occ", None))
    out_specs = P("aux", "occ", None)
    return jax.shard_map(
        on_device, mesh=mesh, in_specs=in_specs, out_specs=out_specs, check_vma=False
    )
```

```python
import functools

import jax
import jax.numpy as jnp
from jax import lax
from jax.experimental import pallas as pl
from jax.experimental.pallas import tpu as pltpu
from jax.sharding import PartitionSpec as P

LANES = 128
SUBLANES = 8
PLANE = 4
CHUNKS = 4
VMEM_LIMIT = 16 * 1024 * 1024
NN = (((1,), (0,)), ((), ()))


def split(value):
    high = value.astype(jnp.bfloat16)
    low = (value - high.astype(jnp.float32)).astype(jnp.bfloat16)
    return high, low


def deep_left(value):
    high, low = split(value)
    return jnp.concatenate([high, low, high], axis=1)


def deep_right(value):
    high, low = split(value)
    return jnp.concatenate([high, high, low], axis=0)


def dot(left, right):
    return lax.dot_general(left, right, NN, preferred_element_type=jnp.float32)


def rows_of(places, start, count, width):
    lines = width // LANES
    columns = []
    for at in range(lines):
        parts = [ref[pl.ds(base + start * lines + at, count, stride=lines), :] for ref, base in places]
        columns.append(functools.reduce(jnp.add, parts))
    return jnp.concatenate(columns, axis=1)


def distinct(slots):
    return list({id(array): array for slot in slots for chunk in slot for array, _ in chunk}.values())


def located(chunk, ref_of):
    return [(ref_of[id(array)], base) for array, base in chunk]


def call(kernel, inputs, outputs, scratch=(), flops=0, smem=()):
    specs = [pl.BlockSpec(memory_space=pltpu.SMEM)] * len(smem)
    specs += [pl.BlockSpec(memory_space=pltpu.VMEM)] * len(inputs)
    moved = sum(a.size * a.dtype.itemsize for a in (*inputs, *outputs))
    return pl.pallas_call(
        kernel,
        out_shape=outputs,
        in_specs=specs,
        out_specs=[pl.BlockSpec(memory_space=pltpu.VMEM)] * len(outputs),
        scratch_shapes=list(scratch),
        compiler_params=pltpu.CompilerParams(vmem_limit_bytes=VMEM_LIMIT),
        cost_estimate=pl.CostEstimate(flops=flops, bytes_accessed=moved, transcendentals=0),
    )(*smem, *inputs)


def prepare(own, rows, width):
    def kernel(own_ref, high_ref, low_ref, integrals_ref):
        tile = min(256, rows)
        integrals_ref[...] = jnp.zeros_like(integrals_ref)

        def step(at, _):
            start = pl.multiple_of(at * tile, tile)
            block = rows_of([(own_ref, 0)], start, tile, width)
            high, low = split(block.T)
            high_ref[:, pl.ds(start, tile)] = high
            low_ref[:, pl.ds(start, tile)] = low
            left = jnp.concatenate([high, low, high], axis=1)
            integrals_ref[...] += dot(left, deep_right(block))
            return 0

        lax.fori_loop(0, rows // tile, step, 0)

    half = jax.ShapeDtypeStruct((width, rows), jnp.bfloat16)
    square = jax.ShapeDtypeStruct((width, width), jnp.float32)
    return call(kernel, [own], [half, half, square], flops=6 * rows * width * width)


def integrate(turned, slots, first, size, width, before=()):
    count = len(slots)
    flat = distinct(slots)
    before = list(before)

    def kernel(high_ref, low_ref, *refs):
        ref_of = {id(array): ref for array, ref in zip(flat, refs)}
        before_refs = refs[len(flat) : len(flat) + len(before)]
        outs = refs[len(flat) + len(before) :]
        for slot in range(count):
            left, right = [], []
            for number, chunk in enumerate(slots[slot], first[slot]):
                where = pl.ds(number * size, size)
                high, low = high_ref[:, where], low_ref[:, where]
                left.append(jnp.concatenate([high, low, high], axis=1))
                right.append(deep_right(rows_of(located(chunk, ref_of), 0, size, width)))
            total = dot(jnp.concatenate(left, axis=1), jnp.concatenate(right, axis=0))
            outs[slot][...] = total + before_refs[slot][...] if before else total

    out = [jax.ShapeDtypeStruct((width, width), jnp.float32)] * count
    flops = 6 * sum(map(len, slots)) * size * width * width
    return call(kernel, [*turned, *flat, *before], out, flops=flops)


def contract(partials, slots, signs, energies, eps_virt, size, before=None):
    count = len(slots)
    chunks = len(slots[0])
    virt = eps_virt.shape[1]
    occ_rows = energies[0].shape[0]
    width = occ_rows * virt
    lines = width // LANES
    summed = [array for slot in partials for array in slot]
    flat = distinct(slots)
    inputs = [eps_virt] + summed + flat + ([before] if before is not None else [])

    def kernel(sign_ref, *refs):
        energy_refs, virt_ref, refs = refs[: count + 1], refs[count + 1], refs[count + 2 :]
        given = iter(refs)
        sums = [[next(given) for _ in slot] for slot in partials]
        ref_of = {id(array): next(given) for array in flat}
        before_ref = next(given) if before is not None else None
        out_ref, right_ref = refs[-2:]

        def line(ref):
            virtual = virt_ref[...]
            return jnp.concatenate([virtual - ref[i] for i in range(occ_rows)], axis=1)

        row = jnp.broadcast_to(line(energy_refs[0]), (SUBLANES, width)).T[:, :1]
        for slot in range(count):
            total = functools.reduce(jnp.add, [ref[...] for ref in sums[slot]])
            amplitude = (sign_ref[slot] * total) / (row + line(energy_refs[slot + 1]))
            right_ref[pl.ds(slot * 3 * width, 3 * width), :] = deep_right(amplitude.T)
        tile = min(256, size)
        for at in range(chunks):
            for start in range(0, size, tile):
                left = []
                for slot in range(count):
                    left.append(deep_left(rows_of(located(slots[slot][at], ref_of), start, tile, width)))
                value = dot(jnp.concatenate(left, axis=1), right_ref[...])
                base = (at * size + start) * lines
                for column in range(lines):
                    lanes = value[:, column * LANES : (column + 1) * LANES]
                    where = pl.ds(base + column, tile, stride=lines)
                    if before_ref is not None:
                        lanes = lanes + before_ref[where, :]
                    out_ref[where, :] = lanes

    rows = chunks * size
    out = jax.ShapeDtypeStruct((rows * lines, LANES), jnp.float32)
    held = pltpu.VMEM((count * 3 * width, width), jnp.bfloat16)
    flops = 6 * count * rows * width * width
    return call(kernel, inputs, [out], [held], flops, [signs, *energies])[0]


def after(block, *others):
    return lax.optimization_barrier((block, *others))[0]


def on_device(factors, eps_occ, eps_virt, pair_mask):
    rows, occ_rows, virt = factors.shape
    width = occ_rows * virt
    lines = width // LANES
    groups = lax.axis_size("occ")
    shares = lax.axis_size("aux")
    size = rows // CHUNKS
    cut = size * lines
    half = CHUNKS // 2
    group = lax.axis_index("occ")
    place = group % PLANE
    odd_x = place % 2 == 1

    own = factors.reshape(rows * lines, LANES)

    def shifted(block, offset):
        return lax.ppermute(block, "occ", [(g, g + offset) for g in range(groups - offset)])

    def within(block, moves, first_plane=0):
        planes = range(first_plane * PLANE, groups, PLANE)
        return lax.ppermute(block, "occ", [(g + a, g + b) for g in planes for a, b in moves])

    def totals(partial):
        if shares == 2:
            return [partial, lax.ppermute(partial, "aux", [(0, 1), (1, 0)])]
        return [lax.psum(partial, "aux")]

    def sign(offset):
        flag = lax.dynamic_index_in_dim(pair_mask[0], offset - 1, 0, keepdims=False)
        return jnp.where((group >= offset) & (flag > 0), -1.0, 0.0).astype(jnp.float32)

    def add(partials, slots, signs, energies, before=None):
        return contract(partials, slots, jnp.stack(signs), [eps_occ, *energies], eps_virt[None, :], size, before)

    parts = [slice(0, half * cut), slice(half * cut, CHUNKS * cut)]
    from_z = [shifted(own[:cut], PLANE)]
    eps_of = [shifted(eps_occ, offset) for offset in range(1, PLANE + 1)]
    own_d = within(own[parts[0]], [(1, 2)])
    own_x = [within(own[parts[0]], [(0, 1), (2, 3)])]
    own_y = [within(own[parts[0]], [(0, 2), (1, 3)])]
    high, low, partial_own = prepare(own, rows, width)
    turned = (high, low)
    sums_own = totals(partial_own)

    from_x, from_y = [], []
    for at in range(CHUNKS):
        from_x.append(within(from_z[at], [(1, 0), (3, 2)], 1))
        from_y.append(within(from_z[at], [(2, 0), (3, 1)], 1))
        if at == 0:
            mine = after(own, from_z[0], partial_own, *eps_of)
        if at == 1:
            mine = after(own, from_z[1], from_y[0], own_d, own_x[0], own_y[0])
            own_x.append(within(mine[parts[1]], [(0, 1), (2, 3)]))
            own_y.append(within(mine[parts[1]], [(0, 2), (1, 3)]))
        if at == 2:
            mine = after(own, from_z[2], from_y[1], from_x[0])
        if at + 1 < CHUNKS:
            from_z.append(shifted(mine[(at + 1) * cut : (at + 2) * cut], PLANE))
    own_d_x = within(own_x[0], [(1, 3)])
    own_d_y = within(own_y[1], [(2, 3), (3, 2)])
    from_d = []
    for at in range(CHUNKS):
        sent = after(from_y[at], *(from_d[at - 1] if 0 < at <= half else []))
        if at < half:
            from_d.append([within(sent, [(0, 1), (1, 0)], 1)])
        else:
            from_d.append([within(sent, [(0, 1)], 1), within(from_x[at], [(2, 0)], 1)])

    def half_of(pieces, at):
        return pieces[at // half], (at % half) * cut

    slot_own = [[(own, at * cut)] for at in range(CHUNKS)]
    slot_z = [[(from_z[at], 0)] for at in range(CHUNKS)]
    slot_x = [[half_of(own_x, at), (from_x[at], 0)] for at in range(CHUNKS)]
    slot_y = [[half_of(own_y, at), (from_y[at], 0)] for at in range(CHUNKS)]
    slot_d = [[(own_d, at * cut), (own_d_x, at * cut), (from_d[at][0], 0)] for at in range(half)]
    slot_d += [
        [(own_d_y, (at - half) * cut), (from_d[at][0], 0), (from_d[at][1], 0)] for at in range(half, CHUNKS)
    ]

    def chosen(offset):
        return jnp.where(odd_x, eps_of[offset], eps_of[PLANE - 2 - offset])

    offset_x = jnp.where(odd_x, 1, PLANE - 1)
    offset_d = PLANE - offset_x

    last = CHUNKS - 1
    (partial_z,) = integrate(after(turned, own_x[1], own_y[1], from_x[1], from_y[2]), [slot_z], [0], size, width)
    gradient = add(
        [after(sums_own, *from_d[0], from_x[2]), totals(partial_z)], [slot_own, slot_z],
        [jnp.float32(-1.0), sign(jnp.int32(PLANE))], [eps_occ, eps_of[PLANE - 1]],
    )
    early = integrate(after(turned, gradient), [slot_x[:last], slot_y[:last]], [0, 0], size, width)
    partial_x, partial_y = integrate(
        after(turned, own_d_x, own_d_y, *from_d[1], *from_d[2]), [slot_x[last:], slot_y[last:]], [last, last], size, width, early
    )
    gradient = add(
        [totals(partial_x), totals(partial_y)], [slot_x, slot_y],
        [sign(offset_x), sign(jnp.int32(PLANE // 2))], [chosen(0), eps_of[PLANE // 2 - 1]], gradient,
    )
    partial_d = integrate(after(turned, gradient), [slot_d[:last]], [0], size, width)
    (partial_d,) = integrate(turned, [slot_d[last:]], [last], size, width, partial_d)
    gradient = add(
        [totals(partial_d)], [slot_d], [sign(offset_d)], [chosen(PLANE - 2)], gradient
    )
    return gradient.reshape(rows, occ_rows, virt)


def solution(mesh):
    if mesh.shape["occ"] % PLANE:
        raise ValueError("incomplete plane")
    in_specs = (P("aux", "occ", None), P("occ"), P(), P("occ", None))
    out_specs = P("aux", "occ", None)
    return jax.shard_map(
        on_device, mesh=mesh, in_specs=in_specs, out_specs=out_specs, check_vma=False
    )
```

```python
import functools

import jax
import jax.numpy as jnp
from jax import lax
from jax.experimental import pallas as pl
from jax.experimental.pallas import tpu as pltpu
from jax.sharding import PartitionSpec as P

LANES = 128
SUBLANES = 8
PLANE = 4
CHUNKS = 4
VMEM_LIMIT = 40 * 1024 * 1024


def split(value):
    high = value.astype(jnp.bfloat16)
    low = (value - high.astype(jnp.float32)).astype(jnp.bfloat16)
    return high, low


def deep_left(value):
    high, low = split(value)
    return jnp.concatenate([high, low, high], axis=1)


def deep_right(value):
    high, low = split(value)
    return jnp.concatenate([high, high, low], axis=0)


def dot(left, right):
    numbers = (((1,), (0,)), ((), ()))
    return lax.dot_general(left, right, numbers, preferred_element_type=jnp.float32)


def rows_of(ref, start, count, width):
    lines = width // LANES
    columns = [ref[pl.ds(start * lines + at, count, stride=lines), :] for at in range(lines)]
    return jnp.concatenate(columns, axis=1)


def distinct(arrays):
    return list({id(array): array for array in arrays}.values())


class Copies:
    def __init__(self, semaphores):
        self.semaphores = semaphores
        self.used = 0

    def start(self, source, target):
        copy = pltpu.make_async_copy(source, target, self.semaphores.at[self.used])
        self.used += 1
        copy.start()
        return copy


def call(kernel, smem, vmem, anywhere, outputs, out_space, scratch, flops):
    spaces = [pltpu.SMEM] * len(smem) + [pltpu.VMEM] * len(vmem) + [pl.ANY] * len(anywhere)
    moved = sum(a.size * a.dtype.itemsize for a in (*vmem, *anywhere, *outputs))
    return pl.pallas_call(
        kernel,
        out_shape=outputs,
        in_specs=[pl.BlockSpec(memory_space=space) for space in spaces],
        out_specs=[pl.BlockSpec(memory_space=out_space)] * len(outputs),
        scratch_shapes=scratch,
        compiler_params=pltpu.CompilerParams(vmem_limit_bytes=VMEM_LIMIT),
        cost_estimate=pl.CostEstimate(flops=flops, bytes_accessed=moved, transcendentals=0),
    )(*smem, *vmem, *anywhere)


def prepare(own, rows, width):
    size = rows // CHUNKS
    cut = size * width // LANES

    def kernel(own_ref, high_ref, low_ref, integrals_ref, block_ref, semaphores):
        copies = Copies(semaphores)
        coming = [copies.start(own_ref.at[pl.ds(at * cut, cut)], block_ref.at[at]) for at in range(CHUNKS)]
        for at in range(CHUNKS):
            coming[at].wait()
            block = rows_of(block_ref.at[at], 0, size, width)
            high, low = split(block.T)
            high_ref[at] = high
            low_ref[at] = low
            value = dot(jnp.concatenate([high, low, high], axis=1), deep_right(block))
            integrals_ref[...] = integrals_ref[...] + value if at else value

    half = jax.ShapeDtypeStruct((CHUNKS, width, size), jnp.bfloat16)
    square = jax.ShapeDtypeStruct((width, width), jnp.float32)
    scratch = [pltpu.VMEM((CHUNKS, cut, LANES), jnp.float32), pltpu.SemaphoreType.DMA((CHUNKS,))]
    flops = 6 * rows * width * width
    return call(kernel, [], [], [own], [half, half, square], pltpu.VMEM, scratch, flops)


def integrate(turned, slots, first, size, width, before=()):
    cut = size * width // LANES
    count = len(slots)
    pieces = [piece for slot in slots for piece in slot]
    arrays = distinct([array for array, _ in pieces])
    numbers = [list(range(start, start + len(slot))) for slot, start in zip(slots, first)]
    needed = sorted({number for some in numbers for number in some})
    before = list(before)

    def kernel(*refs):
        given = iter(refs)
        high_ref, low_ref = next(given), next(given)
        before_refs = [next(given) for _ in before]
        ref_of = {id(array): next(given) for array in arrays}
        outs = [next(given) for _ in range(count)]
        turned_ref, block_ref, before_ref, semaphores = given
        copies = Copies(semaphores)
        coming, turning = [], {}

        def turn(number):
            if number not in turning:
                at = needed.index(number)
                turning[number] = [
                    copies.start(high_ref.at[number], turned_ref.at[at, 0]),
                    copies.start(low_ref.at[number], turned_ref.at[at, 1]),
                ]

        at = 0
        for slot in range(count):
            for number, (array, base) in zip(numbers[slot], slots[slot]):
                turn(number)
                coming.append(copies.start(ref_of[id(array)].at[pl.ds(base, cut)], block_ref.at[at]))
                at += 1
        adding = [copies.start(ref, before_ref.at[slot]) for slot, ref in enumerate(before_refs)]
        at = 0
        for slot in range(count):
            for place, number in enumerate(numbers[slot]):
                for copy in turning.pop(number, []):
                    copy.wait()
                coming[at].wait()
                there = needed.index(number)
                high, low = turned_ref[there, 0], turned_ref[there, 1]
                left = jnp.concatenate([high, low, high], axis=1)
                value = dot(left, deep_right(rows_of(block_ref.at[at], 0, size, width)))
                outs[slot][...] = outs[slot][...] + value if place else value
                at += 1
            if before:
                adding[slot].wait()
                outs[slot][...] += before_ref[slot]

    out = [jax.ShapeDtypeStruct((width, width), jnp.float32)] * count
    scratch = [
        pltpu.VMEM((len(needed), 2, width, size), jnp.bfloat16),
        pltpu.VMEM((len(pieces), cut, LANES), jnp.float32),
        pltpu.VMEM((max(len(before), 1), width, width), jnp.float32),
        pltpu.SemaphoreType.DMA((2 * len(needed) + len(pieces) + len(before),)),
    ]
    flops = 6 * len(pieces) * size * width * width
    return call(kernel, [], [], [*turned, *before, *arrays], out, pltpu.VMEM, scratch, flops)


def contract(partials, slots, signs, energies, eps_virt, size, before=None):
    count = len(slots)
    chunks = len(slots[0])
    virt = eps_virt.shape[1]
    width = partials[0][0].shape[0]
    occ_rows = width // virt
    lines = width // LANES
    cut = size * lines
    sums = [array for slot in partials for array in slot]
    pieces = [piece for slot in slots for piece in slot]
    arrays = distinct([array for array, _ in (*pieces, *energies)])
    last = [before] if before is not None else []

    def kernel(*refs):
        given = iter(refs)
        sign_ref, virt_ref = next(given), next(given)
        sum_refs = [next(given) for _ in sums]
        before_refs = [next(given) for _ in last]
        ref_of = {id(array): next(given) for array in arrays}
        out_ref, energy_ref, sum_ref, block_ref, result_ref, right_ref, semaphores = given
        copies = Copies(semaphores)
        arriving = [
            copies.start(ref_of[id(array)].at[pl.ds(base, SUBLANES)], energy_ref.at[at])
            for at, (array, base) in enumerate(energies)
        ]
        arriving += [copies.start(ref, sum_ref.at[at]) for at, ref in enumerate(sum_refs)]
        coming = [
            [
                copies.start(ref_of[id(slots[slot][at][0])].at[pl.ds(slots[slot][at][1], cut)], block_ref.at[slot, at])
                for slot in range(count)
            ]
            for at in range(chunks)
        ]
        adding = [
            [copies.start(ref.at[pl.ds(at * cut, cut)], result_ref.at[at]) for ref in before_refs]
            for at in range(chunks)
        ]
        for copy in arriving:
            copy.wait()

        def line(at):
            virtual = virt_ref[...]
            energy = energy_ref[at]
            return jnp.concatenate([virtual - energy[:1, i : i + 1] for i in range(occ_rows)], axis=1)

        row = jnp.broadcast_to(line(0), (SUBLANES, width)).T[:, :1]
        at = 0
        for slot in range(count):
            total = sum_ref[at]
            for extra in range(1, len(partials[slot])):
                total = total + sum_ref[at + extra]
            at += len(partials[slot])
            amplitude = (sign_ref[slot] * total) / (row + line(slot + 1))
            right_ref[pl.ds(slot * 3 * width, 3 * width), :] = deep_right(amplitude.T)
        leaving = []
        for at in range(chunks):
            for copy in coming[at] + adding[at]:
                copy.wait()
            left = [deep_left(rows_of(block_ref.at[slot, at], 0, size, width)) for slot in range(count)]
            value = dot(jnp.concatenate(left, axis=1), right_ref[...])
            for column in range(lines):
                lanes = value[:, column * LANES : (column + 1) * LANES]
                where = pl.ds(column, size, stride=lines)
                if last:
                    lanes = lanes + result_ref[at, where, :]
                result_ref[at, where, :] = lanes
            leaving.append(copies.start(result_ref.at[at], out_ref.at[pl.ds(at * cut, cut)]))
        for copy in leaving:
            copy.wait()

    rows = chunks * size
    out = jax.ShapeDtypeStruct((rows * lines, LANES), jnp.float32)
    scratch = [
        pltpu.VMEM((len(energies), SUBLANES, LANES), jnp.float32),
        pltpu.VMEM((len(sums), width, width), jnp.float32),
        pltpu.VMEM((count, chunks, cut, LANES), jnp.float32),
        pltpu.VMEM((chunks, cut, LANES), jnp.float32),
        pltpu.VMEM((count * 3 * width, width), jnp.bfloat16),
        pltpu.SemaphoreType.DMA((len(energies) + len(sums) + len(pieces) + 2 * chunks,)),
    ]
    flops = 6 * count * rows * width * width
    return call(kernel, [signs], [eps_virt], [*sums, *last, *arrays], [out], pl.ANY, scratch, flops)[0]


def after(block, *others):
    return lax.optimization_barrier((block, *others))[0]


def on_device(factors, eps_occ, eps_virt, pair_mask):
    rows, occ_rows, virt = factors.shape
    width = occ_rows * virt
    lines = width // LANES
    groups = lax.axis_size("occ")
    shares = lax.axis_size("aux")
    size = rows // CHUNKS
    cut = size * lines
    last = CHUNKS - 1
    group = lax.axis_index("occ")
    place = group % PLANE
    odd_x = place % 2 == 1
    odd_y = place // 2 == 1

    own = factors.reshape(rows * lines, LANES)
    energies = jnp.zeros((SUBLANES * LANES,), jnp.float32).at[:occ_rows].set(eps_occ)
    energies = energies.reshape(SUBLANES, LANES)

    def part(whole, at):
        return whole[at * cut : (at + 1) * cut]

    def swap(block, bit):
        return lax.ppermute(block, "occ", [(g, g ^ bit) for g in range(groups)])

    def up(block):
        return lax.ppermute(block, "occ", [(g, g + PLANE) for g in range(groups - PLANE)])

    def totals(partial):
        if shares == 2:
            return [partial, lax.ppermute(partial, "aux", [(0, 1), (1, 0)])]
        return [lax.psum(partial, "aux")]

    def sign(offset):
        flag = lax.dynamic_index_in_dim(pair_mask[0], offset - 1, 0, keepdims=False)
        return jnp.where((group >= offset) & (flag > 0), -1.0, 0.0).astype(jnp.float32)

    sign_own = jnp.float32(-1.0)
    sign_z = sign(jnp.int32(PLANE))
    sign_x = sign(jnp.where(odd_x, 1, PLANE - 1))
    sign_y = sign(jnp.int32(PLANE // 2))
    sign_d = sign(jnp.where(odd_x, PLANE - 1, 1))

    first_sent = jnp.concatenate([part(own, 0), energies])

    def add(partials, slots, signs, carriers, before=None):
        where = [(first_sent, cut)] + [(carrier, cut) for carrier in carriers]
        return contract(partials, slots, jnp.stack(signs), where, eps_virt[None, :], size, before)

    from_z, from_x, from_y, from_d = [], [], [], []
    from_z.append(up(first_sent))
    high, low, partial_own = prepare(own, rows, width)
    turned = (high, low)
    sums_own = totals(partial_own)
    ready = [partial_own]
    for at in range(CHUNKS):
        mine, came = lax.optimization_barrier((own, from_z[at]))
        mine = part(mine, at) if at else first_sent
        send_x = after(jnp.where(odd_x, came, mine), *ready)
        send_y = jnp.where(odd_y, came, mine)
        from_x.append(swap(send_x, 1))
        from_y.append(swap(send_y, 2))
        if at < last:
            from_z.append(up(part(after(own, from_z[at], partial_own), at + 1)))
        ready = [from_x[at]]
        from_d.append(swap(after(from_y[at], from_d[at - 1] if at else from_x[0]), 1))

    def slot_of(blocks):
        return [(block, 0) for block in blocks]

    slot_own = [(own, at * cut) for at in range(CHUNKS)]
    slot_z, slot_x, slot_y, slot_d = map(slot_of, (from_z, from_x, from_y, from_d))

    (partial_z,) = integrate(turned, [slot_z], [0], size, width)
    gradient = add(
        [sums_own, totals(partial_z)], [slot_own, slot_z], [sign_own, sign_z], [first_sent, from_z[0]]
    )
    turned = after(turned, gradient)
    early = integrate(
        turned, [slot_x[:last], slot_y[:last], slot_d[: last - 1]], [0, 0, 0], size, width
    )
    partial_x, partial_y, partial_d = integrate(
        turned, [slot_x[last:], slot_y[last:], slot_d[last - 1 : last]], [last, last, last - 1], size, width, early
    )
    (partial_d,) = integrate(turned, [slot_d[last:]], [last], size, width, [partial_d])
    gradient = add(
        [totals(partial_x), totals(partial_y), totals(partial_d)], [slot_x, slot_y, slot_d],
        [sign_x, sign_y, sign_d], [from_x[0], from_y[0], from_d[0]], gradient,
    )
    return gradient.reshape(rows, occ_rows, virt)


def solution(mesh):
    if mesh.shape["occ"] % PLANE:
        raise ValueError("incomplete plane")
    in_specs = (P("aux", "occ", None), P("occ"), P(), P("occ", None))
    out_specs = P("aux", "occ", None)
    return jax.shard_map(
        on_device, mesh=mesh, in_specs=in_specs, out_specs=out_specs, check_vma=False
    )
```

```python
import functools

import jax
import jax.numpy as jnp
from jax import lax
from jax.experimental import pallas as pl
from jax.experimental.pallas import tpu as pltpu
from jax.sharding import PartitionSpec as P

LANES = 128
SUBLANES = 8
PLANE = 4
CHUNKS = 4
VMEM_LIMIT = 40 * 1024 * 1024


def split(value):
    high = value.astype(jnp.bfloat16)
    low = (value - high.astype(jnp.float32)).astype(jnp.bfloat16)
    return high, low


def deep_left(value):
    high, low = split(value)
    return jnp.concatenate([high, low, high], axis=1)


def deep_right(value):
    high, low = split(value)
    return jnp.concatenate([high, high, low], axis=0)


def dot(left, right):
    numbers = (((1,), (0,)), ((), ()))
    return lax.dot_general(left, right, numbers, preferred_element_type=jnp.float32)


def rows_of(ref, start, count, width):
    lines = width // LANES
    columns = [ref[pl.ds(start * lines + at, count, stride=lines), :] for at in range(lines)]
    return jnp.concatenate(columns, axis=1)


def distinct(arrays):
    return list({id(array): array for array in arrays}.values())


class Copies:
    def __init__(self, semaphores):
        self.semaphores = semaphores
        self.used = 0

    def start(self, source, target):
        copy = pltpu.make_async_copy(source, target, self.semaphores.at[self.used])
        self.used += 1
        copy.start()
        return copy


def call(kernel, smem, vmem, anywhere, outputs, out_space, scratch, flops):
    spaces = [pltpu.SMEM] * len(smem) + [pltpu.VMEM] * len(vmem) + [pltpu.HBM] * len(anywhere)
    moved = sum(a.size * a.dtype.itemsize for a in (*vmem, *anywhere, *outputs))
    return pl.pallas_call(
        kernel,
        out_shape=outputs,
        in_specs=[pl.BlockSpec(memory_space=space) for space in spaces],
        out_specs=[pl.BlockSpec(memory_space=out_space)] * len(outputs),
        scratch_shapes=scratch,
        compiler_params=pltpu.CompilerParams(vmem_limit_bytes=VMEM_LIMIT),
        cost_estimate=pl.CostEstimate(flops=flops, bytes_accessed=moved, transcendentals=0),
    )(*smem, *vmem, *anywhere)


def prepare(own, rows, width):
    size = rows // CHUNKS
    cut = size * width // LANES

    def kernel(own_ref, high_ref, low_ref, integrals_ref, block_ref, semaphores):
        copies = Copies(semaphores)
        coming = [copies.start(own_ref.at[pl.ds(at * cut, cut)], block_ref.at[at]) for at in range(CHUNKS)]
        for at in range(CHUNKS):
            coming[at].wait()
            block = rows_of(block_ref.at[at], 0, size, width)
            high, low = split(block.T)
            high_ref[at] = high
            low_ref[at] = low
            value = dot(jnp.concatenate([high, low, high], axis=1), deep_right(block))
            integrals_ref[...] = integrals_ref[...] + value if at else value

    half = jax.ShapeDtypeStruct((CHUNKS, width, size), jnp.bfloat16)
    square = jax.ShapeDtypeStruct((width, width), jnp.float32)
    scratch = [pltpu.VMEM((CHUNKS, cut, LANES), jnp.float32), pltpu.SemaphoreType.DMA((CHUNKS,))]
    flops = 6 * rows * width * width
    return call(kernel, [], [], [own], [half, half, square], pltpu.VMEM, scratch, flops)


def integrate(turned, slots, first, size, width, before=()):
    cut = size * width // LANES
    count = len(slots)
    pieces = [piece for slot in slots for piece in slot]
    arrays = distinct([array for array, _ in pieces])
    numbers = [list(range(start, start + len(slot))) for slot, start in zip(slots, first)]
    needed = sorted({number for some in numbers for number in some})
    before = list(before)

    def kernel(*refs):
        given = iter(refs)
        high_ref, low_ref = next(given), next(given)
        before_refs = [next(given) for _ in before]
        ref_of = {id(array): next(given) for array in arrays}
        outs = [next(given) for _ in range(count)]
        turned_ref, block_ref, before_ref, semaphores = given
        copies = Copies(semaphores)
        coming, turning = [], {}

        def turn(number):
            if number not in turning:
                at = needed.index(number)
                turning[number] = [
                    copies.start(high_ref.at[number], turned_ref.at[at, 0]),
                    copies.start(low_ref.at[number], turned_ref.at[at, 1]),
                ]

        at = 0
        for slot in range(count):
            for number, (array, base) in zip(numbers[slot], slots[slot]):
                turn(number)
                coming.append(copies.start(ref_of[id(array)].at[pl.ds(base, cut)], block_ref.at[at]))
                at += 1
        adding = [copies.start(ref, before_ref.at[slot]) for slot, ref in enumerate(before_refs)]
        at = 0
        for slot in range(count):
            for place, number in enumerate(numbers[slot]):
                for copy in turning.pop(number, []):
                    copy.wait()
                coming[at].wait()
                there = needed.index(number)
                high, low = turned_ref[there, 0], turned_ref[there, 1]
                left = jnp.concatenate([high, low, high], axis=1)
                value = dot(left, deep_right(rows_of(block_ref.at[at], 0, size, width)))
                outs[slot][...] = outs[slot][...] + value if place else value
                at += 1
            if before:
                adding[slot].wait()
                outs[slot][...] += before_ref[slot]

    out = [jax.ShapeDtypeStruct((width, width), jnp.float32)] * count
    scratch = [
        pltpu.VMEM((len(needed), 2, width, size), jnp.bfloat16),
        pltpu.VMEM((len(pieces), cut, LANES), jnp.float32),
        pltpu.VMEM((max(len(before), 1), width, width), jnp.float32),
        pltpu.SemaphoreType.DMA((2 * len(needed) + len(pieces) + len(before),)),
    ]
    flops = 6 * len(pieces) * size * width * width
    return call(kernel, [], [], [*turned, *before, *arrays], out, pltpu.VMEM, scratch, flops)


def contract(partials, slots, signs, energies, eps_virt, size, before=None):
    count = len(slots)
    chunks = len(slots[0])
    virt = eps_virt.shape[1]
    width = partials[0][0].shape[0]
    occ_rows = width // virt
    lines = width // LANES
    cut = size * lines
    sums = [array for slot in partials for array in slot]
    pieces = [piece for slot in slots for piece in slot]
    arrays = distinct([array for array, _ in (*pieces, *energies)])
    last = [before] if before is not None else []

    def kernel(*refs):
        given = iter(refs)
        sign_ref, virt_ref = next(given), next(given)
        sum_refs = [next(given) for _ in sums]
        before_refs = [next(given) for _ in last]
        ref_of = {id(array): next(given) for array in arrays}
        out_ref, energy_ref, sum_ref, block_ref, result_ref, right_ref, semaphores = given
        copies = Copies(semaphores)
        arriving = [
            copies.start(ref_of[id(array)].at[pl.ds(base, SUBLANES)], energy_ref.at[at])
            for at, (array, base) in enumerate(energies)
        ]
        arriving += [copies.start(ref, sum_ref.at[at]) for at, ref in enumerate(sum_refs)]
        coming = [
            [
                copies.start(ref_of[id(slots[slot][at][0])].at[pl.ds(slots[slot][at][1], cut)], block_ref.at[slot, at])
                for slot in range(count)
            ]
            for at in range(chunks)
        ]
        adding = [
            [copies.start(ref.at[pl.ds(at * cut, cut)], result_ref.at[at]) for ref in before_refs]
            for at in range(chunks)
        ]
        for copy in arriving:
            copy.wait()

        def line(at):
            virtual = virt_ref[...]
            energy = energy_ref[at]
            return jnp.concatenate([virtual - energy[:1, i : i + 1] for i in range(occ_rows)], axis=1)

        row = jnp.broadcast_to(line(0), (SUBLANES, width)).T[:, :1]
        at = 0
        for slot in range(count):
            total = sum_ref[at]
            for extra in range(1, len(partials[slot])):
                total = total + sum_ref[at + extra]
            at += len(partials[slot])
            amplitude = (sign_ref[slot] * total) / (row + line(slot + 1))
            right_ref[pl.ds(slot * 3 * width, 3 * width), :] = deep_right(amplitude.T)
        leaving = []
        for at in range(chunks):
            for copy in coming[at] + adding[at]:
                copy.wait()
            left = [deep_left(rows_of(block_ref.at[slot, at], 0, size, width)) for slot in range(count)]
            value = dot(jnp.concatenate(left, axis=1), right_ref[...])
            for column in range(lines):
                lanes = value[:, column * LANES : (column + 1) * LANES]
                where = pl.ds(column, size, stride=lines)
                if last:
                    lanes = lanes + result_ref[at, where, :]
                result_ref[at, where, :] = lanes
            leaving.append(copies.start(result_ref.at[at], out_ref.at[pl.ds(at * cut, cut)]))
        for copy in leaving:
            copy.wait()

    rows = chunks * size
    out = jax.ShapeDtypeStruct((rows * lines, LANES), jnp.float32)
    scratch = [
        pltpu.VMEM((len(energies), SUBLANES, LANES), jnp.float32),
        pltpu.VMEM((len(sums), width, width), jnp.float32),
        pltpu.VMEM((count, chunks, cut, LANES), jnp.float32),
        pltpu.VMEM((chunks, cut, LANES), jnp.float32),
        pltpu.VMEM((count * 3 * width, width), jnp.bfloat16),
        pltpu.SemaphoreType.DMA((len(energies) + len(sums) + len(pieces) + 2 * chunks,)),
    ]
    flops = 6 * count * rows * width * width
    return call(kernel, [signs], [eps_virt], [*sums, *last, *arrays], [out], pltpu.HBM, scratch, flops)[0]


def after(block, *others):
    return lax.optimization_barrier((block, *others))[0]


def on_device(factors, eps_occ, eps_virt, pair_mask):
    rows, occ_rows, virt = factors.shape
    width = occ_rows * virt
    lines = width // LANES
    groups = lax.axis_size("occ")
    shares = lax.axis_size("aux")
    size = rows // CHUNKS
    cut = size * lines
    last = CHUNKS - 1
    group = lax.axis_index("occ")
    place = group % PLANE
    odd_x = place % 2 == 1
    odd_y = place // 2 == 1

    own = factors.reshape(rows * lines, LANES)
    energies = jnp.zeros((SUBLANES * LANES,), jnp.float32).at[:occ_rows].set(eps_occ)
    energies = energies.reshape(SUBLANES, LANES)

    def part(whole, at):
        return whole[at * cut : (at + 1) * cut]

    def swap(block, bit):
        return lax.ppermute(block, "occ", [(g, g ^ bit) for g in range(groups)])

    def up(block):
        return lax.ppermute(block, "occ", [(g, g + PLANE) for g in range(groups - PLANE)])

    def totals(partial):
        if shares == 2:
            return [partial, lax.ppermute(partial, "aux", [(0, 1), (1, 0)])]
        return [lax.psum(partial, "aux")]

    def sign(offset):
        flag = lax.dynamic_index_in_dim(pair_mask[0], offset - 1, 0, keepdims=False)
        return jnp.where((group >= offset) & (flag > 0), -1.0, 0.0).astype(jnp.float32)

    sign_own = jnp.float32(-1.0)
    sign_z = sign(jnp.int32(PLANE))
    sign_x = sign(jnp.where(odd_x, 1, PLANE - 1))
    sign_y = sign(jnp.int32(PLANE // 2))
    sign_d = sign(jnp.where(odd_x, PLANE - 1, 1))

    first_sent = jnp.concatenate([part(own, 0), energies])

    def add(partials, slots, signs, carriers, before=None):
        where = [(first_sent, cut)] + [(carrier, cut) for carrier in carriers]
        return contract(partials, slots, jnp.stack(signs), where, eps_virt[None, :], size, before)

    from_z, from_x, from_y, from_d = [], [], [], []
    from_z.append(up(first_sent))
    high, low, partial_own = prepare(own, rows, width)
    turned = (high, low)
    sums_own = totals(partial_own)
    def slot_of(blocks):
        return [(block, 0) for block in blocks]

    slot_own = [(own, at * cut) for at in range(CHUNKS)]
    ready = [partial_own]
    for at in range(CHUNKS):
        mine, came = lax.optimization_barrier((own, from_z[at]))
        mine = part(mine, at) if at else first_sent
        send_x = after(jnp.where(odd_x, came, mine), *ready)
        send_y = jnp.where(odd_y, came, mine)
        from_x.append(swap(send_x, 1))
        from_y.append(swap(send_y, 2))
        if at < last:
            held = [from_x[0], from_y[0]] if at else [partial_own]
            from_z.append(up(part(after(own, from_z[at], *held), at + 1)))
        ready = [from_x[at]]
        from_d.append(swap(after(from_y[at], from_d[at - 1] if at else from_x[0]), 1))

    slot_z, slot_x, slot_y, slot_d = map(slot_of, (from_z, from_x, from_y, from_d))
    partial_z, partial_y = integrate(turned, [slot_z, slot_y], [0, 0], size, width)
    gradient = add(
        [sums_own, totals(partial_z), totals(partial_y)], [slot_own, slot_z, slot_y],
        [sign_own, sign_z, sign_y], [first_sent, from_z[0], from_y[0]],
    )
    turned = after(turned, gradient)
    early = integrate(turned, [slot_x[:last], slot_d[: last - 1]], [0, 0], size, width)
    partial_x, partial_d = integrate(
        turned, [slot_x[last:], slot_d[last - 1 : last]], [last, last - 1], size, width, early
    )
    (partial_d,) = integrate(turned, [slot_d[last:]], [last], size, width, [partial_d])
    gradient = add(
        [totals(partial_x), totals(partial_d)], [slot_x, slot_d],
        [sign_x, sign_d], [from_x[0], from_d[0]], gradient,
    )
    return gradient.reshape(rows, occ_rows, virt)


def solution(mesh):
    if mesh.shape["occ"] % PLANE:
        raise ValueError("incomplete plane")
    in_specs = (P("aux", "occ", None), P("occ"), P(), P("occ", None))
    out_specs = P("aux", "occ", None)
    return jax.shard_map(
        on_device, mesh=mesh, in_specs=in_specs, out_specs=out_specs, check_vma=False
    )
```

```python
import functools

import jax
import jax.numpy as jnp
from jax import lax
from jax.experimental import pallas as pl
from jax.experimental.pallas import tpu as pltpu
from jax.sharding import PartitionSpec as P

LANES = 128
SUBLANES = 8
PLANE = 4
CHUNKS = 4
VMEM_LIMIT = 60 * 1024 * 1024


def split(value):
    high = value.astype(jnp.bfloat16)
    low = (value - high.astype(jnp.float32)).astype(jnp.bfloat16)
    return high, low


def deep_left(value):
    high, low = split(value)
    return jnp.concatenate([high, low, high], axis=1)


def deep_right(value):
    high, low = split(value)
    return jnp.concatenate([high, high, low], axis=0)


def dot(left, right):
    numbers = (((1,), (0,)), ((), ()))
    return lax.dot_general(left, right, numbers, preferred_element_type=jnp.float32)


def rows_of(ref, start, count, width):
    lines = width // LANES
    columns = [ref[pl.ds(start * lines + at, count, stride=lines), :] for at in range(lines)]
    return jnp.concatenate(columns, axis=1)


def distinct(arrays):
    return list({id(array): array for array in arrays}.values())


class Copies:
    def __init__(self, semaphores):
        self.semaphores = semaphores
        self.used = 0

    def start(self, source, target):
        copy = pltpu.make_async_copy(source, target, self.semaphores.at[self.used])
        self.used += 1
        copy.start()
        return copy


def call(kernel, smem, vmem, anywhere, outputs, out_space, scratch, flops):
    spaces = [pltpu.SMEM] * len(smem) + [pltpu.VMEM] * len(vmem) + [pl.ANY] * len(anywhere)
    moved = sum(a.size * a.dtype.itemsize for a in (*vmem, *anywhere, *outputs))
    return pl.pallas_call(
        kernel,
        out_shape=outputs,
        in_specs=[pl.BlockSpec(memory_space=space) for space in spaces],
        out_specs=[pl.BlockSpec(memory_space=out_space)] * len(outputs),
        scratch_shapes=scratch,
        compiler_params=pltpu.CompilerParams(vmem_limit_bytes=VMEM_LIMIT),
        cost_estimate=pl.CostEstimate(flops=flops, bytes_accessed=moved, transcendentals=0),
    )(*smem, *vmem, *anywhere)


def prepare(own, rows, width):
    size = rows // CHUNKS
    cut = size * width // LANES

    def kernel(own_ref, high_ref, low_ref, integrals_ref, block_ref, semaphores):
        copies = Copies(semaphores)
        coming = [copies.start(own_ref.at[pl.ds(at * cut, cut)], block_ref.at[at]) for at in range(CHUNKS)]
        for at in range(CHUNKS):
            coming[at].wait()
            block = rows_of(block_ref.at[at], 0, size, width)
            high, low = split(block.T)
            high_ref[at] = high
            low_ref[at] = low
            value = dot(jnp.concatenate([high, low, high], axis=1), deep_right(block))
            integrals_ref[...] = integrals_ref[...] + value if at else value

    half = jax.ShapeDtypeStruct((CHUNKS, width, size), jnp.bfloat16)
    square = jax.ShapeDtypeStruct((width, width), jnp.float32)
    scratch = [pltpu.VMEM((CHUNKS, cut, LANES), jnp.float32), pltpu.SemaphoreType.DMA((CHUNKS,))]
    flops = 6 * rows * width * width
    return call(kernel, [], [], [own], [half, half, square], pltpu.VMEM, scratch, flops)


def integrate(turned, slots, first, size, width, before=()):
    cut = size * width // LANES
    count = len(slots)
    pieces = [piece for slot in slots for piece in slot]
    arrays = distinct([array for array, _ in pieces])
    numbers = [list(range(start, start + len(slot))) for slot, start in zip(slots, first)]
    needed = sorted({number for some in numbers for number in some})
    before = list(before)

    def kernel(*refs):
        given = iter(refs)
        high_ref, low_ref = next(given), next(given)
        before_refs = [next(given) for _ in before]
        ref_of = {id(array): next(given) for array in arrays}
        outs = [next(given) for _ in range(count)]
        turned_ref, block_ref, before_ref, semaphores = given
        copies = Copies(semaphores)
        coming, turning = [], {}

        def turn(number):
            if number not in turning:
                at = needed.index(number)
                turning[number] = [
                    copies.start(high_ref.at[number], turned_ref.at[at, 0]),
                    copies.start(low_ref.at[number], turned_ref.at[at, 1]),
                ]

        at = 0
        for slot in range(count):
            for number, (array, base) in zip(numbers[slot], slots[slot]):
                turn(number)
                coming.append(copies.start(ref_of[id(array)].at[pl.ds(base, cut)], block_ref.at[at]))
                at += 1
        adding = [copies.start(ref, before_ref.at[slot]) for slot, ref in enumerate(before_refs)]
        at = 0
        for slot in range(count):
            for place, number in enumerate(numbers[slot]):
                for copy in turning.pop(number, []):
                    copy.wait()
                coming[at].wait()
                there = needed.index(number)
                high, low = turned_ref[there, 0], turned_ref[there, 1]
                left = jnp.concatenate([high, low, high], axis=1)
                value = dot(left, deep_right(rows_of(block_ref.at[at], 0, size, width)))
                outs[slot][...] = outs[slot][...] + value if place else value
                at += 1
            if before:
                adding[slot].wait()
                outs[slot][...] += before_ref[slot]

    out = [jax.ShapeDtypeStruct((width, width), jnp.float32)] * count
    scratch = [
        pltpu.VMEM((len(needed), 2, width, size), jnp.bfloat16),
        pltpu.VMEM((len(pieces), cut, LANES), jnp.float32),
        pltpu.VMEM((max(len(before), 1), width, width), jnp.float32),
        pltpu.SemaphoreType.DMA((2 * len(needed) + len(pieces) + len(before),)),
    ]
    flops = 6 * len(pieces) * size * width * width
    return call(kernel, [], [], [*turned, *before, *arrays], out, pltpu.VMEM, scratch, flops)


def contract(partials, slots, signs, energies, eps_virt, size, before=None):
    count = len(slots)
    chunks = len(slots[0])
    virt = eps_virt.shape[1]
    width = partials[0][0].shape[0]
    occ_rows = width // virt
    lines = width // LANES
    cut = size * lines
    sums = [array for slot in partials for array in slot]
    pieces = [piece for slot in slots for piece in slot]
    arrays = distinct([array for array, _ in (*pieces, *energies)])
    last = [before] if before is not None else []

    def kernel(*refs):
        given = iter(refs)
        sign_ref, virt_ref = next(given), next(given)
        sum_refs = [next(given) for _ in sums]
        before_refs = [next(given) for _ in last]
        ref_of = {id(array): next(given) for array in arrays}
        out_ref, energy_ref, sum_ref, block_ref, result_ref, right_ref, semaphores = given
        copies = Copies(semaphores)
        arriving = [
            copies.start(ref_of[id(array)].at[pl.ds(base, SUBLANES)], energy_ref.at[at])
            for at, (array, base) in enumerate(energies)
        ]
        arriving += [copies.start(ref, sum_ref.at[at]) for at, ref in enumerate(sum_refs)]
        coming = [
            [
                copies.start(ref_of[id(slots[slot][at][0])].at[pl.ds(slots[slot][at][1], cut)], block_ref.at[slot, at])
                for slot in range(count)
            ]
            for at in range(chunks)
        ]
        adding = [
            [copies.start(ref.at[pl.ds(at * cut, cut)], result_ref.at[at]) for ref in before_refs]
            for at in range(chunks)
        ]
        for copy in arriving:
            copy.wait()

        def line(at):
            virtual = virt_ref[...]
            energy = energy_ref[at]
            return jnp.concatenate([virtual - energy[:1, i : i + 1] for i in range(occ_rows)], axis=1)

        row = jnp.broadcast_to(line(0), (SUBLANES, width)).T[:, :1]
        at = 0
        for slot in range(count):
            total = sum_ref[at]
            for extra in range(1, len(partials[slot])):
                total = total + sum_ref[at + extra]
            at += len(partials[slot])
            amplitude = (sign_ref[slot] * total) / (row + line(slot + 1))
            right_ref[pl.ds(slot * 3 * width, 3 * width), :] = deep_right(amplitude.T)
        leaving = []
        for at in range(chunks):
            for copy in coming[at] + adding[at]:
                copy.wait()
            left = [deep_left(rows_of(block_ref.at[slot, at], 0, size, width)) for slot in range(count)]
            value = dot(jnp.concatenate(left, axis=1), right_ref[...])
            for column in range(lines):
                lanes = value[:, column * LANES : (column + 1) * LANES]
                where = pl.ds(column, size, stride=lines)
                if last:
                    lanes = lanes + result_ref[at, where, :]
                result_ref[at, where, :] = lanes
            leaving.append(copies.start(result_ref.at[at], out_ref.at[pl.ds(at * cut, cut)]))
        for copy in leaving:
            copy.wait()

    rows = chunks * size
    out = jax.ShapeDtypeStruct((rows * lines, LANES), jnp.float32)
    scratch = [
        pltpu.VMEM((len(energies), SUBLANES, LANES), jnp.float32),
        pltpu.VMEM((len(sums), width, width), jnp.float32),
        pltpu.VMEM((count, chunks, cut, LANES), jnp.float32),
        pltpu.VMEM((chunks, cut, LANES), jnp.float32),
        pltpu.VMEM((count * 3 * width, width), jnp.bfloat16),
        pltpu.SemaphoreType.DMA((len(energies) + len(sums) + len(pieces) + 2 * chunks,)),
    ]
    flops = 6 * count * rows * width * width
    return call(kernel, [signs], [eps_virt], [*sums, *last, *arrays], [out], pl.ANY, scratch, flops)[0]


def after(block, *others):
    return lax.optimization_barrier((block, *others))[0]


def on_device(factors, eps_occ, eps_virt, pair_mask):
    rows, occ_rows, virt = factors.shape
    width = occ_rows * virt
    lines = width // LANES
    groups = lax.axis_size("occ")
    shares = lax.axis_size("aux")
    size = rows // CHUNKS
    cut = size * lines
    last = CHUNKS - 1
    group = lax.axis_index("occ")
    place = group % PLANE
    odd_x = place % 2 == 1
    odd_y = place // 2 == 1

    own = factors.reshape(rows * lines, LANES)
    energies = jnp.zeros((SUBLANES * LANES,), jnp.float32).at[:occ_rows].set(eps_occ)
    energies = energies.reshape(SUBLANES, LANES)

    def part(whole, at):
        return whole[at * cut : (at + 1) * cut]

    def swap(block, bit):
        return lax.ppermute(block, "occ", [(g, g ^ bit) for g in range(groups)])

    def up(block):
        return lax.ppermute(block, "occ", [(g, g + PLANE) for g in range(groups - PLANE)])

    def totals(partial):
        if shares == 2:
            return [partial, lax.ppermute(partial, "aux", [(0, 1), (1, 0)])]
        return [lax.psum(partial, "aux")]

    def sign(offset):
        flag = lax.dynamic_index_in_dim(pair_mask[0], offset - 1, 0, keepdims=False)
        return jnp.where((group >= offset) & (flag > 0), -1.0, 0.0).astype(jnp.float32)

    sign_own = jnp.float32(-1.0)
    sign_z = sign(jnp.int32(PLANE))
    sign_x = sign(jnp.where(odd_x, 1, PLANE - 1))
    sign_y = sign(jnp.int32(PLANE // 2))
    sign_d = sign(jnp.where(odd_x, PLANE - 1, 1))

    first_sent = jnp.concatenate([part(own, 0), energies])

    def add(partials, slots, signs, carriers, before=None):
        where = [(first_sent, cut)] + [(carrier, cut) for carrier in carriers]
        return contract(partials, slots, jnp.stack(signs), where, eps_virt[None, :], size, before)

    from_z, from_x, from_y, from_d = [], [], [], []
    from_z.append(up(first_sent))
    high, low, partial_own = prepare(own, rows, width)
    turned = (high, low)
    sums_own = totals(partial_own)
    def slot_of(blocks):
        return [(block, 0) for block in blocks]

    slot_own = [(own, at * cut) for at in range(CHUNKS)]
    ready = [partial_own]
    for at in range(CHUNKS):
        mine, came = lax.optimization_barrier((own, from_z[at]))
        mine = part(mine, at) if at else first_sent
        send_x = after(jnp.where(odd_x, came, mine), *ready)
        send_y = jnp.where(odd_y, came, mine)
        from_x.append(swap(send_x, 1))
        from_y.append(swap(send_y, 2))
        if at < last:
            from_z.append(up(part(after(own, from_z[at], partial_own), at + 1)))
        ready = [from_x[at]]
        from_d.append(swap(after(from_y[at], from_d[at - 1] if at else from_x[0]), 1))

    slot_z, slot_x, slot_y, slot_d = map(slot_of, (from_z, from_x, from_y, from_d))
    partial_z, partial_y = integrate(after(turned, from_x[2]), [slot_z, slot_y], [0, 0], size, width)
    gradient = add(
        [sums_own, totals(partial_z), totals(partial_y)], [slot_own, slot_z, slot_y],
        [sign_own, sign_z, sign_y], [first_sent, from_z[0], from_y[0]],
    )
    turned = after(turned, gradient)
    early = integrate(turned, [slot_x[:last], slot_d[: last - 1]], [0, 0], size, width)
    partial_x, partial_d = integrate(
        turned, [slot_x[last:], slot_d[last - 1 : last]], [last, last - 1], size, width, early
    )
    (partial_d,) = integrate(turned, [slot_d[last:]], [last], size, width, [partial_d])
    gradient = add(
        [totals(partial_x), totals(partial_d)], [slot_x, slot_d],
        [sign_x, sign_d], [from_x[0], from_d[0]], gradient,
    )
    return gradient.reshape(rows, occ_rows, virt)


def solution(mesh):
    if mesh.shape["occ"] % PLANE:
        raise ValueError("incomplete plane")
    in_specs = (P("aux", "occ", None), P("occ"), P(), P("occ", None))
    out_specs = P("aux", "occ", None)
    return jax.shard_map(
        on_device, mesh=mesh, in_specs=in_specs, out_specs=out_specs, check_vma=False
    )
```

```python
import dataclasses
import functools

import jax
import jax.numpy as jnp
from jax import lax
from jax.experimental import pallas as pl
from jax.experimental.pallas import tpu as pltpu
from jax.sharding import PartitionSpec as P

LANES = 128
SUBLANES = 8
PLANE = 4
CHUNKS = 4
VMEM_LIMIT = 60 * 1024 * 1024


def split(value):
    high = value.astype(jnp.bfloat16)
    low = (value - high.astype(jnp.float32)).astype(jnp.bfloat16)
    return high, low


def deep_left(value):
    high, low = split(value)
    return jnp.concatenate([high, low, high], axis=1)


def deep_right(value):
    high, low = split(value)
    return jnp.concatenate([high, high, low], axis=0)


def dot(left, right):
    numbers = (((1,), (0,)), ((), ()))
    return lax.dot_general(left, right, numbers, preferred_element_type=jnp.float32)


def rows_of(ref, start, count, width):
    lines = width // LANES
    columns = [ref[pl.ds(start * lines + at, count, stride=lines), :] for at in range(lines)]
    return jnp.concatenate(columns, axis=1)


def distinct(arrays):
    return list({id(array): array for array in arrays}.values())


class Copies:
    def __init__(self, semaphores):
        self.semaphores = semaphores
        self.used = 0

    def start(self, source, target):
        copy = pltpu.make_async_copy(source, target, self.semaphores.at[self.used])
        self.used += 1
        copy.start()
        return copy

    def start_piece(self, piece, ref_of, flags, count, target):
        made = []
        for array, base in piece.places:
            source = ref_of[id(array)].at[pl.ds(base, count)]
            made.append(pltpu.make_async_copy(source, target, self.semaphores.at[self.used]))
        self.used += 1
        if len(made) == 1:
            made[0].start()
        else:
            pl.when(flags[piece.flag] > 0)(made[0].start)
            pl.when(flags[piece.flag] <= 0)(made[1].start)
        return made[0]


@dataclasses.dataclass(frozen=True)
class Piece:
    places: tuple
    flag: int = 0


def call(kernel, smem, vmem, anywhere, outputs, out_space, scratch):
    spaces = [pltpu.SMEM] * len(smem) + [pltpu.VMEM] * len(vmem) + [pl.ANY] * len(anywhere)
    return pl.pallas_call(
        kernel,
        out_shape=outputs,
        in_specs=[pl.BlockSpec(memory_space=space) for space in spaces],
        out_specs=[pl.BlockSpec(memory_space=out_space)] * len(outputs),
        scratch_shapes=scratch,
        compiler_params=pltpu.CompilerParams(vmem_limit_bytes=VMEM_LIMIT),
        cost_estimate=pl.CostEstimate(flops=0, bytes_accessed=0, transcendentals=0),
    )(*smem, *vmem, *anywhere)


def prepare(own, rows, width):
    size = rows // CHUNKS
    cut = size * width // LANES

    def kernel(own_ref, high_ref, low_ref, integrals_ref, block_ref, semaphores):
        copies = Copies(semaphores)
        coming = [copies.start(own_ref.at[pl.ds(at * cut, cut)], block_ref.at[at]) for at in range(CHUNKS)]
        for at in range(CHUNKS):
            coming[at].wait()
            block = rows_of(block_ref.at[at], 0, size, width)
            high, low = split(block.T)
            high_ref[at] = high
            low_ref[at] = low
            value = dot(jnp.concatenate([high, low, high], axis=1), deep_right(block))
            integrals_ref[...] = integrals_ref[...] + value if at else value

    half = jax.ShapeDtypeStruct((CHUNKS, width, size), jnp.bfloat16)
    square = jax.ShapeDtypeStruct((width, width), jnp.float32)
    scratch = [pltpu.VMEM((CHUNKS, cut, LANES), jnp.float32), pltpu.SemaphoreType.DMA((CHUNKS,))]
    return call(kernel, [], [], [own], [half, half, square], pltpu.VMEM, scratch)


def arrays_of(pieces):
    return distinct([array for piece in pieces for array, _ in piece.places])


def integrate(turned, slots, first, flags, size, width, before=()):
    cut = size * width // LANES
    count = len(slots)
    pieces = [piece for slot in slots for piece in slot]
    arrays = arrays_of(pieces)
    numbers = [list(range(start, start + len(slot))) for slot, start in zip(slots, first)]
    needed = sorted({number for some in numbers for number in some})
    before = list(before)

    def kernel(flag_ref, *refs):
        given = iter(refs)
        high_ref, low_ref = next(given), next(given)
        before_refs = [next(given) for _ in before]
        ref_of = {id(array): next(given) for array in arrays}
        outs = [next(given) for _ in range(count)]
        turned_ref, block_ref, before_ref, semaphores = given
        copies = Copies(semaphores)
        coming, turning = [], {}

        def turn(number):
            if number not in turning:
                at = needed.index(number)
                turning[number] = [
                    copies.start(high_ref.at[number], turned_ref.at[at, 0]),
                    copies.start(low_ref.at[number], turned_ref.at[at, 1]),
                ]

        at = 0
        for slot in range(count):
            for number, piece in zip(numbers[slot], slots[slot]):
                turn(number)
                coming.append(copies.start_piece(piece, ref_of, flag_ref, cut, block_ref.at[at]))
                at += 1
        adding = [copies.start(ref, before_ref.at[slot]) for slot, ref in enumerate(before_refs)]
        at = 0
        for slot in range(count):
            for place, number in enumerate(numbers[slot]):
                for copy in turning.pop(number, []):
                    copy.wait()
                coming[at].wait()
                there = needed.index(number)
                high, low = turned_ref[there, 0], turned_ref[there, 1]
                left = jnp.concatenate([high, low, high], axis=1)
                value = dot(left, deep_right(rows_of(block_ref.at[at], 0, size, width)))
                outs[slot][...] = outs[slot][...] + value if place else value
                at += 1
            if before:
                adding[slot].wait()
                outs[slot][...] += before_ref[slot]

    out = [jax.ShapeDtypeStruct((width, width), jnp.float32)] * count
    scratch = [
        pltpu.VMEM((len(needed), 2, width, size), jnp.bfloat16),
        pltpu.VMEM((len(pieces), cut, LANES), jnp.float32),
        pltpu.VMEM((max(len(before), 1), width, width), jnp.float32),
        pltpu.SemaphoreType.DMA((2 * len(needed) + len(pieces) + len(before),)),
    ]
    return call(kernel, [flags], [], [*turned, *before, *arrays], out, pltpu.VMEM, scratch)


def contract(partials, slots, signs, energies, flags, eps_virt, size, before=None):
    count = len(slots)
    chunks = len(slots[0])
    virt = eps_virt.shape[1]
    width = partials[0][0].shape[0]
    occ_rows = width // virt
    lines = width // LANES
    cut = size * lines
    sums = [array for slot in partials for array in slot]
    pieces = [piece for slot in slots for piece in slot]
    arrays = arrays_of([*pieces, *energies])
    last = [before] if before is not None else []

    def kernel(*refs):
        given = iter(refs)
        sign_ref, flag_ref, virt_ref = next(given), next(given), next(given)
        sum_refs = [next(given) for _ in sums]
        before_refs = [next(given) for _ in last]
        ref_of = {id(array): next(given) for array in arrays}
        out_ref, energy_ref, sum_ref, block_ref, result_ref, right_ref, semaphores = given
        copies = Copies(semaphores)
        arriving = [
            copies.start_piece(piece, ref_of, flag_ref, SUBLANES, energy_ref.at[at])
            for at, piece in enumerate(energies)
        ]
        arriving += [copies.start(ref, sum_ref.at[at]) for at, ref in enumerate(sum_refs)]
        coming = [
            [
                copies.start_piece(slots[slot][at], ref_of, flag_ref, cut, block_ref.at[slot, at])
                for slot in range(count)
            ]
            for at in range(chunks)
        ]
        adding = [
            [copies.start(ref.at[pl.ds(at * cut, cut)], result_ref.at[at]) for ref in before_refs]
            for at in range(chunks)
        ]
        for copy in arriving:
            copy.wait()

        def line(at):
            virtual = virt_ref[...]
            energy = energy_ref[at]
            return jnp.concatenate([virtual - energy[:1, i : i + 1] for i in range(occ_rows)], axis=1)

        row = jnp.broadcast_to(line(0), (SUBLANES, width)).T[:, :1]
        at = 0
        for slot in range(count):
            total = sum_ref[at]
            for extra in range(1, len(partials[slot])):
                total = total + sum_ref[at + extra]
            at += len(partials[slot])
            amplitude = (sign_ref[slot] * total) / (row + line(slot + 1))
            right_ref[pl.ds(slot * 3 * width, 3 * width), :] = deep_right(amplitude.T)
        leaving = []
        for at in range(chunks):
            for copy in coming[at] + adding[at]:
                copy.wait()
            left = [deep_left(rows_of(block_ref.at[slot, at], 0, size, width)) for slot in range(count)]
            value = dot(jnp.concatenate(left, axis=1), right_ref[...])
            for column in range(lines):
                lanes = value[:, column * LANES : (column + 1) * LANES]
                where = pl.ds(column, size, stride=lines)
                if last:
                    lanes = lanes + result_ref[at, where, :]
                result_ref[at, where, :] = lanes
            leaving.append(copies.start(result_ref.at[at], out_ref.at[pl.ds(at * cut, cut)]))
        for copy in leaving:
            copy.wait()

    rows = chunks * size
    out = jax.ShapeDtypeStruct((rows * lines, LANES), jnp.float32)
    scratch = [
        pltpu.VMEM((len(energies), SUBLANES, LANES), jnp.float32),
        pltpu.VMEM((len(sums), width, width), jnp.float32),
        pltpu.VMEM((count, chunks, cut, LANES), jnp.float32),
        pltpu.VMEM((chunks, cut, LANES), jnp.float32),
        pltpu.VMEM((count * 3 * width, width), jnp.bfloat16),
        pltpu.SemaphoreType.DMA((len(energies) + len(sums) + len(pieces) + 2 * chunks,)),
    ]
    return call(kernel, [signs, flags], [eps_virt], [*sums, *last, *arrays], [out], pl.ANY, scratch)[0]


def after(block, *others):
    return lax.optimization_barrier((block, *others))[0]


def on_device(factors, eps_occ, eps_virt, pair_mask):
    rows, occ_rows, virt = factors.shape
    width = occ_rows * virt
    lines = width // LANES
    groups = lax.axis_size("occ")
    shares = lax.axis_size("aux")
    size = rows // CHUNKS
    cut = size * lines
    last = CHUNKS - 1
    group = lax.axis_index("occ")
    place = group % PLANE
    odd_x = place % 2 == 1
    odd_y = place // 2 == 1

    own = factors.reshape(rows * lines, LANES)
    energies = jnp.zeros((SUBLANES * LANES,), jnp.float32).at[:occ_rows].set(eps_occ)
    energies = energies.reshape(SUBLANES, LANES)

    def part(whole, at):
        return whole[at * cut : (at + 1) * cut]

    def within(block, moves):
        planes = range(0, groups, PLANE)
        return lax.ppermute(block, "occ", [(g + a, g + b) for g in planes for a, b in moves])

    def up(block):
        return lax.ppermute(block, "occ", [(g, g + PLANE) for g in range(groups - PLANE)])

    def totals(partial):
        if shares == 2:
            return [partial, lax.ppermute(partial, "aux", [(0, 1), (1, 0)])]
        return [lax.psum(partial, "aux")]

    def sign(offset):
        flag = lax.dynamic_index_in_dim(pair_mask[0], offset - 1, 0, keepdims=False)
        return jnp.where((group >= offset) & (flag > 0), -1.0, 0.0).astype(jnp.float32)

    sign_own = jnp.float32(-1.0)
    sign_z = sign(jnp.int32(PLANE))
    sign_x = sign(jnp.where(odd_x, 1, PLANE - 1))
    sign_y = sign(jnp.int32(PLANE // 2))
    sign_d = sign(jnp.where(odd_x, PLANE - 1, 1))

    first_sent = jnp.concatenate([part(own, 0), energies])
    flags = jnp.stack([odd_x, odd_y]).astype(jnp.int32)

    def add(partials, slots, signs, carriers, before=None):
        return contract(partials, slots, jnp.stack(signs), carriers, flags, eps_virt[None, :], size, before)

    from_z = [up(first_sent)]
    up_x = within(first_sent, [(0, 1), (2, 3), (1, 0)])
    up_y = within(first_sent, [(0, 2), (1, 3)])
    high, low, partial_own = prepare(own, rows, width)
    turned = (high, low)
    sums_own = totals(partial_own)
    swap_x, swap_y = [], []
    passed = [partial_own, up_x, up_y]
    for at in range(CHUNKS):
        came, mine, *_ = lax.optimization_barrier((from_z[at], own, *passed))
        if at < last:
            from_z.append(up(part(mine, at + 1)))
            up_part = part(mine, at + 1)
            if at == 0:
                up_part = jnp.concatenate([up_part, energies])
            swap_x.append(within(jnp.where(odd_x, came, up_part), [(0, 1), (1, 0), (2, 3), (3, 2)]))
            swap_y.append(within(jnp.where(odd_y, came, up_part), [(0, 2), (2, 0), (1, 3), (3, 1)]))
        else:
            swap_x.append(within(came, [(1, 0), (3, 2)]))
            swap_y.append(within(came, [(2, 0), (3, 1)]))
        passed = [swap_x[at], swap_y[at]]
        if at == 0:
            up_d = within(up_x, [(0, 2), (1, 3)])
        if at == 2:
            passed.append(up_d)

    middle = (place == 1) | (place == 2)
    half = CHUNKS // 2
    block = jnp.where(middle, jnp.concatenate(swap_x[:half]), jnp.concatenate(swap_y[:half]))
    block = after(block, swap_x[half], swap_y[half])
    cycle = within(block, [(0, 1), (1, 3), (3, 2), (2, 0)])
    swap_d = [(cycle, 0)] + [(cycle, at * cut + SUBLANES) for at in range(1, half)]
    for at in range(half, CHUNKS):
        moves = [(0, 1), (1, 0), (2, 3), (3, 2)] if at < last else [(0, 1), (1, 0)]
        swap_d.append((within(swap_y[at], moves), 0))

    def pieces_of(first, swaps, flag, base):
        places = [(array, start + base) for array, start in [(first, 0), *swaps]]
        return [Piece((places[at], places[at + 1]), flag) for at in range(CHUNKS)]

    swap_x = [(block, 0) for block in swap_x]
    swap_y = [(block, 0) for block in swap_y]

    def whole(array, base):
        return Piece(((array, base),))

    slot_own = [whole(own, at * cut) for at in range(CHUNKS)]
    slot_z = [whole(block, 0) for block in from_z]
    slot_x = pieces_of(up_x, swap_x, 0, 0)
    slot_y = pieces_of(up_y, swap_y, 1, 0)
    slot_d = pieces_of(up_d, swap_d, 1, 0)
    eps_x = pieces_of(up_x, swap_x, 0, cut)[0]
    eps_y = pieces_of(up_y, swap_y, 1, cut)[0]
    eps_d = pieces_of(up_d, swap_d, 1, cut)[0]

    (partial_z,) = integrate(after(turned, block), [slot_z], [0], flags, size, width)
    gradient = add(
        [sums_own, totals(partial_z)], [slot_own, slot_z], [sign_own, sign_z],
        [whole(first_sent, cut), whole(first_sent, cut), whole(from_z[0], cut)],
    )
    partial_x, partial_y = integrate(turned, [slot_x, slot_y], [0, 0], flags, size, width)
    gradient = add(
        [totals(partial_x), totals(partial_y)], [slot_x, slot_y], [sign_x, sign_y],
        [whole(first_sent, cut), eps_x, eps_y], gradient,
    )
    turned = after(turned, gradient)
    partial_d = integrate(turned, [slot_d[:last]], [0], flags, size, width)
    (partial_d,) = integrate(turned, [slot_d[last:]], [last], flags, size, width, partial_d)
    gradient = add([totals(partial_d)], [slot_d], [sign_d], [whole(first_sent, cut), eps_d], gradient)
    return gradient.reshape(rows, occ_rows, virt)


def solution(mesh):
    if mesh.shape["occ"] % PLANE:
        raise ValueError("incomplete plane")
    in_specs = (P("aux", "occ", None), P("occ"), P(), P("occ", None))
    out_specs = P("aux", "occ", None)
    return jax.shard_map(
        on_device, mesh=mesh, in_specs=in_specs, out_specs=out_specs, check_vma=False
    )
```

```python
import dataclasses
import functools

import jax
import jax.numpy as jnp
from jax import lax
from jax.experimental import pallas as pl
from jax.experimental.pallas import tpu as pltpu
from jax.sharding import PartitionSpec as P

LANES = 128
SUBLANES = 8
PLANE = 4
CHUNKS = 4
VMEM_LIMIT = 60 * 1024 * 1024


def split(value):
    high = value.astype(jnp.bfloat16)
    low = (value - high.astype(jnp.float32)).astype(jnp.bfloat16)
    return high, low


def deep_left(value):
    high, low = split(value)
    return jnp.concatenate([high, low, high], axis=1)


def deep_right(value):
    high, low = split(value)
    return jnp.concatenate([high, high, low], axis=0)


def dot(left, right):
    numbers = (((1,), (0,)), ((), ()))
    return lax.dot_general(left, right, numbers, preferred_element_type=jnp.float32)


def rows_of(ref, start, count, width):
    lines = width // LANES
    columns = [ref[pl.ds(start * lines + at, count, stride=lines), :] for at in range(lines)]
    return jnp.concatenate(columns, axis=1)


def distinct(arrays):
    return list({id(array): array for array in arrays}.values())


class Copies:
    def __init__(self, semaphores):
        self.semaphores = semaphores
        self.used = 0

    def start(self, source, target):
        copy = pltpu.make_async_copy(source, target, self.semaphores.at[self.used])
        self.used += 1
        copy.start()
        return copy

    def start_piece(self, piece, ref_of, flags, count, target):
        made = []
        for array, base in piece.places:
            source = ref_of[id(array)].at[pl.ds(base, count)]
            made.append(pltpu.make_async_copy(source, target, self.semaphores.at[self.used]))
        self.used += 1
        if len(made) == 1:
            made[0].start()
        else:
            pl.when(flags[piece.flag] > 0)(made[0].start)
            pl.when(flags[piece.flag] <= 0)(made[1].start)
        return made[0]


@dataclasses.dataclass(frozen=True)
class Piece:
    places: tuple
    flag: int = 0


def call(kernel, smem, vmem, anywhere, outputs, out_space, scratch):
    spaces = [pltpu.SMEM] * len(smem) + [pltpu.VMEM] * len(vmem) + [pl.ANY] * len(anywhere)
    return pl.pallas_call(
        kernel,
        out_shape=outputs,
        in_specs=[pl.BlockSpec(memory_space=space) for space in spaces],
        out_specs=[pl.BlockSpec(memory_space=out_space)] * len(outputs),
        scratch_shapes=scratch,
        compiler_params=pltpu.CompilerParams(vmem_limit_bytes=VMEM_LIMIT),
        cost_estimate=pl.CostEstimate(flops=0, bytes_accessed=0, transcendentals=0),
    )(*smem, *vmem, *anywhere)


def prepare(own, rows, width):
    size = rows // CHUNKS
    cut = size * width // LANES

    def kernel(own_ref, high_ref, low_ref, integrals_ref, block_ref, semaphores):
        copies = Copies(semaphores)
        coming = [copies.start(own_ref.at[pl.ds(at * cut, cut)], block_ref.at[at]) for at in range(CHUNKS)]
        for at in range(CHUNKS):
            coming[at].wait()
            block = rows_of(block_ref.at[at], 0, size, width)
            high, low = split(block.T)
            high_ref[at] = high
            low_ref[at] = low
            value = dot(jnp.concatenate([high, low, high], axis=1), deep_right(block))
            integrals_ref[...] = integrals_ref[...] + value if at else value

    half = jax.ShapeDtypeStruct((CHUNKS, width, size), jnp.bfloat16)
    square = jax.ShapeDtypeStruct((width, width), jnp.float32)
    scratch = [pltpu.VMEM((CHUNKS, cut, LANES), jnp.float32), pltpu.SemaphoreType.DMA((CHUNKS,))]
    return call(kernel, [], [], [own], [half, half, square], pltpu.VMEM, scratch)


def arrays_of(pieces):
    return distinct([array for piece in pieces for array, _ in piece.places])


def integrate(turned, slots, first, flags, size, width, before=()):
    cut = size * width // LANES
    count = len(slots)
    pieces = [piece for slot in slots for piece in slot]
    arrays = arrays_of(pieces)
    numbers = [list(range(start, start + len(slot))) for slot, start in zip(slots, first)]
    needed = sorted({number for some in numbers for number in some})
    before = list(before)

    def kernel(flag_ref, *refs):
        given = iter(refs)
        high_ref, low_ref = next(given), next(given)
        before_refs = [next(given) for _ in before]
        ref_of = {id(array): next(given) for array in arrays}
        outs = [next(given) for _ in range(count)]
        turned_ref, block_ref, before_ref, semaphores = given
        copies = Copies(semaphores)
        coming, turning = [], {}

        def turn(number):
            if number not in turning:
                at = needed.index(number)
                turning[number] = [
                    copies.start(high_ref.at[number], turned_ref.at[at, 0]),
                    copies.start(low_ref.at[number], turned_ref.at[at, 1]),
                ]

        at = 0
        for slot in range(count):
            for number, piece in zip(numbers[slot], slots[slot]):
                turn(number)
                coming.append(copies.start_piece(piece, ref_of, flag_ref, cut, block_ref.at[at]))
                at += 1
        adding = [copies.start(ref, before_ref.at[slot]) for slot, ref in enumerate(before_refs)]
        at = 0
        for slot in range(count):
            for place, number in enumerate(numbers[slot]):
                for copy in turning.pop(number, []):
                    copy.wait()
                coming[at].wait()
                there = needed.index(number)
                high, low = turned_ref[there, 0], turned_ref[there, 1]
                left = jnp.concatenate([high, low, high], axis=1)
                value = dot(left, deep_right(rows_of(block_ref.at[at], 0, size, width)))
                outs[slot][...] = outs[slot][...] + value if place else value
                at += 1
            if before:
                adding[slot].wait()
                outs[slot][...] += before_ref[slot]

    out = [jax.ShapeDtypeStruct((width, width), jnp.float32)] * count
    scratch = [
        pltpu.VMEM((len(needed), 2, width, size), jnp.bfloat16),
        pltpu.VMEM((len(pieces), cut, LANES), jnp.float32),
        pltpu.VMEM((max(len(before), 1), width, width), jnp.float32),
        pltpu.SemaphoreType.DMA((2 * len(needed) + len(pieces) + len(before),)),
    ]
    return call(kernel, [flags], [], [*turned, *before, *arrays], out, pltpu.VMEM, scratch)


def contract(partials, slots, signs, energies, flags, eps_virt, size, before=None):
    count = len(slots)
    chunks = len(slots[0])
    virt = eps_virt.shape[1]
    width = partials[0][0].shape[0]
    occ_rows = width // virt
    lines = width // LANES
    cut = size * lines
    sums = [array for slot in partials for array in slot]
    pieces = [piece for slot in slots for piece in slot]
    arrays = arrays_of([*pieces, *energies])
    last = [before] if before is not None else []

    def kernel(*refs):
        given = iter(refs)
        sign_ref, flag_ref, virt_ref = next(given), next(given), next(given)
        sum_refs = [next(given) for _ in sums]
        before_refs = [next(given) for _ in last]
        ref_of = {id(array): next(given) for array in arrays}
        out_ref, energy_ref, sum_ref, block_ref, result_ref, right_ref, semaphores = given
        copies = Copies(semaphores)
        arriving = [
            copies.start_piece(piece, ref_of, flag_ref, SUBLANES, energy_ref.at[at])
            for at, piece in enumerate(energies)
        ]
        arriving += [copies.start(ref, sum_ref.at[at]) for at, ref in enumerate(sum_refs)]
        coming = [
            [
                copies.start_piece(slots[slot][at], ref_of, flag_ref, cut, block_ref.at[slot, at])
                for slot in range(count)
            ]
            for at in range(chunks)
        ]
        adding = [
            [copies.start(ref.at[pl.ds(at * cut, cut)], result_ref.at[at]) for ref in before_refs]
            for at in range(chunks)
        ]
        for copy in arriving:
            copy.wait()

        def line(at):
            virtual = virt_ref[...]
            energy = energy_ref[at]
            return jnp.concatenate([virtual - energy[:1, i : i + 1] for i in range(occ_rows)], axis=1)

        row = jnp.broadcast_to(line(0), (SUBLANES, width)).T[:, :1]
        at = 0
        for slot in range(count):
            total = sum_ref[at]
            for extra in range(1, len(partials[slot])):
                total = total + sum_ref[at + extra]
            at += len(partials[slot])
            amplitude = (sign_ref[slot] * total) / (row + line(slot + 1))
            right_ref[pl.ds(slot * 3 * width, 3 * width), :] = deep_right(amplitude.T)
        leaving = []
        for at in range(chunks):
            for copy in coming[at] + adding[at]:
                copy.wait()
            left = [deep_left(rows_of(block_ref.at[slot, at], 0, size, width)) for slot in range(count)]
            value = dot(jnp.concatenate(left, axis=1), right_ref[...])
            for column in range(lines):
                lanes = value[:, column * LANES : (column + 1) * LANES]
                where = pl.ds(column, size, stride=lines)
                if last:
                    lanes = lanes + result_ref[at, where, :]
                result_ref[at, where, :] = lanes
            leaving.append(copies.start(result_ref.at[at], out_ref.at[pl.ds(at * cut, cut)]))
        for copy in leaving:
            copy.wait()

    rows = chunks * size
    out = jax.ShapeDtypeStruct((rows * lines, LANES), jnp.float32)
    scratch = [
        pltpu.VMEM((len(energies), SUBLANES, LANES), jnp.float32),
        pltpu.VMEM((len(sums), width, width), jnp.float32),
        pltpu.VMEM((count, chunks, cut, LANES), jnp.float32),
        pltpu.VMEM((chunks, cut, LANES), jnp.float32),
        pltpu.VMEM((count * 3 * width, width), jnp.bfloat16),
        pltpu.SemaphoreType.DMA((len(energies) + len(sums) + len(pieces) + 2 * chunks,)),
    ]
    return call(kernel, [signs, flags], [eps_virt], [*sums, *last, *arrays], [out], pl.ANY, scratch)[0]


def after(block, *others):
    return lax.optimization_barrier((block, *others))[0]


def on_device(factors, eps_occ, eps_virt, pair_mask):
    rows, occ_rows, virt = factors.shape
    width = occ_rows * virt
    lines = width // LANES
    groups = lax.axis_size("occ")
    shares = lax.axis_size("aux")
    size = rows // CHUNKS
    cut = size * lines
    last = CHUNKS - 1
    group = lax.axis_index("occ")
    place = group % PLANE
    odd_x = place % 2 == 1
    odd_y = place // 2 == 1

    own = factors.reshape(rows * lines, LANES)
    energies = jnp.zeros((SUBLANES * LANES,), jnp.float32).at[:occ_rows].set(eps_occ)
    energies = energies.reshape(SUBLANES, LANES)

    def part(whole, at):
        return whole[at * cut : (at + 1) * cut]

    def within(block, moves):
        planes = range(0, groups, PLANE)
        return lax.ppermute(block, "occ", [(g + a, g + b) for g in planes for a, b in moves])

    def up(block):
        return lax.ppermute(block, "occ", [(g, g + PLANE) for g in range(groups - PLANE)])

    def totals(partial):
        if shares == 2:
            return [partial, lax.ppermute(partial, "aux", [(0, 1), (1, 0)])]
        return [lax.psum(partial, "aux")]

    def sign(offset):
        flag = lax.dynamic_index_in_dim(pair_mask[0], offset - 1, 0, keepdims=False)
        return jnp.where((group >= offset) & (flag > 0), -1.0, 0.0).astype(jnp.float32)

    sign_own = jnp.float32(-1.0)
    sign_z = sign(jnp.int32(PLANE))
    sign_x = sign(jnp.where(odd_x, 1, PLANE - 1))
    sign_y = sign(jnp.int32(PLANE // 2))
    sign_d = sign(jnp.where(odd_x, PLANE - 1, 1))

    first_sent = jnp.concatenate([part(own, 0), energies])
    flags = jnp.stack([odd_x, odd_y]).astype(jnp.int32)

    def add(partials, slots, signs, carriers, before=None):
        return contract(partials, slots, jnp.stack(signs), carriers, flags, eps_virt[None, :], size, before)

    from_z = [up(first_sent)]
    up_x = within(first_sent, [(0, 1), (2, 3), (1, 0)])
    up_y = within(first_sent, [(0, 2), (1, 3)])
    high, low, partial_own = prepare(own, rows, width)
    turned = (high, low)
    sums_own = totals(partial_own)
    swap_x, swap_y, swap_d = [], [], []
    middle = (place == 1) | (place == 2)
    for at in range(CHUNKS):
        came, mine = lax.optimization_barrier((from_z[at], own))
        if at < last:
            up_part = part(mine, at + 1)
            if at == 0:
                up_part = jnp.concatenate([up_part, energies])
            send_x, send_y = jnp.where(odd_x, came, up_part), jnp.where(odd_y, came, up_part)
            moves_x, moves_y = [(0, 1), (1, 0), (2, 3), (3, 2)], [(0, 2), (2, 0), (1, 3), (3, 1)]
            from_z.append(up(part(after(own, from_z[at], partial_own), at + 1)))
        else:
            send_x, send_y = came, came
            moves_x, moves_y = [(1, 0), (3, 2)], [(2, 0), (3, 1)]
        swap_x.append(within(after(send_x, swap_x[at - 1] if at else (partial_own, up_x)), moves_x))
        swap_y.append(within(after(send_y, swap_y[at - 1] if at else up_y), moves_y))
        if at == 0:
            up_d = within(up_x, [(0, 2), (1, 3)])
            send_d, moves_d = jnp.where(middle, swap_x[0], swap_y[0]), [(0, 1), (1, 3), (3, 2), (2, 0)]
        else:
            send_d, moves_d = after(swap_y[at], swap_d[at - 1]), moves_x if at < last else [(0, 1), (1, 0)]
        swap_d.append(within(send_d, moves_d))

    def pieces_of(first, swaps, flag, base):
        places = [(array, base) for array in [first, *swaps]]
        return [Piece((places[at], places[at + 1]), flag) for at in range(CHUNKS)]

    def whole(array, base):
        return Piece(((array, base),))

    slot_own = [whole(own, at * cut) for at in range(CHUNKS)]
    slot_z = [whole(block, 0) for block in from_z]
    slot_x = pieces_of(up_x, swap_x, 0, 0)
    slot_y = pieces_of(up_y, swap_y, 1, 0)
    slot_d = pieces_of(up_d, swap_d, 1, 0)
    eps_x = pieces_of(up_x, swap_x, 0, cut)[0]
    eps_y = pieces_of(up_y, swap_y, 1, cut)[0]
    eps_d = pieces_of(up_d, swap_d, 1, cut)[0]

    partial_z, partial_y = integrate(
        after(turned, swap_x[2]), [slot_z, slot_y], [0, 0], flags, size, width
    )
    own_eps = whole(first_sent, cut)
    gradient = add(
        [sums_own, totals(partial_z), totals(partial_y)], [slot_own, slot_z, slot_y],
        [sign_own, sign_z, sign_y], [own_eps, own_eps, whole(from_z[0], cut), eps_y],
    )
    turned = after(turned, gradient)
    early = integrate(turned, [slot_x[:last], slot_d[: last - 1]], [0, 0], flags, size, width)
    partial_x, partial_d = integrate(
        turned, [slot_x[last:], slot_d[last - 1 : last]], [last, last - 1], flags, size, width, early
    )
    (partial_d,) = integrate(turned, [slot_d[last:]], [last], flags, size, width, [partial_d])
    gradient = add(
        [totals(partial_x), totals(partial_d)], [slot_x, slot_d], [sign_x, sign_d], [own_eps, eps_x, eps_d], gradient
    )
    return gradient.reshape(rows, occ_rows, virt)


def solution(mesh):
    if mesh.shape["occ"] % PLANE:
        raise ValueError("incomplete plane")
    in_specs = (P("aux", "occ", None), P("occ"), P(), P("occ", None))
    out_specs = P("aux", "occ", None)
    return jax.shard_map(
        on_device, mesh=mesh, in_specs=in_specs, out_specs=out_specs, check_vma=False
    )
```

```python
import functools

import jax
import jax.numpy as jnp
from jax import lax
from jax.experimental import pallas as pl
from jax.experimental.pallas import tpu as pltpu
from jax.sharding import PartitionSpec as P

LANES = 128
SUBLANES = 8
PLANE = 4
CHUNKS = 4
PART_BYTES = 64 * 1024
VMEM_LIMIT = 60 * 1024 * 1024


def split(value):
    high = value.astype(jnp.bfloat16)
    low = (value - high.astype(jnp.float32)).astype(jnp.bfloat16)
    return high, low


def deep_left(value):
    high, low = split(value)
    return jnp.concatenate([high, low, high], axis=1)


def deep_right(value):
    high, low = split(value)
    return jnp.concatenate([high, high, low], axis=0)


def dot(left, right):
    numbers = (((1,), (0,)), ((), ()))
    return lax.dot_general(left, right, numbers, preferred_element_type=jnp.float32)


def rows_of(ref, start, count, width):
    lines = width // LANES
    columns = [ref[pl.ds(start * lines + at, count, stride=lines), :] for at in range(lines)]
    return jnp.concatenate(columns, axis=1)


def distinct(arrays):
    return list({id(array): array for array in arrays}.values())


class Copies:
    def __init__(self, semaphores):
        self.semaphores = semaphores
        self.used = 0

    def start(self, source, target):
        semaphore = self.semaphores.at[self.used]
        self.used += 1
        rows = source.shape[0]
        step = max(min(rows, PART_BYTES * rows // (source.size * source.dtype.itemsize) // 16 * 16), 16)
        for at in range(0, rows, step):
            part = pl.ds(at, min(step, rows - at))
            pltpu.make_async_copy(source.at[part], target.at[part], semaphore).start()
        return pltpu.make_async_copy(source, target, semaphore)


def call(kernel, smem, vmem, anywhere, outputs, out_space, scratch, flops):
    spaces = [pltpu.SMEM] * len(smem) + [pltpu.VMEM] * len(vmem) + [pl.ANY] * len(anywhere)
    moved = sum(a.size * a.dtype.itemsize for a in (*vmem, *anywhere, *outputs))
    return pl.pallas_call(
        kernel,
        out_shape=outputs,
        in_specs=[pl.BlockSpec(memory_space=space) for space in spaces],
        out_specs=[pl.BlockSpec(memory_space=out_space)] * len(outputs),
        scratch_shapes=scratch,
        compiler_params=pltpu.CompilerParams(vmem_limit_bytes=VMEM_LIMIT),
        cost_estimate=pl.CostEstimate(flops=flops, bytes_accessed=moved, transcendentals=0),
    )(*smem, *vmem, *anywhere)


def prepare(own, rows, width):
    size = rows // CHUNKS
    cut = size * width // LANES

    def kernel(own_ref, high_ref, low_ref, integrals_ref, block_ref, semaphores):
        copies = Copies(semaphores)
        coming = [copies.start(own_ref.at[pl.ds(at * cut, cut)], block_ref.at[at]) for at in range(CHUNKS)]
        for at in range(CHUNKS):
            coming[at].wait()
            block = rows_of(block_ref.at[at], 0, size, width)
            high, low = split(block.T)
            high_ref[at] = high
            low_ref[at] = low
            value = dot(jnp.concatenate([high, low, high], axis=1), deep_right(block))
            integrals_ref[...] = integrals_ref[...] + value if at else value

    half = jax.ShapeDtypeStruct((CHUNKS, width, size), jnp.bfloat16)
    square = jax.ShapeDtypeStruct((width, width), jnp.float32)
    scratch = [pltpu.VMEM((CHUNKS, cut, LANES), jnp.float32), pltpu.SemaphoreType.DMA((CHUNKS,))]
    flops = 6 * rows * width * width
    return call(kernel, [], [], [own], [half, half, square], pltpu.VMEM, scratch, flops)


def integrate(turned, slots, first, size, width, before=()):
    cut = size * width // LANES
    count = len(slots)
    pieces = [piece for slot in slots for piece in slot]
    arrays = distinct([array for array, _ in pieces])
    numbers = [list(range(start, start + len(slot))) for slot, start in zip(slots, first)]
    needed = sorted({number for some in numbers for number in some})
    before = list(before)

    def kernel(*refs):
        given = iter(refs)
        high_ref, low_ref = next(given), next(given)
        before_refs = [next(given) for _ in before]
        ref_of = {id(array): next(given) for array in arrays}
        outs = [next(given) for _ in range(count)]
        turned_ref, block_ref, before_ref, semaphores = given
        copies = Copies(semaphores)
        coming, turning = [], {}

        def turn(number):
            if number not in turning:
                at = needed.index(number)
                turning[number] = [
                    copies.start(high_ref.at[number], turned_ref.at[at, 0]),
                    copies.start(low_ref.at[number], turned_ref.at[at, 1]),
                ]

        at = 0
        for slot in range(count):
            for number, (array, base) in zip(numbers[slot], slots[slot]):
                turn(number)
                coming.append(copies.start(ref_of[id(array)].at[pl.ds(base, cut)], block_ref.at[at]))
                at += 1
        adding = [copies.start(ref, before_ref.at[slot]) for slot, ref in enumerate(before_refs)]
        at = 0
        for slot in range(count):
            for place, number in enumerate(numbers[slot]):
                for copy in turning.pop(number, []):
                    copy.wait()
                coming[at].wait()
                there = needed.index(number)
                high, low = turned_ref[there, 0], turned_ref[there, 1]
                left = jnp.concatenate([high, low, high], axis=1)
                value = dot(left, deep_right(rows_of(block_ref.at[at], 0, size, width)))
                outs[slot][...] = outs[slot][...] + value if place else value
                at += 1
            if before:
                adding[slot].wait()
                outs[slot][...] += before_ref[slot]

    out = [jax.ShapeDtypeStruct((width, width), jnp.float32)] * count
    scratch = [
        pltpu.VMEM((len(needed), 2, width, size), jnp.bfloat16),
        pltpu.VMEM((len(pieces), cut, LANES), jnp.float32),
        pltpu.VMEM((max(len(before), 1), width, width), jnp.float32),
        pltpu.SemaphoreType.DMA((2 * len(needed) + len(pieces) + len(before),)),
    ]
    flops = 6 * len(pieces) * size * width * width
    return call(kernel, [], [], [*turned, *before, *arrays], out, pltpu.VMEM, scratch, flops)


def contract(partials, slots, signs, energies, eps_virt, size, before=None):
    count = len(slots)
    chunks = len(slots[0])
    virt = eps_virt.shape[1]
    width = partials[0][0].shape[0]
    occ_rows = width // virt
    lines = width // LANES
    cut = size * lines
    sums = [array for slot in partials for array in slot]
    pieces = [piece for slot in slots for piece in slot]
    arrays = distinct([array for array, _ in (*pieces, *energies)])
    last = [before] if before is not None else []

    def kernel(*refs):
        given = iter(refs)
        sign_ref, virt_ref = next(given), next(given)
        sum_refs = [next(given) for _ in sums]
        before_refs = [next(given) for _ in last]
        ref_of = {id(array): next(given) for array in arrays}
        out_ref, energy_ref, sum_ref, block_ref, result_ref, right_ref, semaphores = given
        copies = Copies(semaphores)
        arriving = [
            copies.start(ref_of[id(array)].at[pl.ds(base, SUBLANES)], energy_ref.at[at])
            for at, (array, base) in enumerate(energies)
        ]
        arriving += [copies.start(ref, sum_ref.at[at]) for at, ref in enumerate(sum_refs)]
        coming = [
            [
                copies.start(ref_of[id(slots[slot][at][0])].at[pl.ds(slots[slot][at][1], cut)], block_ref.at[slot, at])
                for slot in range(count)
            ]
            for at in range(chunks)
        ]
        adding = [
            [copies.start(ref.at[pl.ds(at * cut, cut)], result_ref.at[at]) for ref in before_refs]
            for at in range(chunks)
        ]
        for copy in arriving:
            copy.wait()

        def line(at):
            virtual = virt_ref[...]
            energy = energy_ref[at]
            return jnp.concatenate([virtual - energy[:1, i : i + 1] for i in range(occ_rows)], axis=1)

        row = jnp.broadcast_to(line(0), (SUBLANES, width)).T[:, :1]
        at = 0
        for slot in range(count):
            total = sum_ref[at]
            for extra in range(1, len(partials[slot])):
                total = total + sum_ref[at + extra]
            at += len(partials[slot])
            amplitude = (sign_ref[slot] * total) / (row + line(slot + 1))
            right_ref[pl.ds(slot * 3 * width, 3 * width), :] = deep_right(amplitude.T)
        leaving = []
        for at in range(chunks):
            for copy in coming[at] + adding[at]:
                copy.wait()
            left = [deep_left(rows_of(block_ref.at[slot, at], 0, size, width)) for slot in range(count)]
            value = dot(jnp.concatenate(left, axis=1), right_ref[...])
            for column in range(lines):
                lanes = value[:, column * LANES : (column + 1) * LANES]
                where = pl.ds(column, size, stride=lines)
                if last:
                    lanes = lanes + result_ref[at, where, :]
                result_ref[at, where, :] = lanes
            leaving.append(copies.start(result_ref.at[at], out_ref.at[pl.ds(at * cut, cut)]))
        for copy in leaving:
            copy.wait()

    rows = chunks * size
    out = jax.ShapeDtypeStruct((rows * lines, LANES), jnp.float32)
    scratch = [
        pltpu.VMEM((len(energies), SUBLANES, LANES), jnp.float32),
        pltpu.VMEM((len(sums), width, width), jnp.float32),
        pltpu.VMEM((count, chunks, cut, LANES), jnp.float32),
        pltpu.VMEM((chunks, cut, LANES), jnp.float32),
        pltpu.VMEM((count * 3 * width, width), jnp.bfloat16),
        pltpu.SemaphoreType.DMA((len(energies) + len(sums) + len(pieces) + 2 * chunks,)),
    ]
    flops = 6 * count * rows * width * width
    return call(kernel, [signs], [eps_virt], [*sums, *last, *arrays], [out], pl.ANY, scratch, flops)[0]


def after(block, *others):
    return lax.optimization_barrier((block, *others))[0]


def on_device(factors, eps_occ, eps_virt, pair_mask):
    rows, occ_rows, virt = factors.shape
    width = occ_rows * virt
    lines = width // LANES
    groups = lax.axis_size("occ")
    shares = lax.axis_size("aux")
    size = rows // CHUNKS
    cut = size * lines
    last = CHUNKS - 1
    group = lax.axis_index("occ")
    place = group % PLANE
    odd_x = place % 2 == 1
    odd_y = place // 2 == 1

    own = factors.reshape(rows * lines, LANES)
    energies = jnp.zeros((SUBLANES * LANES,), jnp.float32).at[:occ_rows].set(eps_occ)
    energies = energies.reshape(SUBLANES, LANES)

    def part(whole, at):
        return whole[at * cut : (at + 1) * cut]

    def swap(block, bit):
        return lax.ppermute(block, "occ", [(g, g ^ bit) for g in range(groups)])

    def up(block):
        return lax.ppermute(block, "occ", [(g, g + PLANE) for g in range(groups - PLANE)])

    def totals(partial):
        if shares == 2:
            return [partial, lax.ppermute(partial, "aux", [(0, 1), (1, 0)])]
        return [lax.psum(partial, "aux")]

    def sign(offset):
        flag = lax.dynamic_index_in_dim(pair_mask[0], offset - 1, 0, keepdims=False)
        return jnp.where((group >= offset) & (flag > 0), -1.0, 0.0).astype(jnp.float32)

    sign_own = jnp.float32(-1.0)
    sign_z = sign(jnp.int32(PLANE))
    sign_x = sign(jnp.where(odd_x, 1, PLANE - 1))
    sign_y = sign(jnp.int32(PLANE // 2))
    sign_d = sign(jnp.where(odd_x, PLANE - 1, 1))

    first_sent = jnp.concatenate([part(own, 0), energies])

    def add(partials, slots, signs, carriers, before=None):
        where = [(first_sent, cut)] + [(carrier, cut) for carrier in carriers]
        return contract(partials, slots, jnp.stack(signs), where, eps_virt[None, :], size, before)

    from_z, from_x, from_y, from_d = [], [], [], []
    from_z.append(up(first_sent))
    high, low, partial_own = prepare(own, rows, width)
    turned = (high, low)
    sums_own = totals(partial_own)
    def slot_of(blocks):
        return [(block, 0) for block in blocks]

    slot_own = [(own, at * cut) for at in range(CHUNKS)]
    ready = [partial_own]
    for at in range(CHUNKS):
        mine, came = lax.optimization_barrier((own, from_z[at]))
        mine = part(mine, at) if at else first_sent
        send_x = after(jnp.where(odd_x, came, mine), *ready)
        send_y = jnp.where(odd_y, came, mine)
        from_x.append(swap(send_x, 1))
        from_y.append(swap(send_y, 2))
        if at < last:
            from_z.append(up(part(after(own, from_z[at], partial_own), at + 1)))
        ready = [from_x[at], from_y[0]]
        from_d.append(swap(after(from_y[at], from_d[at - 1] if at else from_x[0]), 1))

    slot_z, slot_x, slot_y, slot_d = map(slot_of, (from_z, from_x, from_y, from_d))
    partial_z, partial_y = integrate(after(turned, from_x[2]), [slot_z, slot_y], [0, 0], size, width)
    gradient = add(
        [sums_own, totals(partial_z), totals(partial_y)], [slot_own, slot_z, slot_y],
        [sign_own, sign_z, sign_y], [first_sent, from_z[0], from_y[0]],
    )
    turned = after(turned, gradient)
    early = integrate(turned, [slot_x[:last], slot_d[: last - 1]], [0, 0], size, width)
    partial_x, partial_d = integrate(
        turned, [slot_x[last:], slot_d[last - 1 : last]], [last, last - 1], size, width, early
    )
    (partial_d,) = integrate(turned, [slot_d[last:]], [last], size, width, [partial_d])
    gradient = add(
        [totals(partial_x), totals(partial_d)], [slot_x, slot_d],
        [sign_x, sign_d], [from_x[0], from_d[0]], gradient,
    )
    return gradient.reshape(rows, occ_rows, virt)


def solution(mesh):
    if mesh.shape["occ"] % PLANE:
        raise ValueError("incomplete plane")
    in_specs = (P("aux", "occ", None), P("occ"), P(), P("occ", None))
    out_specs = P("aux", "occ", None)
    return jax.shard_map(
        on_device, mesh=mesh, in_specs=in_specs, out_specs=out_specs, check_vma=False
    )
```

```python
import dataclasses
import functools

import jax
import jax.numpy as jnp
from jax import lax
from jax.experimental import pallas as pl
from jax.experimental.pallas import tpu as pltpu
from jax.sharding import PartitionSpec as P

LANES = 128
SUBLANES = 8
PLANE = 4
CHUNKS = 4
VMEM_LIMIT = 60 * 1024 * 1024


def split(value):
    high = value.astype(jnp.bfloat16)
    low = (value - high.astype(jnp.float32)).astype(jnp.bfloat16)
    return high, low


def deep_left(value):
    high, low = split(value)
    return jnp.concatenate([high, low, high], axis=1)


def deep_right(value):
    high, low = split(value)
    return jnp.concatenate([high, high, low], axis=0)


def dot(left, right):
    numbers = (((1,), (0,)), ((), ()))
    return lax.dot_general(left, right, numbers, preferred_element_type=jnp.float32)


def rows_of(ref, start, count, width):
    lines = width // LANES
    columns = [ref[pl.ds(start * lines + at, count, stride=lines), :] for at in range(lines)]
    return jnp.concatenate(columns, axis=1)


def distinct(arrays):
    return list({id(array): array for array in arrays}.values())


class Copies:
    def __init__(self, semaphores):
        self.semaphores = semaphores
        self.used = 0

    def start(self, source, target):
        copy = pltpu.make_async_copy(source, target, self.semaphores.at[self.used])
        self.used += 1
        copy.start()
        return copy

    def start_piece(self, piece, ref_of, choices, count, target):
        made = []
        for array, base in piece.places:
            source = ref_of[id(array)].at[pl.ds(base, count)]
            made.append(pltpu.make_async_copy(source, target, self.semaphores.at[self.used]))
        self.used += 1
        if len(made) == 1:
            made[0].start()
        else:
            for at, copy in enumerate(made):
                pl.when(choices[piece.choice] == at)(copy.start)
        return made[0]


@dataclasses.dataclass(frozen=True)
class Piece:
    places: tuple
    choice: int = 0


def call(kernel, smem, vmem, anywhere, outputs, out_space, scratch):
    spaces = [pltpu.SMEM] * len(smem) + [pltpu.VMEM] * len(vmem) + [pl.ANY] * len(anywhere)
    return pl.pallas_call(
        kernel,
        out_shape=outputs,
        in_specs=[pl.BlockSpec(memory_space=space) for space in spaces],
        out_specs=[pl.BlockSpec(memory_space=out_space)] * len(outputs),
        scratch_shapes=scratch,
        compiler_params=pltpu.CompilerParams(vmem_limit_bytes=VMEM_LIMIT),
        cost_estimate=pl.CostEstimate(flops=0, bytes_accessed=0, transcendentals=0),
    )(*smem, *vmem, *anywhere)


def prepare(own, rows, width):
    size = rows // CHUNKS
    cut = size * width // LANES

    def kernel(own_ref, high_ref, low_ref, integrals_ref, block_ref, semaphores):
        copies = Copies(semaphores)
        coming = [copies.start(own_ref.at[pl.ds(at * cut, cut)], block_ref.at[at]) for at in range(CHUNKS)]
        for at in range(CHUNKS):
            coming[at].wait()
            block = rows_of(block_ref.at[at], 0, size, width)
            high, low = split(block.T)
            high_ref[at] = high
            low_ref[at] = low
            value = dot(jnp.concatenate([high, low, high], axis=1), deep_right(block))
            integrals_ref[...] = integrals_ref[...] + value if at else value

    half = jax.ShapeDtypeStruct((CHUNKS, width, size), jnp.bfloat16)
    square = jax.ShapeDtypeStruct((width, width), jnp.float32)
    scratch = [pltpu.VMEM((CHUNKS, cut, LANES), jnp.float32), pltpu.SemaphoreType.DMA((CHUNKS,))]
    return call(kernel, [], [], [own], [half, half, square], pltpu.VMEM, scratch)


def arrays_of(pieces):
    return distinct([array for piece in pieces for array, _ in piece.places])


def integrate(turned, slots, first, flags, size, width, before=()):
    cut = size * width // LANES
    count = len(slots)
    pieces = [piece for slot in slots for piece in slot]
    arrays = arrays_of(pieces)
    numbers = [list(range(start, start + len(slot))) for slot, start in zip(slots, first)]
    needed = sorted({number for some in numbers for number in some})
    before = list(before)

    def kernel(flag_ref, *refs):
        given = iter(refs)
        high_ref, low_ref = next(given), next(given)
        before_refs = [next(given) for _ in before]
        ref_of = {id(array): next(given) for array in arrays}
        outs = [next(given) for _ in range(count)]
        turned_ref, block_ref, before_ref, semaphores = given
        copies = Copies(semaphores)
        coming, turning = [], {}

        def turn(number):
            if number not in turning:
                at = needed.index(number)
                turning[number] = [
                    copies.start(high_ref.at[number], turned_ref.at[at, 0]),
                    copies.start(low_ref.at[number], turned_ref.at[at, 1]),
                ]

        at = 0
        for slot in range(count):
            for number, piece in zip(numbers[slot], slots[slot]):
                turn(number)
                coming.append(copies.start_piece(piece, ref_of, flag_ref, cut, block_ref.at[at]))
                at += 1
        adding = [copies.start(ref, before_ref.at[slot]) for slot, ref in enumerate(before_refs)]
        at = 0
        for slot in range(count):
            for place, number in enumerate(numbers[slot]):
                for copy in turning.pop(number, []):
                    copy.wait()
                coming[at].wait()
                there = needed.index(number)
                high, low = turned_ref[there, 0], turned_ref[there, 1]
                left = jnp.concatenate([high, low, high], axis=1)
                value = dot(left, deep_right(rows_of(block_ref.at[at], 0, size, width)))
                outs[slot][...] = outs[slot][...] + value if place else value
                at += 1
            if before:
                adding[slot].wait()
                outs[slot][...] += before_ref[slot]

    out = [jax.ShapeDtypeStruct((width, width), jnp.float32)] * count
    scratch = [
        pltpu.VMEM((len(needed), 2, width, size), jnp.bfloat16),
        pltpu.VMEM((len(pieces), cut, LANES), jnp.float32),
        pltpu.VMEM((max(len(before), 1), width, width), jnp.float32),
        pltpu.SemaphoreType.DMA((2 * len(needed) + len(pieces) + len(before),)),
    ]
    return call(kernel, [flags], [], [*turned, *before, *arrays], out, pltpu.VMEM, scratch)


def contract(partials, slots, signs, energies, flags, eps_virt, size, before=None):
    count = len(slots)
    chunks = len(slots[0])
    virt = eps_virt.shape[1]
    width = partials[0][0].shape[0]
    occ_rows = width // virt
    lines = width // LANES
    cut = size * lines
    sums = [array for slot in partials for array in slot]
    pieces = [piece for slot in slots for piece in slot]
    arrays = arrays_of([*pieces, *energies])
    last = [before] if before is not None else []

    def kernel(*refs):
        given = iter(refs)
        sign_ref, flag_ref, virt_ref = next(given), next(given), next(given)
        sum_refs = [next(given) for _ in sums]
        before_refs = [next(given) for _ in last]
        ref_of = {id(array): next(given) for array in arrays}
        out_ref, energy_ref, sum_ref, block_ref, result_ref, right_ref, semaphores = given
        copies = Copies(semaphores)
        arriving = [
            copies.start_piece(piece, ref_of, flag_ref, SUBLANES, energy_ref.at[at])
            for at, piece in enumerate(energies)
        ]
        arriving += [copies.start(ref, sum_ref.at[at]) for at, ref in enumerate(sum_refs)]
        coming = [
            [
                copies.start_piece(slots[slot][at], ref_of, flag_ref, cut, block_ref.at[slot, at])
                for slot in range(count)
            ]
            for at in range(chunks)
        ]
        adding = [
            [copies.start(ref.at[pl.ds(at * cut, cut)], result_ref.at[at]) for ref in before_refs]
            for at in range(chunks)
        ]
        for copy in arriving:
            copy.wait()

        def line(at):
            virtual = virt_ref[...]
            energy = energy_ref[at]
            return jnp.concatenate([virtual - energy[:1, i : i + 1] for i in range(occ_rows)], axis=1)

        row = jnp.broadcast_to(line(0), (SUBLANES, width)).T[:, :1]
        at = 0
        for slot in range(count):
            total = sum_ref[at]
            for extra in range(1, len(partials[slot])):
                total = total + sum_ref[at + extra]
            at += len(partials[slot])
            amplitude = (sign_ref[slot] * total) / (row + line(slot + 1))
            right_ref[pl.ds(slot * 3 * width, 3 * width), :] = deep_right(amplitude.T)
        leaving = []
        for at in range(chunks):
            for copy in coming[at] + adding[at]:
                copy.wait()
            left = [deep_left(rows_of(block_ref.at[slot, at], 0, size, width)) for slot in range(count)]
            value = dot(jnp.concatenate(left, axis=1), right_ref[...])
            for column in range(lines):
                lanes = value[:, column * LANES : (column + 1) * LANES]
                where = pl.ds(column, size, stride=lines)
                if last:
                    lanes = lanes + result_ref[at, where, :]
                result_ref[at, where, :] = lanes
            leaving.append(copies.start(result_ref.at[at], out_ref.at[pl.ds(at * cut, cut)]))
        for copy in leaving:
            copy.wait()

    rows = chunks * size
    out = jax.ShapeDtypeStruct((rows * lines, LANES), jnp.float32)
    scratch = [
        pltpu.VMEM((len(energies), SUBLANES, LANES), jnp.float32),
        pltpu.VMEM((len(sums), width, width), jnp.float32),
        pltpu.VMEM((count, chunks, cut, LANES), jnp.float32),
        pltpu.VMEM((chunks, cut, LANES), jnp.float32),
        pltpu.VMEM((count * 3 * width, width), jnp.bfloat16),
        pltpu.SemaphoreType.DMA((len(energies) + len(sums) + len(pieces) + 2 * chunks,)),
    ]
    return call(kernel, [signs, flags], [eps_virt], [*sums, *last, *arrays], [out], pl.ANY, scratch)[0]


def after(block, *others):
    return lax.optimization_barrier((block, *others))[0]


def on_device(factors, eps_occ, eps_virt, pair_mask):
    rows, occ_rows, virt = factors.shape
    width = occ_rows * virt
    lines = width // LANES
    groups = lax.axis_size("occ")
    shares = lax.axis_size("aux")
    size = rows // CHUNKS
    cut = size * lines
    last = CHUNKS - 1
    group = lax.axis_index("occ")
    place = group % PLANE
    odd_x = place % 2 == 1
    odd_y = place // 2 == 1

    own = factors.reshape(rows * lines, LANES)
    energies = jnp.zeros((SUBLANES * LANES,), jnp.float32).at[:occ_rows].set(eps_occ)
    energies = energies.reshape(SUBLANES, LANES)

    def part(whole, at):
        return whole[at * cut : (at + 1) * cut]

    def within(block, moves):
        planes = range(0, groups, PLANE)
        return lax.ppermute(block, "occ", [(g + a, g + b) for g in planes for a, b in moves])

    def up(block):
        return lax.ppermute(block, "occ", [(g, g + PLANE) for g in range(groups - PLANE)])

    def totals(partial):
        if shares == 2:
            return [partial, lax.ppermute(partial, "aux", [(0, 1), (1, 0)])]
        return [lax.psum(partial, "aux")]

    def sign(offset):
        flag = lax.dynamic_index_in_dim(pair_mask[0], offset - 1, 0, keepdims=False)
        return jnp.where((group >= offset) & (flag > 0), -1.0, 0.0).astype(jnp.float32)

    sign_own = jnp.float32(-1.0)
    sign_z = sign(jnp.int32(PLANE))
    sign_x = sign(jnp.where(odd_x, 1, PLANE - 1))
    sign_y = sign(jnp.int32(PLANE // 2))
    sign_d = sign(jnp.where(odd_x, PLANE - 1, 1))

    first_sent = jnp.concatenate([part(own, 0), energies])
    down_x, down_y = 1 - place % 2, 1 - place // 2
    flags = jnp.stack(
        [down_x, down_y, jnp.where(odd_y, 0, 1 + place), jnp.where(odd_y, place - 1, 0)]
    ).astype(jnp.int32)

    def add(partials, slots, signs, carriers, before=None):
        return contract(partials, slots, jnp.stack(signs), carriers, flags, eps_virt[None, :], size, before)

    from_z = [up(first_sent)]
    up_x = within(first_sent, [(0, 1), (2, 3), (1, 0)])
    up_y = within(first_sent, [(0, 2), (1, 3)])
    high, low, partial_own = prepare(own, rows, width)
    turned = (high, low)
    sums_own = totals(partial_own)
    swap_x, swap_y = [], []
    passed = [partial_own, up_x, up_y]
    for at in range(CHUNKS):
        came, mine, *_ = lax.optimization_barrier((from_z[at], own, *passed))
        if at < last:
            from_z.append(up(part(mine, at + 1)))
            up_part = part(mine, at + 1)
            if at == 0:
                up_part = jnp.concatenate([up_part, energies])
            swap_x.append(within(jnp.where(odd_x, came, up_part), [(0, 1), (1, 0), (2, 3), (3, 2)]))
            swap_y.append(within(jnp.where(odd_y, came, up_part), [(0, 2), (2, 0), (1, 3), (3, 1)]))
        else:
            came_x = jnp.concatenate([came, energies])
            swap_x.append(within(jnp.where(odd_x, came_x, swap_y[0]), [(0, 1), (1, 0), (2, 3), (3, 2)]))
            swap_y.append(within(came, [(2, 0), (3, 1)]))
        passed = [swap_x[at], swap_y[at]]

    middle = (place == 1) | (place == 2)
    cross = within(jnp.where(place == 2, swap_x[0], swap_y[0]), [(2, 0), (3, 2)])
    cycle = within(jnp.where(middle, swap_x[1], swap_y[1]), [(0, 1), (1, 3), (3, 2), (2, 0)])
    swap_d = within(swap_y[2], [(0, 1), (1, 0), (2, 3), (3, 2)])
    last_d = within(swap_y[3], [(0, 1), (1, 0)])
    up_d = within(after(up_x, cross), [(0, 2), (1, 3)])

    def pieces_of(first, swaps, choice, base):
        arrays = [first, *swaps]
        return [Piece(((arrays[at], base), (arrays[at + 1], base)), choice) for at in range(CHUNKS)]

    def whole(array, base):
        return Piece(((array, base),))

    slot_own = [whole(own, at * cut) for at in range(CHUNKS)]
    slot_z = [whole(block, 0) for block in from_z]
    slot_x = pieces_of(up_x, swap_x, 0, 0)
    slot_y = pieces_of(up_y, swap_y, 1, 0)
    slot_d = [
        Piece(((up_d, 0), (cross, 0), (swap_x[last], 0)), 2),
        Piece(((cycle, 0), (cross, 0), (swap_x[last], 0)), 3),
        Piece(((cycle, 0), (swap_d, 0)), 1),
        Piece(((swap_d, 0), (last_d, 0)), 1),
    ]
    eps_x = pieces_of(up_x, swap_x, 0, cut)[0]
    eps_y = pieces_of(up_y, swap_y, 1, cut)[0]
    eps_d = Piece(((up_d, cut), (cross, cut), (swap_x[last], cut)), 2)

    partial_z, *early = integrate(
        turned, [slot_z, slot_x[:last], slot_y[:last]], [0, 0, 0], flags, size, width
    )
    gradient = add(
        [sums_own, totals(partial_z)], [slot_own, slot_z], [sign_own, sign_z],
        [whole(first_sent, cut), whole(first_sent, cut), whole(from_z[0], cut)],
    )
    partial_x, partial_y = integrate(
        turned, [slot_x[last:], slot_y[last:]], [last, last], flags, size, width, early
    )
    gradient = add(
        [totals(partial_x), totals(partial_y)], [slot_x, slot_y], [sign_x, sign_y],
        [whole(first_sent, cut), eps_x, eps_y], gradient,
    )
    turned = after(turned, gradient)
    partial_d = integrate(turned, [slot_d[:last]], [0], flags, size, width)
    (partial_d,) = integrate(turned, [slot_d[last:]], [last], flags, size, width, partial_d)
    gradient = add([totals(partial_d)], [slot_d], [sign_d], [whole(first_sent, cut), eps_d], gradient)
    return gradient.reshape(rows, occ_rows, virt)


def solution(mesh):
    if mesh.shape["occ"] % PLANE:
        raise ValueError("incomplete plane")
    in_specs = (P("aux", "occ", None), P("occ"), P(), P("occ", None))
    out_specs = P("aux", "occ", None)
    return jax.shard_map(
        on_device, mesh=mesh, in_specs=in_specs, out_specs=out_specs, check_vma=False
    )
```

```python
import dataclasses
import functools

import jax
import jax.numpy as jnp
from jax import lax
from jax.experimental import pallas as pl
from jax.experimental.pallas import tpu as pltpu
from jax.sharding import PartitionSpec as P

LANES = 128
SUBLANES = 8
PLANE = 4
CHUNKS = 4
VMEM_LIMIT = 60 * 1024 * 1024


def split(value):
    high = value.astype(jnp.bfloat16)
    low = (value - high.astype(jnp.float32)).astype(jnp.bfloat16)
    return high, low


def deep_left(value):
    high, low = split(value)
    return jnp.concatenate([high, low, high], axis=1)


def deep_right(value):
    high, low = split(value)
    return jnp.concatenate([high, high, low], axis=0)


def dot(left, right):
    numbers = (((1,), (0,)), ((), ()))
    return lax.dot_general(left, right, numbers, preferred_element_type=jnp.float32)


def rows_of(ref, start, count, width):
    lines = width // LANES
    columns = [ref[pl.ds(start * lines + at, count, stride=lines), :] for at in range(lines)]
    return jnp.concatenate(columns, axis=1)


def distinct(arrays):
    return list({id(array): array for array in arrays}.values())


class Copies:
    def __init__(self, semaphores):
        self.semaphores = semaphores
        self.used = 0

    def start(self, source, target):
        copy = pltpu.make_async_copy(source, target, self.semaphores.at[self.used])
        self.used += 1
        copy.start()
        return copy

    def start_piece(self, piece, ref_of, choices, count, target):
        made = []
        for array, base in piece.places:
            source = ref_of[id(array)].at[pl.ds(base, count)]
            made.append(pltpu.make_async_copy(source, target, self.semaphores.at[self.used]))
        self.used += 1
        if len(made) == 1:
            made[0].start()
        else:
            for at, copy in enumerate(made):
                pl.when(choices[piece.choice] == at)(copy.start)
        return made[0]


@dataclasses.dataclass(frozen=True)
class Piece:
    places: tuple
    choice: int = 0


def call(kernel, smem, vmem, anywhere, outputs, out_space, scratch):
    spaces = [pltpu.SMEM] * len(smem) + [pltpu.VMEM] * len(vmem) + [pl.ANY] * len(anywhere)
    return pl.pallas_call(
        kernel,
        out_shape=outputs,
        in_specs=[pl.BlockSpec(memory_space=space) for space in spaces],
        out_specs=[pl.BlockSpec(memory_space=out_space)] * len(outputs),
        scratch_shapes=scratch,
        compiler_params=pltpu.CompilerParams(vmem_limit_bytes=VMEM_LIMIT),
        cost_estimate=pl.CostEstimate(flops=0, bytes_accessed=0, transcendentals=0),
    )(*smem, *vmem, *anywhere)


def prepare(own, rows, width):
    size = rows // CHUNKS
    cut = size * width // LANES

    def kernel(own_ref, high_ref, low_ref, integrals_ref, block_ref, semaphores):
        copies = Copies(semaphores)
        coming = [copies.start(own_ref.at[pl.ds(at * cut, cut)], block_ref.at[at]) for at in range(CHUNKS)]
        for at in range(CHUNKS):
            coming[at].wait()
            block = rows_of(block_ref.at[at], 0, size, width)
            high, low = split(block.T)
            high_ref[at] = high
            low_ref[at] = low
            value = dot(jnp.concatenate([high, low, high], axis=1), deep_right(block))
            integrals_ref[...] = integrals_ref[...] + value if at else value

    half = jax.ShapeDtypeStruct((CHUNKS, width, size), jnp.bfloat16)
    square = jax.ShapeDtypeStruct((width, width), jnp.float32)
    scratch = [pltpu.VMEM((CHUNKS, cut, LANES), jnp.float32), pltpu.SemaphoreType.DMA((CHUNKS,))]
    return call(kernel, [], [], [own], [half, half, square], pltpu.VMEM, scratch)


def arrays_of(pieces):
    return distinct([array for piece in pieces for array, _ in piece.places])


def integrate(turned, slots, first, flags, size, width, before=()):
    cut = size * width // LANES
    count = len(slots)
    pieces = [piece for slot in slots for piece in slot]
    arrays = arrays_of(pieces)
    numbers = [list(range(start, start + len(slot))) for slot, start in zip(slots, first)]
    needed = sorted({number for some in numbers for number in some})
    before = list(before)

    def kernel(flag_ref, *refs):
        given = iter(refs)
        high_ref, low_ref = next(given), next(given)
        before_refs = [next(given) for _ in before]
        ref_of = {id(array): next(given) for array in arrays}
        outs = [next(given) for _ in range(count)]
        turned_ref, block_ref, before_ref, semaphores = given
        copies = Copies(semaphores)
        coming, turning = [], {}

        def turn(number):
            if number not in turning:
                at = needed.index(number)
                turning[number] = [
                    copies.start(high_ref.at[number], turned_ref.at[at, 0]),
                    copies.start(low_ref.at[number], turned_ref.at[at, 1]),
                ]

        at = 0
        for slot in range(count):
            for number, piece in zip(numbers[slot], slots[slot]):
                turn(number)
                coming.append(copies.start_piece(piece, ref_of, flag_ref, cut, block_ref.at[at]))
                at += 1
        adding = [copies.start(ref, before_ref.at[slot]) for slot, ref in enumerate(before_refs)]
        at = 0
        for slot in range(count):
            for place, number in enumerate(numbers[slot]):
                for copy in turning.pop(number, []):
                    copy.wait()
                coming[at].wait()
                there = needed.index(number)
                high, low = turned_ref[there, 0], turned_ref[there, 1]
                left = jnp.concatenate([high, low, high], axis=1)
                value = dot(left, deep_right(rows_of(block_ref.at[at], 0, size, width)))
                outs[slot][...] = outs[slot][...] + value if place else value
                at += 1
            if before:
                adding[slot].wait()
                outs[slot][...] += before_ref[slot]

    out = [jax.ShapeDtypeStruct((width, width), jnp.float32)] * count
    scratch = [
        pltpu.VMEM((len(needed), 2, width, size), jnp.bfloat16),
        pltpu.VMEM((len(pieces), cut, LANES), jnp.float32),
        pltpu.VMEM((max(len(before), 1), width, width), jnp.float32),
        pltpu.SemaphoreType.DMA((2 * len(needed) + len(pieces) + len(before),)),
    ]
    return call(kernel, [flags], [], [*turned, *before, *arrays], out, pltpu.VMEM, scratch)


def contract(partials, slots, signs, energies, flags, eps_virt, size, before=None):
    count = len(slots)
    chunks = len(slots[0])
    virt = eps_virt.shape[1]
    width = partials[0][0].shape[0]
    occ_rows = width // virt
    lines = width // LANES
    cut = size * lines
    sums = [array for slot in partials for array in slot]
    pieces = [piece for slot in slots for piece in slot]
    arrays = arrays_of([*pieces, *energies])
    last = [before] if before is not None else []

    def kernel(*refs):
        given = iter(refs)
        sign_ref, flag_ref, virt_ref = next(given), next(given), next(given)
        sum_refs = [next(given) for _ in sums]
        before_refs = [next(given) for _ in last]
        ref_of = {id(array): next(given) for array in arrays}
        out_ref, energy_ref, sum_ref, block_ref, result_ref, right_ref, semaphores = given
        copies = Copies(semaphores)
        arriving = [
            copies.start_piece(piece, ref_of, flag_ref, SUBLANES, energy_ref.at[at])
            for at, piece in enumerate(energies)
        ]
        arriving += [copies.start(ref, sum_ref.at[at]) for at, ref in enumerate(sum_refs)]
        coming = [
            [
                copies.start_piece(slots[slot][at], ref_of, flag_ref, cut, block_ref.at[slot, at])
                for slot in range(count)
            ]
            for at in range(chunks)
        ]
        adding = [
            [copies.start(ref.at[pl.ds(at * cut, cut)], result_ref.at[at]) for ref in before_refs]
            for at in range(chunks)
        ]
        for copy in arriving:
            copy.wait()

        def line(at):
            virtual = virt_ref[...]
            energy = energy_ref[at]
            return jnp.concatenate([virtual - energy[:1, i : i + 1] for i in range(occ_rows)], axis=1)

        row = jnp.broadcast_to(line(0), (SUBLANES, width)).T[:, :1]
        at = 0
        for slot in range(count):
            total = sum_ref[at]
            for extra in range(1, len(partials[slot])):
                total = total + sum_ref[at + extra]
            at += len(partials[slot])
            amplitude = (sign_ref[slot] * total) / (row + line(slot + 1))
            right_ref[pl.ds(slot * 3 * width, 3 * width), :] = deep_right(amplitude.T)
        leaving = []
        for at in range(chunks):
            for copy in coming[at] + adding[at]:
                copy.wait()
            left = [deep_left(rows_of(block_ref.at[slot, at], 0, size, width)) for slot in range(count)]
            value = dot(jnp.concatenate(left, axis=1), right_ref[...])
            for column in range(lines):
                lanes = value[:, column * LANES : (column + 1) * LANES]
                where = pl.ds(column, size, stride=lines)
                if last:
                    lanes = lanes + result_ref[at, where, :]
                result_ref[at, where, :] = lanes
            leaving.append(copies.start(result_ref.at[at], out_ref.at[pl.ds(at * cut, cut)]))
        for copy in leaving:
            copy.wait()

    rows = chunks * size
    out = jax.ShapeDtypeStruct((rows * lines, LANES), jnp.float32)
    scratch = [
        pltpu.VMEM((len(energies), SUBLANES, LANES), jnp.float32),
        pltpu.VMEM((len(sums), width, width), jnp.float32),
        pltpu.VMEM((count, chunks, cut, LANES), jnp.float32),
        pltpu.VMEM((chunks, cut, LANES), jnp.float32),
        pltpu.VMEM((count * 3 * width, width), jnp.bfloat16),
        pltpu.SemaphoreType.DMA((len(energies) + len(sums) + len(pieces) + 2 * chunks,)),
    ]
    return call(kernel, [signs, flags], [eps_virt], [*sums, *last, *arrays], [out], pl.ANY, scratch)[0]


def after(block, *others):
    return lax.optimization_barrier((block, *others))[0]


def on_device(factors, eps_occ, eps_virt, pair_mask):
    rows, occ_rows, virt = factors.shape
    width = occ_rows * virt
    lines = width // LANES
    groups = lax.axis_size("occ")
    shares = lax.axis_size("aux")
    size = rows // CHUNKS
    cut = size * lines
    last = CHUNKS - 1
    group = lax.axis_index("occ")
    place = group % PLANE
    odd_x = place % 2 == 1
    odd_y = place // 2 == 1

    own = factors.reshape(rows * lines, LANES)
    energies = jnp.zeros((SUBLANES * LANES,), jnp.float32).at[:occ_rows].set(eps_occ)
    energies = energies.reshape(SUBLANES, LANES)

    def part(whole, at):
        return whole[at * cut : (at + 1) * cut]

    def within(block, moves):
        planes = range(0, groups, PLANE)
        return lax.ppermute(block, "occ", [(g + a, g + b) for g in planes for a, b in moves])

    def up(block):
        return lax.ppermute(block, "occ", [(g, g + PLANE) for g in range(groups - PLANE)])

    def totals(partial):
        if shares == 2:
            return [partial, lax.ppermute(partial, "aux", [(0, 1), (1, 0)])]
        return [lax.psum(partial, "aux")]

    def sign(offset):
        flag = lax.dynamic_index_in_dim(pair_mask[0], offset - 1, 0, keepdims=False)
        return jnp.where((group >= offset) & (flag > 0), -1.0, 0.0).astype(jnp.float32)

    sign_own = jnp.float32(-1.0)
    sign_z = sign(jnp.int32(PLANE))
    sign_x = sign(jnp.where(odd_x, 1, PLANE - 1))
    sign_y = sign(jnp.int32(PLANE // 2))
    sign_d = sign(jnp.where(odd_x, PLANE - 1, 1))

    first_sent = jnp.concatenate([part(own, 0), energies])
    down_x, down_y = 1 - place % 2, 1 - place // 2
    flags = jnp.stack(
        [down_x, down_y, jnp.where(odd_y, 0, 1 + place), jnp.where(odd_y, place - 1, 0)]
    ).astype(jnp.int32)

    def add(partials, slots, signs, carriers, before=None):
        return contract(partials, slots, jnp.stack(signs), carriers, flags, eps_virt[None, :], size, before)

    from_z = [up(first_sent)]
    up_x = within(first_sent, [(0, 1), (2, 3), (1, 0)])
    up_y = within(first_sent, [(0, 2), (1, 3)])
    high, low, partial_own = prepare(own, rows, width)
    turned = (high, low)
    sums_own = totals(partial_own)
    swap_x, swap_y = [], []
    passed = [partial_own, up_x, up_y]
    for at in range(CHUNKS):
        came, mine, *_ = lax.optimization_barrier((from_z[at], own, *passed))
        if at < last:
            from_z.append(up(part(mine, at + 1)))
            up_part = part(mine, at + 1)
            if at == 0:
                up_part = jnp.concatenate([up_part, energies])
            swap_x.append(within(jnp.where(odd_x, came, up_part), [(0, 1), (1, 0), (2, 3), (3, 2)]))
            swap_y.append(within(jnp.where(odd_y, came, up_part), [(0, 2), (2, 0), (1, 3), (3, 1)]))
        else:
            came_x = jnp.concatenate([came, energies])
            swap_x.append(within(jnp.where(odd_x, came_x, swap_y[0]), [(0, 1), (1, 0), (2, 3), (3, 2)]))
            swap_y.append(within(jnp.where(odd_y, came_x, up_x), [(0, 2), (2, 0), (1, 3), (3, 1)]))
        passed = [swap_x[at], swap_y[at]]

    middle = (place == 1) | (place == 2)
    cross = within(jnp.where(place == 2, swap_x[0], swap_y[0]), [(2, 0), (3, 2)])
    cycle = within(jnp.where(middle, swap_x[1], swap_y[1]), [(0, 1), (1, 3), (3, 2), (2, 0)])
    swap_d = within(swap_y[2], [(0, 1), (1, 0), (2, 3), (3, 2)])
    last_d = within(swap_y[3], [(0, 1), (1, 0)])

    def pieces_of(first, swaps, choice, base):
        arrays = [first, *swaps]
        return [Piece(((arrays[at], base), (arrays[at + 1], base)), choice) for at in range(CHUNKS)]

    def whole(array, base):
        return Piece(((array, base),))

    slot_own = [whole(own, at * cut) for at in range(CHUNKS)]
    slot_z = [whole(block, 0) for block in from_z]
    slot_x = pieces_of(up_x, swap_x, 0, 0)
    slot_y = pieces_of(up_y, swap_y, 1, 0)
    slot_d = [
        Piece(((swap_y[last], 0), (cross, 0), (swap_x[last], 0)), 2),
        Piece(((cycle, 0), (cross, 0), (swap_x[last], 0)), 3),
        Piece(((cycle, 0), (swap_d, 0)), 1),
        Piece(((swap_d, 0), (last_d, 0)), 1),
    ]
    eps_x = pieces_of(up_x, swap_x, 0, cut)[0]
    eps_y = pieces_of(up_y, swap_y, 1, cut)[0]
    eps_d = Piece(((swap_y[last], cut), (cross, cut), (swap_x[last], cut)), 2)

    partial_z, *early = integrate(
        turned, [slot_z, slot_x[:last], slot_y[:last]], [0, 0, 0], flags, size, width
    )
    gradient = add(
        [after(sums_own, cross), totals(partial_z)], [slot_own, slot_z], [sign_own, sign_z],
        [whole(first_sent, cut), whole(first_sent, cut), whole(from_z[0], cut)],
    )
    partial_x, partial_y = integrate(
        turned, [slot_x[last:], slot_y[last:]], [last, last], flags, size, width, early
    )
    gradient = add(
        [after(totals(partial_x), cycle), totals(partial_y)], [slot_x, slot_y], [sign_x, sign_y],
        [whole(first_sent, cut), eps_x, eps_y], gradient,
    )
    turned = after(turned, gradient)
    half = CHUNKS // 2
    partial_d = integrate(turned, [slot_d[:half]], [0], flags, size, width)
    (partial_d,) = integrate(turned, [slot_d[half:]], [half], flags, size, width, partial_d)
    gradient = add([totals(partial_d)], [slot_d], [sign_d], [whole(first_sent, cut), eps_d], gradient)
    return gradient.reshape(rows, occ_rows, virt)


def solution(mesh):
    if mesh.shape["occ"] % PLANE:
        raise ValueError("incomplete plane")
    in_specs = (P("aux", "occ", None), P("occ"), P(), P("occ", None))
    out_specs = P("aux", "occ", None)
    return jax.shard_map(
        on_device, mesh=mesh, in_specs=in_specs, out_specs=out_specs, check_vma=False
    )
```

```python
import dataclasses
import functools

import jax
import jax.numpy as jnp
from jax import lax
from jax.experimental import pallas as pl
from jax.experimental.pallas import tpu as pltpu
from jax.sharding import PartitionSpec as P

LANES = 128
SUBLANES = 8
PLANE = 4
CHUNKS = 4
VMEM_LIMIT = 60 * 1024 * 1024


def split(value):
    high = value.astype(jnp.bfloat16)
    low = (value - high.astype(jnp.float32)).astype(jnp.bfloat16)
    return high, low


def deep_left(value):
    high, low = split(value)
    return jnp.concatenate([high, low, high], axis=1)


def deep_right(value):
    high, low = split(value)
    return jnp.concatenate([high, high, low], axis=0)


def dot(left, right):
    numbers = (((1,), (0,)), ((), ()))
    return lax.dot_general(left, right, numbers, preferred_element_type=jnp.float32)


def rows_of(ref, start, count, width):
    lines = width // LANES
    columns = [ref[pl.ds(start * lines + at, count, stride=lines), :] for at in range(lines)]
    return jnp.concatenate(columns, axis=1)


def distinct(arrays):
    return list({id(array): array for array in arrays}.values())


class Copies:
    def __init__(self, semaphores):
        self.semaphores = semaphores
        self.used = 0

    def start(self, source, target):
        copy = pltpu.make_async_copy(source, target, self.semaphores.at[self.used])
        self.used += 1
        copy.start()
        return copy

    def start_piece(self, piece, ref_of, choices, count, target):
        made = []
        for array, base in piece.places:
            source = ref_of[id(array)].at[pl.ds(base, count)]
            made.append(pltpu.make_async_copy(source, target, self.semaphores.at[self.used]))
        self.used += 1
        if len(made) == 1:
            made[0].start()
        else:
            for at, copy in enumerate(made):
                pl.when(choices[piece.choice] == at)(copy.start)
        return made[0]


@dataclasses.dataclass(frozen=True)
class Piece:
    places: tuple
    choice: int = 0


def call(kernel, smem, vmem, anywhere, outputs, out_space, scratch):
    spaces = [pltpu.SMEM] * len(smem) + [pltpu.VMEM] * len(vmem) + [pl.ANY] * len(anywhere)
    return pl.pallas_call(
        kernel,
        out_shape=outputs,
        in_specs=[pl.BlockSpec(memory_space=space) for space in spaces],
        out_specs=[pl.BlockSpec(memory_space=out_space)] * len(outputs),
        scratch_shapes=scratch,
        compiler_params=pltpu.CompilerParams(vmem_limit_bytes=VMEM_LIMIT),
        cost_estimate=pl.CostEstimate(flops=0, bytes_accessed=0, transcendentals=0),
    )(*smem, *vmem, *anywhere)


def prepare(own, rows, width):
    size = rows // CHUNKS
    cut = size * width // LANES

    def kernel(own_ref, high_ref, low_ref, integrals_ref, block_ref, semaphores):
        copies = Copies(semaphores)
        coming = [copies.start(own_ref.at[pl.ds(at * cut, cut)], block_ref.at[at]) for at in range(CHUNKS)]
        for at in range(CHUNKS):
            coming[at].wait()
            block = rows_of(block_ref.at[at], 0, size, width)
            high, low = split(block.T)
            high_ref[at] = high
            low_ref[at] = low
            value = dot(jnp.concatenate([high, low, high], axis=1), deep_right(block))
            integrals_ref[...] = integrals_ref[...] + value if at else value

    half = jax.ShapeDtypeStruct((CHUNKS, width, size), jnp.bfloat16)
    square = jax.ShapeDtypeStruct((width, width), jnp.float32)
    scratch = [pltpu.VMEM((CHUNKS, cut, LANES), jnp.float32), pltpu.SemaphoreType.DMA((CHUNKS,))]
    return call(kernel, [], [], [own], [half, half, square], pltpu.VMEM, scratch)


def arrays_of(pieces):
    return distinct([array for piece in pieces for array, _ in piece.places])


def integrate(turned, slots, first, flags, size, width, before=()):
    cut = size * width // LANES
    count = len(slots)
    pieces = [piece for slot in slots for piece in slot]
    arrays = arrays_of(pieces)
    numbers = [list(range(start, start + len(slot))) for slot, start in zip(slots, first)]
    needed = sorted({number for some in numbers for number in some})
    before = list(before)

    def kernel(flag_ref, *refs):
        given = iter(refs)
        high_ref, low_ref = next(given), next(given)
        before_refs = [next(given) for _ in before]
        ref_of = {id(array): next(given) for array in arrays}
        outs = [next(given) for _ in range(count)]
        turned_ref, block_ref, before_ref, semaphores = given
        copies = Copies(semaphores)
        coming, turning = [], {}

        def turn(number):
            if number not in turning:
                at = needed.index(number)
                turning[number] = [
                    copies.start(high_ref.at[number], turned_ref.at[at, 0]),
                    copies.start(low_ref.at[number], turned_ref.at[at, 1]),
                ]

        at = 0
        for slot in range(count):
            for number, piece in zip(numbers[slot], slots[slot]):
                turn(number)
                coming.append(copies.start_piece(piece, ref_of, flag_ref, cut, block_ref.at[at]))
                at += 1
        adding = [copies.start(ref, before_ref.at[slot]) for slot, ref in enumerate(before_refs)]
        at = 0
        for slot in range(count):
            for place, number in enumerate(numbers[slot]):
                for copy in turning.pop(number, []):
                    copy.wait()
                coming[at].wait()
                there = needed.index(number)
                high, low = turned_ref[there, 0], turned_ref[there, 1]
                left = jnp.concatenate([high, low, high], axis=1)
                value = dot(left, deep_right(rows_of(block_ref.at[at], 0, size, width)))
                outs[slot][...] = outs[slot][...] + value if place else value
                at += 1
            if before:
                adding[slot].wait()
                outs[slot][...] += before_ref[slot]

    out = [jax.ShapeDtypeStruct((width, width), jnp.float32)] * count
    scratch = [
        pltpu.VMEM((len(needed), 2, width, size), jnp.bfloat16),
        pltpu.VMEM((len(pieces), cut, LANES), jnp.float32),
        pltpu.VMEM((max(len(before), 1), width, width), jnp.float32),
        pltpu.SemaphoreType.DMA((2 * len(needed) + len(pieces) + len(before),)),
    ]
    return call(kernel, [flags], [], [*turned, *before, *arrays], out, pltpu.VMEM, scratch)


def contract(partials, slots, signs, first_sign, energies, flags, eps_virt, size, before=None):
    count = len(slots)
    chunks = len(slots[0])
    virt = eps_virt.shape[1]
    width = partials[0][0].shape[0]
    occ_rows = width // virt
    lines = width // LANES
    cut = size * lines
    sums = [array for slot in partials for array in slot]
    pieces = [piece for slot in slots for piece in slot]
    arrays = arrays_of([*pieces, *energies])
    last = [before] if before is not None else []

    def kernel(*refs):
        given = iter(refs)
        sign_ref, flag_ref, virt_ref = next(given), next(given), next(given)
        sum_refs = [next(given) for _ in sums]
        before_refs = [next(given) for _ in last]
        ref_of = {id(array): next(given) for array in arrays}
        out_ref, energy_ref, sum_ref, block_ref, result_ref, right_ref, semaphores = given
        copies = Copies(semaphores)
        arriving = [
            copies.start_piece(piece, ref_of, flag_ref, SUBLANES, energy_ref.at[at])
            for at, piece in enumerate(energies)
        ]
        arriving += [copies.start(ref, sum_ref.at[at]) for at, ref in enumerate(sum_refs)]
        coming = [
            [
                copies.start_piece(slots[slot][at], ref_of, flag_ref, cut, block_ref.at[slot, at])
                for slot in range(count)
            ]
            for at in range(chunks)
        ]
        adding = [
            [copies.start(ref.at[pl.ds(at * cut, cut)], result_ref.at[at]) for ref in before_refs]
            for at in range(chunks)
        ]
        for copy in arriving:
            copy.wait()

        def line(at):
            virtual = virt_ref[...]
            energy = energy_ref[at]
            return jnp.concatenate([virtual - energy[:1, i : i + 1] for i in range(occ_rows)], axis=1)

        row = jnp.broadcast_to(line(0), (SUBLANES, width)).T[:, :1]
        at = 0
        for slot in range(count):
            total = sum_ref[at]
            for extra in range(1, len(partials[slot])):
                total = total + sum_ref[at + extra]
            at += len(partials[slot])
            amplitude = (sign_ref[first_sign + slot] * total) / (row + line(slot + 1))
            right_ref[pl.ds(slot * 3 * width, 3 * width), :] = deep_right(amplitude.T)
        leaving = []
        for at in range(chunks):
            for copy in coming[at] + adding[at]:
                copy.wait()
            left = [deep_left(rows_of(block_ref.at[slot, at], 0, size, width)) for slot in range(count)]
            value = dot(jnp.concatenate(left, axis=1), right_ref[...])
            for column in range(lines):
                lanes = value[:, column * LANES : (column + 1) * LANES]
                where = pl.ds(column, size, stride=lines)
                if last:
                    lanes = lanes + result_ref[at, where, :]
                result_ref[at, where, :] = lanes
            leaving.append(copies.start(result_ref.at[at], out_ref.at[pl.ds(at * cut, cut)]))
        for copy in leaving:
            copy.wait()

    rows = chunks * size
    out = jax.ShapeDtypeStruct((rows * lines, LANES), jnp.float32)
    scratch = [
        pltpu.VMEM((len(energies), SUBLANES, LANES), jnp.float32),
        pltpu.VMEM((len(sums), width, width), jnp.float32),
        pltpu.VMEM((count, chunks, cut, LANES), jnp.float32),
        pltpu.VMEM((chunks, cut, LANES), jnp.float32),
        pltpu.VMEM((count * 3 * width, width), jnp.bfloat16),
        pltpu.SemaphoreType.DMA((len(energies) + len(sums) + len(pieces) + 2 * chunks,)),
    ]
    return call(kernel, [signs, flags], [eps_virt], [*sums, *last, *arrays], [out], pl.ANY, scratch)[0]


def after(block, *others):
    return lax.optimization_barrier((block, *others))[0]


def on_device(factors, eps_occ, eps_virt, pair_mask):
    rows, occ_rows, virt = factors.shape
    width = occ_rows * virt
    lines = width // LANES
    groups = lax.axis_size("occ")
    shares = lax.axis_size("aux")
    size = rows // CHUNKS
    cut = size * lines
    last = CHUNKS - 1
    group = lax.axis_index("occ")
    place = group % PLANE
    odd_x = place % 2 == 1
    odd_y = place // 2 == 1

    own = factors.reshape(rows * lines, LANES)
    energies = jnp.zeros((SUBLANES * LANES,), jnp.float32).at[:occ_rows].set(eps_occ)
    energies = energies.reshape(SUBLANES, LANES)

    def part(whole, at):
        return whole[at * cut : (at + 1) * cut]

    def within(block, moves):
        planes = range(0, groups, PLANE)
        return lax.ppermute(block, "occ", [(g + a, g + b) for g in planes for a, b in moves])

    def up(block):
        return lax.ppermute(block, "occ", [(g, g + PLANE) for g in range(groups - PLANE)])

    def totals(partial):
        if shares == 2:
            return [partial, lax.ppermute(partial, "aux", [(0, 1), (1, 0)])]
        return [lax.psum(partial, "aux")]

    def sign(offset):
        flag = jnp.sum(jnp.where(jnp.arange(1, PLANE + 1) == offset, pair_mask[0], 0))
        return jnp.where((group >= offset) & (flag > 0), -1.0, 0.0).astype(jnp.float32)

    near, far = jnp.where(odd_x, 1, PLANE - 1), jnp.where(odd_x, PLANE - 1, 1)
    signs = jnp.stack([jnp.float32(-1.0), sign(PLANE), sign(near), sign(PLANE // 2), sign(far)])

    first_sent = jnp.concatenate([part(own, 0), energies])
    down_x, down_y = 1 - place % 2, 1 - place // 2
    flags = jnp.stack(
        [down_x, down_y, jnp.where(odd_y, 0, 1 + place), jnp.where(odd_y, place - 1, 0)]
    ).astype(jnp.int32)

    def add(first_sign, partials, slots, carriers, before=None):
        return contract(partials, slots, signs, first_sign, carriers, flags, eps_virt[None, :], size, before)

    from_z = [up(first_sent)]
    first_sent, signs, flags = lax.optimization_barrier((first_sent, signs, flags))
    up_x = within(first_sent, [(0, 1), (2, 3), (1, 0)])
    up_y = within(first_sent, [(0, 2), (1, 3)])
    high, low, partial_own = prepare(own, rows, width)
    turned = (high, low)
    sums_own = totals(partial_own)
    swap_x, swap_y = [], []
    passed = [partial_own]
    for at in range(CHUNKS):
        came, mine, *_ = lax.optimization_barrier((from_z[at], own, *passed))
        if at < last:
            from_z.append(up(part(mine, at + 1)))
            up_part = part(mine, at + 1)
            if at == 0:
                up_part = jnp.concatenate([up_part, energies])
            send_x, send_y = jnp.where(odd_x, came, up_part), jnp.where(odd_y, came, up_part)
            if at == 0:
                send_x, send_y = after(send_x, up_x), after(send_y, up_y)
            swap_x.append(within(send_x, [(0, 1), (1, 0), (2, 3), (3, 2)]))
            swap_y.append(within(send_y, [(0, 2), (2, 0), (1, 3), (3, 1)]))
        else:
            came_x = jnp.concatenate([came, energies])
            swap_x.append(within(jnp.where(odd_x, came_x, swap_y[0]), [(0, 1), (1, 0), (2, 3), (3, 2)]))
            swap_y.append(within(jnp.where(odd_y, came_x, up_x), [(0, 2), (2, 0), (1, 3), (3, 1)]))
        passed = [swap_x[at], swap_y[at]]

    middle = (place == 1) | (place == 2)
    cross = within(jnp.where(place == 2, swap_x[0], swap_y[0]), [(2, 0), (3, 2)])
    cycle = within(jnp.where(middle, swap_x[1], swap_y[1]), [(0, 1), (1, 3), (3, 2), (2, 0)])
    swap_d = within(swap_y[2], [(0, 1), (1, 0), (2, 3), (3, 2)])
    last_d = within(swap_y[3], [(0, 1), (1, 0)])

    def pieces_of(first, swaps, choice, base):
        arrays = [first, *swaps]
        return [Piece(((arrays[at], base), (arrays[at + 1], base)), choice) for at in range(CHUNKS)]

    def whole(array, base):
        return Piece(((array, base),))

    slot_own = [whole(own, at * cut) for at in range(CHUNKS)]
    slot_z = [whole(block, 0) for block in from_z]
    slot_x = pieces_of(up_x, swap_x, 0, 0)
    slot_y = pieces_of(up_y, swap_y, 1, 0)
    slot_d = [
        Piece(((swap_y[last], 0), (cross, 0), (swap_x[last], 0)), 2),
        Piece(((cycle, 0), (cross, 0), (swap_x[last], 0)), 3),
        Piece(((cycle, 0), (swap_d, 0)), 1),
        Piece(((swap_d, 0), (last_d, 0)), 1),
    ]
    eps_x = pieces_of(up_x, swap_x, 0, cut)[0]
    eps_y = pieces_of(up_y, swap_y, 1, cut)[0]
    eps_d = Piece(((swap_y[last], cut), (cross, cut), (swap_x[last], cut)), 2)

    partial_z, *early = integrate(
        turned, [slot_z, slot_x[:last], slot_y[:last]], [0, 0, 0], flags, size, width
    )
    own_eps = whole(first_sent, cut)
    gradient = add(
        0, [after(sums_own, cross), totals(partial_z)], [slot_own, slot_z], [own_eps, own_eps, whole(from_z[0], cut)]
    )
    partial_x, partial_y = integrate(
        turned, [slot_x[last:], slot_y[last:]], [last, last], flags, size, width, early
    )
    gradient = add(
        2, [totals(partial_x), totals(partial_y)], [slot_x, slot_y], [own_eps, eps_x, eps_y], gradient
    )
    turned = after(turned, gradient)
    half = CHUNKS // 2
    partial_d = integrate(turned, [slot_d[:half]], [0], flags, size, width)
    (partial_d,) = integrate(turned, [slot_d[half:]], [half], flags, size, width, partial_d)
    gradient = add(4, [totals(partial_d)], [slot_d], [own_eps, eps_d], gradient)
    return gradient.reshape(rows, occ_rows, virt)


def solution(mesh):
    if mesh.shape["occ"] % PLANE:
        raise ValueError("incomplete plane")
    in_specs = (P("aux", "occ", None), P("occ"), P(), P("occ", None))
    out_specs = P("aux", "occ", None)
    return jax.shard_map(
        on_device, mesh=mesh, in_specs=in_specs, out_specs=out_specs, check_vma=False
    )
```

```python
import dataclasses
import functools

import jax
import jax.numpy as jnp
from jax import lax
from jax.experimental import pallas as pl
from jax.experimental.pallas import tpu as pltpu
from jax.sharding import PartitionSpec as P

LANES = 128
SUBLANES = 8
PLANE = 4
CHUNKS = 4
VMEM_LIMIT = 60 * 1024 * 1024


def split(value):
    high = value.astype(jnp.bfloat16)
    low = (value - high.astype(jnp.float32)).astype(jnp.bfloat16)
    return high, low


def deep_left(value):
    high, low = split(value)
    return jnp.concatenate([high, low, high], axis=1)


def deep_right(value):
    high, low = split(value)
    return jnp.concatenate([high, high, low], axis=0)


def dot(left, right):
    numbers = (((1,), (0,)), ((), ()))
    return lax.dot_general(left, right, numbers, preferred_element_type=jnp.float32)


def rows_of(ref, start, count, width):
    lines = width // LANES
    columns = [ref[pl.ds(start * lines + at, count, stride=lines), :] for at in range(lines)]
    return jnp.concatenate(columns, axis=1)


def distinct(arrays):
    return list({id(array): array for array in arrays}.values())


class Copies:
    def __init__(self, semaphores):
        self.semaphores = semaphores
        self.used = 0

    def start(self, source, target):
        copy = pltpu.make_async_copy(source, target, self.semaphores.at[self.used])
        self.used += 1
        copy.start()
        return copy

    def start_piece(self, piece, ref_of, choices, count, target):
        made = []
        for array, base in piece.places:
            source = ref_of[id(array)].at[pl.ds(base, count)]
            made.append(pltpu.make_async_copy(source, target, self.semaphores.at[self.used]))
        self.used += 1
        if len(made) == 1:
            made[0].start()
        else:
            for at, copy in enumerate(made):
                pl.when(choices[piece.choice] == at)(copy.start)
        return made[0]


@dataclasses.dataclass(frozen=True)
class Piece:
    places: tuple
    choice: int = 0


def call(kernel, smem, vmem, anywhere, outputs, out_space, scratch):
    spaces = [pltpu.SMEM] * len(smem) + [pltpu.VMEM] * len(vmem) + [pl.ANY] * len(anywhere)
    return pl.pallas_call(
        kernel,
        out_shape=outputs,
        in_specs=[pl.BlockSpec(memory_space=space) for space in spaces],
        out_specs=[pl.BlockSpec(memory_space=out_space)] * len(outputs),
        scratch_shapes=scratch,
        compiler_params=pltpu.CompilerParams(vmem_limit_bytes=VMEM_LIMIT),
        cost_estimate=pl.CostEstimate(flops=0, bytes_accessed=0, transcendentals=0),
    )(*smem, *vmem, *anywhere)


def prepare(own, rows, width):
    size = rows // CHUNKS
    cut = size * width // LANES

    def kernel(own_ref, high_ref, low_ref, integrals_ref, block_ref, semaphores):
        copies = Copies(semaphores)
        coming = [copies.start(own_ref.at[pl.ds(at * cut, cut)], block_ref.at[at]) for at in range(CHUNKS)]
        for at in range(CHUNKS):
            coming[at].wait()
            block = rows_of(block_ref.at[at], 0, size, width)
            high, low = split(block.T)
            high_ref[at] = high
            low_ref[at] = low
            value = dot(jnp.concatenate([high, low, high], axis=1), deep_right(block))
            integrals_ref[...] = integrals_ref[...] + value if at else value

    half = jax.ShapeDtypeStruct((CHUNKS, width, size), jnp.bfloat16)
    square = jax.ShapeDtypeStruct((width, width), jnp.float32)
    scratch = [pltpu.VMEM((CHUNKS, cut, LANES), jnp.float32), pltpu.SemaphoreType.DMA((CHUNKS,))]
    return call(kernel, [], [], [own], [half, half, square], pltpu.VMEM, scratch)


def arrays_of(pieces):
    return distinct([array for piece in pieces for array, _ in piece.places])


def integrate(turned, slots, first, flags, size, width, before=()):
    cut = size * width // LANES
    count = len(slots)
    pieces = [piece for slot in slots for piece in slot]
    arrays = arrays_of(pieces)
    numbers = [list(range(start, start + len(slot))) for slot, start in zip(slots, first)]
    needed = sorted({number for some in numbers for number in some})
    before = list(before)

    def kernel(flag_ref, *refs):
        given = iter(refs)
        high_ref, low_ref = next(given), next(given)
        before_refs = [next(given) for _ in before]
        ref_of = {id(array): next(given) for array in arrays}
        outs = [next(given) for _ in range(count)]
        turned_ref, block_ref, before_ref, semaphores = given
        copies = Copies(semaphores)
        coming, turning = [], {}

        def turn(number):
            if number not in turning:
                at = needed.index(number)
                turning[number] = [
                    copies.start(high_ref.at[number], turned_ref.at[at, 0]),
                    copies.start(low_ref.at[number], turned_ref.at[at, 1]),
                ]

        at = 0
        for slot in range(count):
            for number, piece in zip(numbers[slot], slots[slot]):
                turn(number)
                coming.append(copies.start_piece(piece, ref_of, flag_ref, cut, block_ref.at[at]))
                at += 1
        adding = [copies.start(ref, before_ref.at[slot]) for slot, ref in enumerate(before_refs)]
        at = 0
        for slot in range(count):
            for place, number in enumerate(numbers[slot]):
                for copy in turning.pop(number, []):
                    copy.wait()
                coming[at].wait()
                there = needed.index(number)
                high, low = turned_ref[there, 0], turned_ref[there, 1]
                left = jnp.concatenate([high, low, high], axis=1)
                value = dot(left, deep_right(rows_of(block_ref.at[at], 0, size, width)))
                outs[slot][...] = outs[slot][...] + value if place else value
                at += 1
            if before:
                adding[slot].wait()
                outs[slot][...] += before_ref[slot]

    out = [jax.ShapeDtypeStruct((width, width), jnp.float32)] * count
    scratch = [
        pltpu.VMEM((len(needed), 2, width, size), jnp.bfloat16),
        pltpu.VMEM((len(pieces), cut, LANES), jnp.float32),
        pltpu.VMEM((max(len(before), 1), width, width), jnp.float32),
        pltpu.SemaphoreType.DMA((2 * len(needed) + len(pieces) + len(before),)),
    ]
    return call(kernel, [flags], [], [*turned, *before, *arrays], out, pltpu.VMEM, scratch)


def contract(partials, slots, signs, first_sign, energies, flags, eps_virt, size, before=None):
    count = len(slots)
    chunks = len(slots[0])
    virt = eps_virt.shape[1]
    width = partials[0][0].shape[0]
    occ_rows = width // virt
    lines = width // LANES
    cut = size * lines
    sums = [array for slot in partials for array in slot]
    pieces = [piece for slot in slots for piece in slot]
    arrays = arrays_of([*pieces, *energies])
    last = [before] if before is not None else []

    def kernel(*refs):
        given = iter(refs)
        sign_ref, flag_ref, virt_ref = next(given), next(given), next(given)
        sum_refs = [next(given) for _ in sums]
        before_refs = [next(given) for _ in last]
        ref_of = {id(array): next(given) for array in arrays}
        out_ref, energy_ref, sum_ref, block_ref, result_ref, right_ref, semaphores = given
        copies = Copies(semaphores)
        arriving = [
            copies.start_piece(piece, ref_of, flag_ref, SUBLANES, energy_ref.at[at])
            for at, piece in enumerate(energies)
        ]
        arriving += [copies.start(ref, sum_ref.at[at]) for at, ref in enumerate(sum_refs)]
        coming = [
            [
                copies.start_piece(slots[slot][at], ref_of, flag_ref, cut, block_ref.at[slot, at])
                for slot in range(count)
            ]
            for at in range(chunks)
        ]
        adding = [
            [copies.start(ref.at[pl.ds(at * cut, cut)], result_ref.at[at]) for ref in before_refs]
            for at in range(chunks)
        ]
        for copy in arriving:
            copy.wait()

        def line(at):
            virtual = virt_ref[...]
            energy = energy_ref[at]
            return jnp.concatenate([virtual - energy[:1, i : i + 1] for i in range(occ_rows)], axis=1)

        row = jnp.broadcast_to(line(0), (SUBLANES, width)).T[:, :1]
        at = 0
        for slot in range(count):
            total = sum_ref[at]
            for extra in range(1, len(partials[slot])):
                total = total + sum_ref[at + extra]
            at += len(partials[slot])
            amplitude = (sign_ref[first_sign + slot] * total) / (row + line(slot + 1))
            right_ref[pl.ds(slot * 3 * width, 3 * width), :] = deep_right(amplitude.T)
        leaving = []
        for at in range(chunks):
            for copy in coming[at] + adding[at]:
                copy.wait()
            left = [deep_left(rows_of(block_ref.at[slot, at], 0, size, width)) for slot in range(count)]
            value = dot(jnp.concatenate(left, axis=1), right_ref[...])
            for column in range(lines):
                lanes = value[:, column * LANES : (column + 1) * LANES]
                where = pl.ds(column, size, stride=lines)
                if last:
                    lanes = lanes + result_ref[at, where, :]
                result_ref[at, where, :] = lanes
            leaving.append(copies.start(result_ref.at[at], out_ref.at[pl.ds(at * cut, cut)]))
        for copy in leaving:
            copy.wait()

    rows = chunks * size
    out = jax.ShapeDtypeStruct((rows * lines, LANES), jnp.float32)
    scratch = [
        pltpu.VMEM((len(energies), SUBLANES, LANES), jnp.float32),
        pltpu.VMEM((len(sums), width, width), jnp.float32),
        pltpu.VMEM((count, chunks, cut, LANES), jnp.float32),
        pltpu.VMEM((chunks, cut, LANES), jnp.float32),
        pltpu.VMEM((count * 3 * width, width), jnp.bfloat16),
        pltpu.SemaphoreType.DMA((len(energies) + len(sums) + len(pieces) + 2 * chunks,)),
    ]
    return call(kernel, [signs, flags], [eps_virt], [*sums, *last, *arrays], [out], pl.ANY, scratch)[0]


def after(block, *others):
    return lax.optimization_barrier((block, *others))[0]


def on_device(factors, eps_occ, eps_virt, pair_mask):
    rows, occ_rows, virt = factors.shape
    width = occ_rows * virt
    lines = width // LANES
    groups = lax.axis_size("occ")
    shares = lax.axis_size("aux")
    size = rows // CHUNKS
    cut = size * lines
    last = CHUNKS - 1
    group = lax.axis_index("occ")
    place = group % PLANE
    odd_x = place % 2 == 1
    odd_y = place // 2 == 1

    own = factors.reshape(rows * lines, LANES)
    energies = jnp.zeros((SUBLANES * LANES,), jnp.float32).at[:occ_rows].set(eps_occ)
    energies = energies.reshape(SUBLANES, LANES)

    def part(whole, at):
        return whole[at * cut : (at + 1) * cut]

    def within(block, moves):
        planes = range(0, groups, PLANE)
        return lax.ppermute(block, "occ", [(g + a, g + b) for g in planes for a, b in moves])

    def up(block):
        return lax.ppermute(block, "occ", [(g, g + PLANE) for g in range(groups - PLANE)])

    def totals(partial):
        if shares == 2:
            return [partial, lax.ppermute(partial, "aux", [(0, 1), (1, 0)])]
        return [lax.psum(partial, "aux")]

    def sign(offset):
        flag = jnp.sum(jnp.where(jnp.arange(1, PLANE + 1) == offset, pair_mask[0], 0))
        return jnp.where((group >= offset) & (flag > 0), -1.0, 0.0).astype(jnp.float32)

    near, far = jnp.where(odd_x, 1, PLANE - 1), jnp.where(odd_x, PLANE - 1, 1)
    signs = jnp.stack([jnp.float32(-1.0), sign(PLANE), sign(near), sign(PLANE // 2), sign(far)])

    first_sent = jnp.concatenate([part(own, 0), energies])
    down_x, down_y = 1 - place % 2, 1 - place // 2
    flags = jnp.stack(
        [down_x, down_y, jnp.where(odd_y, 0, 1 + place), jnp.where(odd_y, place - 1, 0)]
    ).astype(jnp.int32)

    def add(first_sign, partials, slots, carriers, before=None):
        return contract(partials, slots, signs, first_sign, carriers, flags, eps_virt[None, :], size, before)

    from_z = [up(first_sent)]
    up_x = within(first_sent, [(0, 1), (2, 3), (1, 0)])
    up_y = within(first_sent, [(0, 2), (1, 3)])
    high, low, partial_own = prepare(own, rows, width)
    turned = (high, low)
    sums_own = totals(partial_own)
    swap_x, swap_y = [], []
    passed = [partial_own]
    for at in range(CHUNKS):
        came, mine, *_ = lax.optimization_barrier((from_z[at], own, *passed))
        if at < last:
            from_z.append(up(part(mine, at + 1)))
            up_part = part(mine, at + 1)
            if at == 0:
                up_part = jnp.concatenate([up_part, energies])
            send_x, send_y = jnp.where(odd_x, came, up_part), jnp.where(odd_y, came, up_part)
            if at == 0:
                send_x, send_y = after(send_x, up_x), after(send_y, up_y)
            swap_x.append(within(send_x, [(0, 1), (1, 0), (2, 3), (3, 2)]))
            swap_y.append(within(send_y, [(0, 2), (2, 0), (1, 3), (3, 1)]))
        else:
            cycle = within(after(turning, came), [(0, 1), (1, 3), (3, 2), (2, 0)])
            came_x = jnp.concatenate([came, energies])
            swap_x.append(within(jnp.where(odd_x, came_x, swap_y[0]), [(0, 1), (1, 0), (2, 3), (3, 2)]))
            swap_y.append(within(jnp.where(odd_y, came_x, up_x), [(0, 2), (2, 0), (1, 3), (3, 1)]))
        passed = [swap_x[at], swap_y[at]]
        if at == 0:
            passed += [signs, flags]
        if at == 1:
            middle = (place == 1) | (place == 2)
            turning = jnp.where(middle, swap_x[1], swap_y[1])
        if at == 2:
            passed.append(turning)

    cross = within(jnp.where(place == 2, swap_x[0], swap_y[0]), [(2, 0), (3, 2)])
    swap_d = within(swap_y[2], [(0, 1), (1, 0), (2, 3), (3, 2)])
    last_d = within(swap_y[3], [(0, 1), (1, 0)])

    def pieces_of(first, swaps, choice, base):
        arrays = [first, *swaps]
        return [Piece(((arrays[at], base), (arrays[at + 1], base)), choice) for at in range(CHUNKS)]

    def whole(array, base):
        return Piece(((array, base),))

    slot_own = [whole(own, at * cut) for at in range(CHUNKS)]
    slot_z = [whole(block, 0) for block in from_z]
    slot_x = pieces_of(up_x, swap_x, 0, 0)
    slot_y = pieces_of(up_y, swap_y, 1, 0)
    slot_d = [
        Piece(((swap_y[last], 0), (cross, 0), (swap_x[last], 0)), 2),
        Piece(((cycle, 0), (cross, 0), (swap_x[last], 0)), 3),
        Piece(((cycle, 0), (swap_d, 0)), 1),
        Piece(((swap_d, 0), (last_d, 0)), 1),
    ]
    eps_x = pieces_of(up_x, swap_x, 0, cut)[0]
    eps_y = pieces_of(up_y, swap_y, 1, cut)[0]
    eps_d = Piece(((swap_y[last], cut), (cross, cut), (swap_x[last], cut)), 2)

    partial_z, *early = integrate(
        turned, [slot_z, slot_x[:last], slot_y[:last]], [0, 0, 0], flags, size, width
    )
    own_eps = whole(first_sent, cut)
    gradient = add(
        0, [after(sums_own, cycle), totals(partial_z)], [slot_own, slot_z], [own_eps, own_eps, whole(from_z[0], cut)]
    )
    partial_x, partial_y = integrate(
        turned, [slot_x[last:], slot_y[last:]], [last, last], flags, size, width, early
    )
    gradient = add(
        2, [totals(partial_x), totals(partial_y)], [slot_x, slot_y], [own_eps, eps_x, eps_y], gradient
    )
    turned = after(turned, gradient)
    half = CHUNKS // 2
    partial_d = integrate(turned, [slot_d[:half]], [0], flags, size, width)
    (partial_d,) = integrate(turned, [slot_d[half:]], [half], flags, size, width, partial_d)
    gradient = add(4, [totals(partial_d)], [slot_d], [own_eps, eps_d], gradient)
    return gradient.reshape(rows, occ_rows, virt)


def solution(mesh):
    if mesh.shape["occ"] % PLANE:
        raise ValueError("incomplete plane")
    in_specs = (P("aux", "occ", None), P("occ"), P(), P("occ", None))
    out_specs = P("aux", "occ", None)
    return jax.shard_map(
        on_device, mesh=mesh, in_specs=in_specs, out_specs=out_specs, check_vma=False
    )
```

```python
import dataclasses
import functools

import jax
import jax.numpy as jnp
from jax import lax
from jax.experimental import pallas as pl
from jax.experimental.pallas import tpu as pltpu
from jax.sharding import PartitionSpec as P

LANES = 128
SUBLANES = 8
PLANE = 4
CHUNKS = 4
VMEM_LIMIT = 60 * 1024 * 1024


def split(value):
    high = value.astype(jnp.bfloat16)
    low = (value - high.astype(jnp.float32)).astype(jnp.bfloat16)
    return high, low


def deep_left(value):
    high, low = split(value)
    return jnp.concatenate([high, low, high], axis=1)


def deep_right(value, axis=0):
    high, low = split(value)
    return jnp.concatenate([high, high, low], axis=axis)


def dot(left, right, axis=0):
    numbers = (((1,), (axis,)), ((), ()))
    return lax.dot_general(left, right, numbers, preferred_element_type=jnp.float32)


def rows_of(ref, start, count, width):
    lines = width // LANES
    columns = [ref[pl.ds(start * lines + at, count, stride=lines), :] for at in range(lines)]
    return jnp.concatenate(columns, axis=1)


def distinct(arrays):
    return list({id(array): array for array in arrays}.values())


class Copies:
    def __init__(self, semaphores):
        self.semaphores = semaphores
        self.used = 0

    def start(self, source, target):
        copy = pltpu.make_async_copy(source, target, self.semaphores.at[self.used])
        self.used += 1
        copy.start()
        return copy

    def start_piece(self, piece, ref_of, choices, count, target):
        made = []
        for array, base in piece.places:
            source = ref_of[id(array)].at[pl.ds(base, count)]
            made.append(pltpu.make_async_copy(source, target, self.semaphores.at[self.used]))
        self.used += 1
        if len(made) == 1:
            made[0].start()
        else:
            for at, copy in enumerate(made):
                pl.when(choices[piece.choice] == at)(copy.start)
        return made[0]


@dataclasses.dataclass(frozen=True)
class Piece:
    places: tuple
    choice: int = 0


def call(kernel, smem, vmem, anywhere, outputs, out_space, scratch):
    spaces = [pltpu.SMEM] * len(smem) + [pltpu.VMEM] * len(vmem) + [pl.ANY] * len(anywhere)
    return pl.pallas_call(
        kernel,
        out_shape=outputs,
        in_specs=[pl.BlockSpec(memory_space=space) for space in spaces],
        out_specs=[pl.BlockSpec(memory_space=out_space)] * len(outputs),
        scratch_shapes=scratch,
        compiler_params=pltpu.CompilerParams(vmem_limit_bytes=VMEM_LIMIT),
        cost_estimate=pl.CostEstimate(flops=0, bytes_accessed=0, transcendentals=0),
    )(*smem, *vmem, *anywhere)


def prepare(own, energies, rows, width):
    size = rows // CHUNKS
    cut = size * width // LANES

    def kernel(energy_ref, own_ref, high_out, low_out, integrals_out, *refs):
        sent_refs = refs[: CHUNKS - 1]
        block_ref, turned_ref, integrals_ref, semaphores = refs[CHUNKS - 1 :]
        copies = Copies(semaphores)
        coming = [copies.start(own_ref.at[pl.ds(at * cut, cut)], block_ref.at[at]) for at in range(CHUNKS)]
        leaving = [copies.start(energy_ref, ref.at[pl.ds(cut, SUBLANES)]) for ref in sent_refs]
        for at in range(CHUNKS):
            coming[at].wait()
            if at:
                leaving.append(copies.start(block_ref.at[at], sent_refs[at - 1].at[pl.ds(0, cut)]))
            block = rows_of(block_ref.at[at], 0, size, width)
            high, low = split(block.T)
            turned_ref[0, at] = high
            turned_ref[1, at] = low
            leaving.append(copies.start(turned_ref.at[0, at], high_out.at[at]))
            leaving.append(copies.start(turned_ref.at[1, at], low_out.at[at]))
            value = dot(jnp.concatenate([high, low, high], axis=1), deep_right(block))
            integrals_ref[...] = integrals_ref[...] + value if at else value
        leaving.append(copies.start(integrals_ref, integrals_out))
        for copy in leaving:
            copy.wait()

    turned = jax.ShapeDtypeStruct((CHUNKS, width, size), jnp.bfloat16)
    square = jax.ShapeDtypeStruct((width, width), jnp.float32)
    sent = jax.ShapeDtypeStruct((cut + SUBLANES, LANES), jnp.float32)
    scratch = [
        pltpu.VMEM((CHUNKS, cut, LANES), jnp.float32),
        pltpu.VMEM((2, CHUNKS, width, size), jnp.bfloat16),
        pltpu.VMEM((width, width), jnp.float32),
        pltpu.SemaphoreType.DMA((5 * CHUNKS,)),
    ]
    outs = [turned, turned, square] + [sent] * (CHUNKS - 1)
    return call(kernel, [], [energies], [own], outs, pl.ANY, scratch)


def arrays_of(pieces):
    return distinct([array for piece in pieces for array, _ in piece.places])


def integrate(turned, slots, first, flags, size, width, before=()):
    cut = size * width // LANES
    count = len(slots)
    pieces = [piece for slot in slots for piece in slot]
    arrays = arrays_of(pieces)
    numbers = [list(range(start, start + len(slot))) for slot, start in zip(slots, first)]
    needed = sorted({number for some in numbers for number in some})
    before = list(before)

    def kernel(flag_ref, *refs):
        given = iter(refs)
        high_ref, low_ref = next(given), next(given)
        before_refs = [next(given) for _ in before]
        ref_of = {id(array): next(given) for array in arrays}
        outs = [next(given) for _ in range(count)]
        turned_ref, block_ref, before_ref, semaphores = given
        copies = Copies(semaphores)
        coming, turning = [], {}

        def turn(number):
            if number not in turning:
                at = needed.index(number)
                turning[number] = [
                    copies.start(high_ref.at[number], turned_ref.at[at, 0]),
                    copies.start(low_ref.at[number], turned_ref.at[at, 1]),
                ]

        at = 0
        for slot in range(count):
            for number, piece in zip(numbers[slot], slots[slot]):
                turn(number)
                coming.append(copies.start_piece(piece, ref_of, flag_ref, cut, block_ref.at[at]))
                at += 1
        adding = [copies.start(ref, before_ref.at[slot]) for slot, ref in enumerate(before_refs)]
        at = 0
        for slot in range(count):
            for place, number in enumerate(numbers[slot]):
                for copy in turning.pop(number, []):
                    copy.wait()
                coming[at].wait()
                there = needed.index(number)
                high, low = turned_ref[there, 0], turned_ref[there, 1]
                left = jnp.concatenate([high, low, high], axis=1)
                value = dot(left, deep_right(rows_of(block_ref.at[at], 0, size, width)))
                outs[slot][...] = outs[slot][...] + value if place else value
                at += 1
            if before:
                adding[slot].wait()
                outs[slot][...] += before_ref[slot]

    out = [jax.ShapeDtypeStruct((width, width), jnp.float32)] * count
    scratch = [
        pltpu.VMEM((len(needed), 2, width, size), jnp.bfloat16),
        pltpu.VMEM((len(pieces), cut, LANES), jnp.float32),
        pltpu.VMEM((max(len(before), 1), width, width), jnp.float32),
        pltpu.SemaphoreType.DMA((2 * len(needed) + len(pieces) + len(before),)),
    ]
    return call(kernel, [flags], [], [*turned, *before, *arrays], out, pltpu.VMEM, scratch)


def contract(partials, slots, signs, first_sign, energies, flags, eps_virt, size, before=None):
    count = len(slots)
    chunks = len(slots[0])
    virt = eps_virt.shape[1]
    width = partials[0][0].shape[0]
    occ_rows = width // virt
    lines = width // LANES
    cut = size * lines
    sums = [array for slot in partials for array in slot]
    pieces = [piece for slot in slots for piece in slot]
    arrays = arrays_of([*pieces, *energies])
    last = [before] if before is not None else []

    def kernel(*refs):
        given = iter(refs)
        sign_ref, flag_ref, virt_ref = next(given), next(given), next(given)
        sum_refs = [next(given) for _ in sums]
        before_refs = [next(given) for _ in last]
        ref_of = {id(array): next(given) for array in arrays}
        out_ref, energy_ref, sum_ref, block_ref, result_ref, right_ref, semaphores = given
        copies = Copies(semaphores)
        arriving = [
            copies.start_piece(piece, ref_of, flag_ref, SUBLANES, energy_ref.at[at])
            for at, piece in enumerate(energies)
        ]
        arriving += [copies.start(ref, sum_ref.at[at]) for at, ref in enumerate(sum_refs)]
        coming = [
            [
                copies.start_piece(slots[slot][at], ref_of, flag_ref, cut, block_ref.at[slot, at])
                for slot in range(count)
            ]
            for at in range(chunks)
        ]
        adding = [
            [copies.start(ref.at[pl.ds(at * cut, cut)], result_ref.at[at]) for ref in before_refs]
            for at in range(chunks)
        ]
        for copy in arriving:
            copy.wait()

        def line(at):
            virtual = virt_ref[...]
            energy = energy_ref[at]
            return jnp.concatenate([virtual - energy[:1, i : i + 1] for i in range(occ_rows)], axis=1)

        row = jnp.broadcast_to(line(0), (SUBLANES, width)).T[:, :1]
        at = 0
        for slot in range(count):
            total = sum_ref[at]
            for extra in range(1, len(partials[slot])):
                total = total + sum_ref[at + extra]
            at += len(partials[slot])
            amplitude = (sign_ref[first_sign + slot] * total) / (row + line(slot + 1))
            right_ref[:, pl.ds(slot * 3 * width, 3 * width)] = deep_right(amplitude, 1)
        leaving = []
        for at in range(chunks):
            for copy in coming[at] + adding[at]:
                copy.wait()
            left = [deep_left(rows_of(block_ref.at[slot, at], 0, size, width)) for slot in range(count)]
            value = dot(jnp.concatenate(left, axis=1), right_ref[...], 1)
            for column in range(lines):
                lanes = value[:, column * LANES : (column + 1) * LANES]
                where = pl.ds(column, size, stride=lines)
                if last:
                    lanes = lanes + result_ref[at, where, :]
                result_ref[at, where, :] = lanes
            leaving.append(copies.start(result_ref.at[at], out_ref.at[pl.ds(at * cut, cut)]))
        for copy in leaving:
            copy.wait()

    rows = chunks * size
    out = jax.ShapeDtypeStruct((rows * lines, LANES), jnp.float32)
    scratch = [
        pltpu.VMEM((len(energies), SUBLANES, LANES), jnp.float32),
        pltpu.VMEM((len(sums), width, width), jnp.float32),
        pltpu.VMEM((count, chunks, cut, LANES), jnp.float32),
        pltpu.VMEM((chunks, cut, LANES), jnp.float32),
        pltpu.VMEM((width, count * 3 * width), jnp.bfloat16),
        pltpu.SemaphoreType.DMA((len(energies) + len(sums) + len(pieces) + 2 * chunks,)),
    ]
    return call(kernel, [signs, flags], [eps_virt], [*sums, *last, *arrays], [out], pl.ANY, scratch)[0]


def after(block, *others):
    return lax.optimization_barrier((block, *others))[0]


def on_device(factors, eps_occ, eps_virt, pair_mask):
    rows, occ_rows, virt = factors.shape
    width = occ_rows * virt
    lines = width // LANES
    groups = lax.axis_size("occ")
    shares = lax.axis_size("aux")
    size = rows // CHUNKS
    cut = size * lines
    last = CHUNKS - 1
    group = lax.axis_index("occ")
    place = group % PLANE
    odd_x = place % 2 == 1
    odd_y = place // 2 == 1

    own = factors.reshape(rows * lines, LANES)
    energies = jnp.zeros((SUBLANES * LANES,), jnp.float32).at[:occ_rows].set(eps_occ)
    energies = energies.reshape(SUBLANES, LANES)

    def part(whole, at):
        return whole[at * cut : (at + 1) * cut]

    def within(block, moves):
        planes = range(0, groups, PLANE)
        return lax.ppermute(block, "occ", [(g + a, g + b) for g in planes for a, b in moves])

    def up(block):
        return lax.ppermute(block, "occ", [(g, g + PLANE) for g in range(groups - PLANE)])

    def totals(partial):
        if shares == 2:
            return [partial, lax.ppermute(partial, "aux", [(0, 1), (1, 0)])]
        return [lax.psum(partial, "aux")]

    def sign(offset):
        flag = jnp.sum(jnp.where(jnp.arange(1, PLANE + 1) == offset, pair_mask[0], 0))
        return jnp.where((group >= offset) & (flag > 0), -1.0, 0.0).astype(jnp.float32)

    near, far = jnp.where(odd_x, 1, PLANE - 1), jnp.where(odd_x, PLANE - 1, 1)
    signs = jnp.stack([jnp.float32(-1.0), sign(PLANE), sign(near), sign(PLANE // 2), sign(far)])

    first_sent = jnp.concatenate([part(own, 0), energies])
    down_x, down_y = 1 - place % 2, 1 - place // 2
    flags = jnp.stack(
        [down_x, down_y, jnp.where(odd_y, 0, 1 + place), jnp.where(odd_y, place - 1, 0)]
    ).astype(jnp.int32)

    def add(first_sign, partials, slots, carriers, before=None):
        return contract(partials, slots, signs, first_sign, carriers, flags, eps_virt[None, :], size, before)

    from_own = [first_sent]
    from_z = [up(first_sent)]
    up_x = within(first_sent, [(0, 1), (2, 3), (1, 0)])
    up_y = within(first_sent, [(0, 2), (1, 3)])
    high, low, partial_own, *own_sent = prepare(own, energies, rows, width)
    from_own += own_sent
    turned = (high, low)
    sums_own = totals(partial_own)
    swap_x, swap_y = [], []
    passed = [partial_own]
    for at in range(CHUNKS):
        came, *_ = lax.optimization_barrier((from_z[at], *passed))
        if at < last:
            from_z.append(up(after(from_own[at + 1], came)))
            up_part = after(from_own[at + 1], came)
            send_x, send_y = jnp.where(odd_x, came, up_part), jnp.where(odd_y, came, up_part)
            if at == 0:
                send_x, send_y = after(send_x, up_x), after(send_y, up_y)
            swap_x.append(within(send_x, [(0, 1), (1, 0), (2, 3), (3, 2)]))
            swap_y.append(within(send_y, [(0, 2), (2, 0), (1, 3), (3, 1)]))
        else:
            cycle = within(after(turning, came), [(0, 1), (1, 3), (3, 2), (2, 0)])
            swap_x.append(within(jnp.where(odd_x, came, swap_y[0]), [(0, 1), (1, 0), (2, 3), (3, 2)]))
            swap_y.append(within(jnp.where(odd_y, came, up_x), [(0, 2), (2, 0), (1, 3), (3, 1)]))
        passed = [swap_x[at], swap_y[at]]
        if at == 0:
            passed += [signs, flags]
        if at == 1:
            middle = (place == 1) | (place == 2)
            turning = jnp.where(middle, swap_x[1], swap_y[1])
        if at == 2:
            passed.append(turning)

    cross = within(jnp.where(place == 2, swap_x[0], swap_y[0]), [(2, 0), (3, 2)])
    swap_d = within(swap_y[2], [(0, 1), (1, 0), (2, 3), (3, 2)])
    last_d = within(swap_y[3], [(0, 1), (1, 0)])

    def pieces_of(first, swaps, choice, base):
        arrays = [first, *swaps]
        return [Piece(((arrays[at], base), (arrays[at + 1], base)), choice) for at in range(CHUNKS)]

    def whole(array, base):
        return Piece(((array, base),))

    slot_own = [whole(own, at * cut) for at in range(CHUNKS)]
    slot_z = [whole(block, 0) for block in from_z]
    slot_x = pieces_of(up_x, swap_x, 0, 0)
    slot_y = pieces_of(up_y, swap_y, 1, 0)
    slot_d = [
        Piece(((swap_y[last], 0), (cross, 0), (swap_x[last], 0)), 2),
        Piece(((cycle, 0), (cross, 0), (swap_x[last], 0)), 3),
        Piece(((cycle, 0), (swap_d, 0)), 1),
        Piece(((swap_d, 0), (last_d, 0)), 1),
    ]
    eps_x = pieces_of(up_x, swap_x, 0, cut)[0]
    eps_y = pieces_of(up_y, swap_y, 1, cut)[0]
    eps_d = Piece(((swap_y[last], cut), (cross, cut), (swap_x[last], cut)), 2)

    partial_z, *early = integrate(
        turned, [slot_z, slot_x[:last], slot_y[:last]], [0, 0, 0], flags, size, width
    )
    own_eps = whole(first_sent, cut)
    partial_x, partial_y = integrate(
        turned, [slot_x[last:], slot_y[last:]], [last, last], flags, size, width, early
    )
    gradient = add(
        0,
        [after(sums_own, cycle), totals(partial_z), totals(partial_x), totals(partial_y)],
        [slot_own, slot_z, slot_x, slot_y],
        [own_eps, own_eps, whole(from_z[0], cut), eps_x, eps_y],
    )
    turned = after(turned, gradient)
    half = CHUNKS // 2
    partial_d = integrate(turned, [slot_d[:half]], [0], flags, size, width)
    (partial_d,) = integrate(turned, [slot_d[half:]], [half], flags, size, width, partial_d)
    gradient = add(4, [totals(partial_d)], [slot_d], [own_eps, eps_d], gradient)
    return gradient.reshape(rows, occ_rows, virt)


def solution(mesh):
    if mesh.shape["occ"] % PLANE:
        raise ValueError("incomplete plane")
    in_specs = (P("aux", "occ", None), P("occ"), P(), P("occ", None))
    out_specs = P("aux", "occ", None)
    return jax.shard_map(
        on_device, mesh=mesh, in_specs=in_specs, out_specs=out_specs, check_vma=False
    )
```

```python
import dataclasses
import functools

import jax
import jax.numpy as jnp
from jax import lax
from jax.experimental import pallas as pl
from jax.experimental.pallas import tpu as pltpu
from jax.sharding import PartitionSpec as P

LANES = 128
SUBLANES = 8
PLANE = 4
CHUNKS = 4
VMEM_LIMIT = 60 * 1024 * 1024
LAST_LIMIT = 24 * 1024 * 1024


def split(value):
    high = value.astype(jnp.bfloat16)
    low = (value - high.astype(jnp.float32)).astype(jnp.bfloat16)
    return high, low


def deep_left(value):
    high, low = split(value)
    return jnp.concatenate([high, low, high], axis=1)


def deep_right(value, axis=0):
    high, low = split(value)
    return jnp.concatenate([high, high, low], axis=axis)


def dot(left, right, axis=0):
    numbers = (((1,), (axis,)), ((), ()))
    return lax.dot_general(left, right, numbers, preferred_element_type=jnp.float32)


def rows_of(ref, start, count, width):
    lines = width // LANES
    columns = [ref[pl.ds(start * lines + at, count, stride=lines), :] for at in range(lines)]
    return jnp.concatenate(columns, axis=1)


def distinct(arrays):
    return list({id(array): array for array in arrays}.values())


class Copies:
    def __init__(self, semaphores):
        self.semaphores = semaphores
        self.used = 0

    def start(self, source, target):
        copy = pltpu.make_async_copy(source, target, self.semaphores.at[self.used])
        self.used += 1
        copy.start()
        return copy

    def start_piece(self, piece, ref_of, choices, count, target):
        made = []
        for array, base in piece.places:
            source = ref_of[id(array)].at[pl.ds(base, count)]
            made.append(pltpu.make_async_copy(source, target, self.semaphores.at[self.used]))
        self.used += 1
        if len(made) == 1:
            made[0].start()
        else:
            for at, copy in enumerate(made):
                pl.when(choices[piece.choice] == at)(copy.start)
        return made[0]


@dataclasses.dataclass(frozen=True)
class Piece:
    places: tuple
    choice: int = 0


def call(kernel, smem, vmem, anywhere, outputs, out_space, scratch, limit=VMEM_LIMIT):
    spaces = [pltpu.SMEM] * len(smem) + [pltpu.VMEM] * len(vmem) + [pl.ANY] * len(anywhere)
    return pl.pallas_call(
        kernel,
        out_shape=outputs,
        in_specs=[pl.BlockSpec(memory_space=space) for space in spaces],
        out_specs=[pl.BlockSpec(memory_space=out_space)] * len(outputs),
        scratch_shapes=scratch,
        compiler_params=pltpu.CompilerParams(vmem_limit_bytes=limit),
        cost_estimate=pl.CostEstimate(flops=0, bytes_accessed=0, transcendentals=0),
    )(*smem, *vmem, *anywhere)


def prepare(own, energies, rows, width):
    size = rows // CHUNKS
    cut = size * width // LANES

    def kernel(energy_ref, own_ref, high_out, low_out, integrals_out, *refs):
        sent_refs = refs[: CHUNKS - 1]
        block_ref, turned_ref, integrals_ref, semaphores = refs[CHUNKS - 1 :]
        copies = Copies(semaphores)
        coming = [copies.start(own_ref.at[pl.ds(at * cut, cut)], block_ref.at[at]) for at in range(CHUNKS)]
        leaving = [copies.start(energy_ref, ref.at[pl.ds(cut, SUBLANES)]) for ref in sent_refs]
        for at in range(CHUNKS):
            coming[at].wait()
            if at:
                leaving.append(copies.start(block_ref.at[at], sent_refs[at - 1].at[pl.ds(0, cut)]))
            block = rows_of(block_ref.at[at], 0, size, width)
            high, low = split(block.T)
            turned_ref[0, at] = high
            turned_ref[1, at] = low
            leaving.append(copies.start(turned_ref.at[0, at], high_out.at[at]))
            leaving.append(copies.start(turned_ref.at[1, at], low_out.at[at]))
            value = dot(jnp.concatenate([high, low, high], axis=1), deep_right(block))
            integrals_ref[...] = integrals_ref[...] + value if at else value
        leaving.append(copies.start(integrals_ref, integrals_out))
        for copy in leaving:
            copy.wait()

    turned = jax.ShapeDtypeStruct((CHUNKS, width, size), jnp.bfloat16)
    square = jax.ShapeDtypeStruct((width, width), jnp.float32)
    sent = jax.ShapeDtypeStruct((cut + SUBLANES, LANES), jnp.float32)
    scratch = [
        pltpu.VMEM((CHUNKS, cut, LANES), jnp.float32),
        pltpu.VMEM((2, CHUNKS, width, size), jnp.bfloat16),
        pltpu.VMEM((width, width), jnp.float32),
        pltpu.SemaphoreType.DMA((5 * CHUNKS,)),
    ]
    outs = [turned, turned, square] + [sent] * (CHUNKS - 1)
    return call(kernel, [], [energies], [own], outs, pl.ANY, scratch)


def arrays_of(pieces):
    return distinct([array for piece in pieces for array, _ in piece.places])


def integrate(turned, slots, first, flags, size, width, before=(), limit=VMEM_LIMIT):
    cut = size * width // LANES
    count = len(slots)
    pieces = [piece for slot in slots for piece in slot]
    arrays = arrays_of(pieces)
    numbers = [list(range(start, start + len(slot))) for slot, start in zip(slots, first)]
    needed = sorted({number for some in numbers for number in some})
    before = list(before)

    def kernel(flag_ref, *refs):
        given = iter(refs)
        high_ref, low_ref = next(given), next(given)
        before_refs = [next(given) for _ in before]
        ref_of = {id(array): next(given) for array in arrays}
        outs = [next(given) for _ in range(count)]
        turned_ref, block_ref, before_ref, semaphores = given
        copies = Copies(semaphores)
        coming, turning = [], {}

        def turn(number):
            if number not in turning:
                at = needed.index(number)
                turning[number] = [
                    copies.start(high_ref.at[number], turned_ref.at[at, 0]),
                    copies.start(low_ref.at[number], turned_ref.at[at, 1]),
                ]

        at = 0
        for slot in range(count):
            for number, piece in zip(numbers[slot], slots[slot]):
                turn(number)
                coming.append(copies.start_piece(piece, ref_of, flag_ref, cut, block_ref.at[at]))
                at += 1
        adding = [copies.start(ref, before_ref.at[slot]) for slot, ref in enumerate(before_refs)]
        at = 0
        for slot in range(count):
            for place, number in enumerate(numbers[slot]):
                for copy in turning.pop(number, []):
                    copy.wait()
                coming[at].wait()
                there = needed.index(number)
                high, low = turned_ref[there, 0], turned_ref[there, 1]
                left = jnp.concatenate([high, low, high], axis=1)
                value = dot(left, deep_right(rows_of(block_ref.at[at], 0, size, width)))
                outs[slot][...] = outs[slot][...] + value if place else value
                at += 1
            if before:
                adding[slot].wait()
                outs[slot][...] += before_ref[slot]

    out = [jax.ShapeDtypeStruct((width, width), jnp.float32)] * count
    scratch = [
        pltpu.VMEM((len(needed), 2, width, size), jnp.bfloat16),
        pltpu.VMEM((len(pieces), cut, LANES), jnp.float32),
        pltpu.VMEM((max(len(before), 1), width, width), jnp.float32),
        pltpu.SemaphoreType.DMA((2 * len(needed) + len(pieces) + len(before),)),
    ]
    return call(kernel, [flags], [], [*turned, *before, *arrays], out, pltpu.VMEM, scratch, limit)


def contract(partials, slots, signs, first_sign, energies, flags, eps_virt, size, before=None, limit=VMEM_LIMIT):
    count = len(slots)
    chunks = len(slots[0])
    virt = eps_virt.shape[1]
    width = partials[0][0].shape[0]
    occ_rows = width // virt
    lines = width // LANES
    cut = size * lines
    sums = [array for slot in partials for array in slot]
    pieces = [piece for slot in slots for piece in slot]
    arrays = arrays_of([*pieces, *energies])
    last = [before] if before is not None else []

    def kernel(*refs):
        given = iter(refs)
        sign_ref, flag_ref, virt_ref = next(given), next(given), next(given)
        sum_refs = [next(given) for _ in sums]
        before_refs = [next(given) for _ in last]
        ref_of = {id(array): next(given) for array in arrays}
        out_ref, energy_ref, sum_ref, block_ref, result_ref, right_ref, semaphores = given
        copies = Copies(semaphores)
        arriving = [
            copies.start_piece(piece, ref_of, flag_ref, SUBLANES, energy_ref.at[at])
            for at, piece in enumerate(energies)
        ]
        arriving += [copies.start(ref, sum_ref.at[at]) for at, ref in enumerate(sum_refs)]
        coming = [
            [
                copies.start_piece(slots[slot][at], ref_of, flag_ref, cut, block_ref.at[slot, at])
                for slot in range(count)
            ]
            for at in range(chunks)
        ]
        adding = [
            [copies.start(ref.at[pl.ds(at * cut, cut)], result_ref.at[at]) for ref in before_refs]
            for at in range(chunks)
        ]
        for copy in arriving:
            copy.wait()

        def line(at):
            virtual = virt_ref[...]
            energy = energy_ref[at]
            return jnp.concatenate([virtual - energy[:1, i : i + 1] for i in range(occ_rows)], axis=1)

        row = jnp.broadcast_to(line(0), (SUBLANES, width)).T[:, :1]
        at = 0
        for slot in range(count):
            total = sum_ref[at]
            for extra in range(1, len(partials[slot])):
                total = total + sum_ref[at + extra]
            at += len(partials[slot])
            amplitude = (sign_ref[first_sign + slot] * total) / (row + line(slot + 1))
            right_ref[:, pl.ds(slot * 3 * width, 3 * width)] = deep_right(amplitude, 1)
        leaving = []
        for at in range(chunks):
            for copy in coming[at] + adding[at]:
                copy.wait()
            left = [deep_left(rows_of(block_ref.at[slot, at], 0, size, width)) for slot in range(count)]
            value = dot(jnp.concatenate(left, axis=1), right_ref[...], 1)
            for column in range(lines):
                lanes = value[:, column * LANES : (column + 1) * LANES]
                where = pl.ds(column, size, stride=lines)
                if last:
                    lanes = lanes + result_ref[at, where, :]
                result_ref[at, where, :] = lanes
            leaving.append(copies.start(result_ref.at[at], out_ref.at[pl.ds(at * cut, cut)]))
        for copy in leaving:
            copy.wait()

    rows = chunks * size
    out = jax.ShapeDtypeStruct((rows * lines, LANES), jnp.float32)
    scratch = [
        pltpu.VMEM((len(energies), SUBLANES, LANES), jnp.float32),
        pltpu.VMEM((len(sums), width, width), jnp.float32),
        pltpu.VMEM((count, chunks, cut, LANES), jnp.float32),
        pltpu.VMEM((chunks, cut, LANES), jnp.float32),
        pltpu.VMEM((width, count * 3 * width), jnp.bfloat16),
        pltpu.SemaphoreType.DMA((len(energies) + len(sums) + len(pieces) + 2 * chunks,)),
    ]
    return call(kernel, [signs, flags], [eps_virt], [*sums, *last, *arrays], [out], pl.ANY, scratch, limit)[0]


def after(block, *others):
    return lax.optimization_barrier((block, *others))[0]


def on_device(factors, eps_occ, eps_virt, pair_mask):
    rows, occ_rows, virt = factors.shape
    width = occ_rows * virt
    lines = width // LANES
    groups = lax.axis_size("occ")
    shares = lax.axis_size("aux")
    size = rows // CHUNKS
    cut = size * lines
    last = CHUNKS - 1
    group = lax.axis_index("occ")
    place = group % PLANE
    odd_x = place % 2 == 1
    odd_y = place // 2 == 1

    own = factors.reshape(rows * lines, LANES)
    energies = jnp.zeros((SUBLANES * LANES,), jnp.float32).at[:occ_rows].set(eps_occ)
    energies = energies.reshape(SUBLANES, LANES)

    def part(whole, at):
        return whole[at * cut : (at + 1) * cut]

    def within(block, moves):
        planes = range(0, groups, PLANE)
        return lax.ppermute(block, "occ", [(g + a, g + b) for g in planes for a, b in moves])

    def up(block):
        return lax.ppermute(block, "occ", [(g, g + PLANE) for g in range(groups - PLANE)])

    def totals(partial):
        if shares == 2:
            return [partial, lax.ppermute(partial, "aux", [(0, 1), (1, 0)])]
        return [lax.psum(partial, "aux")]

    first_sent = jnp.concatenate([part(own, 0), energies])
    def choices(sent):
        group_then, mask_row, _ = lax.optimization_barrier((group, pair_mask[0], sent))
        place_then = group_then % PLANE

        def sign(offset):
            flag = jnp.sum(jnp.where(jnp.arange(1, PLANE + 1) == offset, mask_row, 0))
            return jnp.where((group_then >= offset) & (flag > 0), -1.0, 0.0).astype(jnp.float32)

        near = jnp.where(place_then % 2 == 1, 1, PLANE - 1)
        signs = [jnp.float32(-1.0), sign(PLANE), sign(near), sign(PLANE // 2), sign(PLANE - near)]
        up_then = place_then // 2 == 1
        flags = [
            1 - place_then % 2,
            1 - place_then // 2,
            jnp.where(up_then, 0, 1 + place_then),
            jnp.where(up_then, place_then - 1, 0),
        ]
        return jnp.stack(signs), jnp.stack(flags).astype(jnp.int32)

    def add(first_sign, partials, slots, carriers, before=None, limit=VMEM_LIMIT):
        return contract(
            partials, slots, signs, first_sign, carriers, flags, eps_virt[None, :], size, before, limit
        )

    from_own = [first_sent]
    from_z = [up(first_sent)]
    up_x = within(first_sent, [(0, 1), (2, 3), (1, 0)])
    up_y = within(first_sent, [(0, 2), (1, 3)])
    high, low, partial_own, *own_sent = prepare(own, energies, rows, width)
    from_own += own_sent
    turned = (high, low)
    sums_own = totals(partial_own)
    swap_x, swap_y = [], []
    passed = [partial_own]
    for at in range(CHUNKS):
        came = after(from_z[at], *passed)
        if at < last:
            from_z.append(up(after(from_own[at + 1], came)))
            up_part = after(from_own[at + 1], came)
            send_x, send_y = jnp.where(odd_x, came, up_part), jnp.where(odd_y, came, up_part)
            send_x = after(send_x, swap_x[at - 1] if at else up_x)
            send_y = after(send_y, swap_y[at - 1] if at else up_y)
            if at == 0:
                signs, flags = choices((send_x, send_y))
            swap_x.append(within(send_x, [(0, 1), (1, 0), (2, 3), (3, 2)]))
            swap_y.append(within(send_y, [(0, 2), (2, 0), (1, 3), (3, 1)]))
        else:
            cycle = within(after(turning, came, swap_x[last - 1]), [(0, 1), (1, 3), (3, 2), (2, 0)])
            send_x = after(jnp.where(odd_x, came, swap_y[0]), swap_x[last - 1])
            send_y = after(jnp.where(odd_y, came, up_x), swap_y[last - 1])
            swap_x.append(within(send_x, [(0, 1), (1, 0), (2, 3), (3, 2)]))
            swap_y.append(within(send_y, [(0, 2), (2, 0), (1, 3), (3, 1)]))
        passed = []
        if at == 1:
            passed = [signs, flags]
            middle = (place == 1) | (place == 2)
            turning = jnp.where(middle, swap_x[1], swap_y[1])
        if at == 2:
            passed.append(turning)

    cross = within(jnp.where(place == 2, swap_x[0], swap_y[0]), [(2, 0), (3, 2)])
    swap_d = within(swap_y[2], [(0, 1), (1, 0), (2, 3), (3, 2)])
    last_d = within(swap_y[3], [(0, 1), (1, 0)])

    def pieces_of(first, swaps, choice, base):
        arrays = [first, *swaps]
        return [Piece(((arrays[at], base), (arrays[at + 1], base)), choice) for at in range(CHUNKS)]

    def whole(array, base):
        return Piece(((array, base),))

    slot_own = [whole(own, at * cut) for at in range(CHUNKS)]
    slot_z = [whole(block, 0) for block in from_z]
    slot_x = pieces_of(up_x, swap_x, 0, 0)
    slot_y = pieces_of(up_y, swap_y, 1, 0)
    slot_d = [
        Piece(((swap_y[last], 0), (cross, 0), (swap_x[last], 0)), 2),
        Piece(((cycle, 0), (cross, 0), (swap_x[last], 0)), 3),
        Piece(((cycle, 0), (swap_d, 0)), 1),
        Piece(((swap_d, 0), (last_d, 0)), 1),
    ]
    eps_x = pieces_of(up_x, swap_x, 0, cut)[0]
    eps_y = pieces_of(up_y, swap_y, 1, cut)[0]
    eps_d = Piece(((swap_y[last], cut), (cross, cut), (swap_x[last], cut)), 2)

    partial_z, *early = integrate(
        turned, [slot_z, slot_x[:last], slot_y[:last]], [0, 0, 0], flags, size, width
    )
    own_eps = whole(first_sent, cut)
    partial_x, partial_y = integrate(
        turned, [slot_x[last:], slot_y[last:]], [last, last], flags, size, width, early
    )
    gradient = add(
        0,
        [after(sums_own, cycle), totals(partial_z), totals(partial_x), totals(partial_y)],
        [slot_own, slot_z, slot_x, slot_y],
        [own_eps, own_eps, whole(from_z[0], cut), eps_x, eps_y],
    )
    turned = after(turned, gradient)
    half = CHUNKS // 2
    partial_d = integrate(turned, [slot_d[:half]], [0], flags, size, width)
    (partial_d,) = integrate(turned, [slot_d[half:]], [half], flags, size, width, partial_d, LAST_LIMIT)
    gradient = add(4, [totals(partial_d)], [slot_d], [own_eps, eps_d], gradient, LAST_LIMIT)
    return gradient.reshape(rows, occ_rows, virt)


def solution(mesh):
    if mesh.shape["occ"] % PLANE:
        raise ValueError("incomplete plane")
    in_specs = (P("aux", "occ", None), P("occ"), P(), P("occ", None))
    out_specs = P("aux", "occ", None)
    return jax.shard_map(
        on_device, mesh=mesh, in_specs=in_specs, out_specs=out_specs, check_vma=False
    )
```

```python
import dataclasses
import functools

import jax
import jax.numpy as jnp
from jax import lax
from jax.experimental import pallas as pl
from jax.experimental.pallas import tpu as pltpu
from jax.sharding import PartitionSpec as P

LANES = 128
SUBLANES = 8
PLANE = 4
CHUNKS = 4
VMEM_LIMIT = 60 * 1024 * 1024
LAST_LIMIT = 24 * 1024 * 1024
HALVES = 2


def split(value):
    high = value.astype(jnp.bfloat16)
    low = (value - high.astype(jnp.float32)).astype(jnp.bfloat16)
    return high, low


def deep_left(value):
    high, low = split(value)
    return jnp.concatenate([high, low, high], axis=1)


def deep_right(value, axis=0):
    high, low = split(value)
    return jnp.concatenate([high, high, low], axis=axis)


def dot(left, right, axis=0):
    numbers = (((1,), (axis,)), ((), ()))
    return lax.dot_general(left, right, numbers, preferred_element_type=jnp.float32)


def rows_of(ref, start, count, width):
    lines = width // LANES
    columns = [ref[pl.ds(start * lines + at, count, stride=lines), :] for at in range(lines)]
    return jnp.concatenate(columns, axis=1)


def distinct(arrays):
    return list({id(array): array for array in arrays}.values())


class Copies:
    def __init__(self, semaphores):
        self.semaphores = semaphores
        self.used = 0

    def start(self, source, target):
        copy = pltpu.make_async_copy(source, target, self.semaphores.at[self.used])
        self.used += 1
        copy.start()
        return copy

    def start_piece(self, piece, ref_of, choices, count, target):
        made = []
        for array, base in piece.places:
            source = ref_of[id(array)].at[pl.ds(base, count)]
            made.append(pltpu.make_async_copy(source, target, self.semaphores.at[self.used]))
        self.used += 1
        if len(made) == 1:
            made[0].start()
        else:
            for at, copy in enumerate(made):
                pl.when(choices[piece.choice] == at)(copy.start)
        return made[0]


@dataclasses.dataclass(frozen=True)
class Piece:
    places: tuple
    choice: int = 0


def call(kernel, smem, vmem, anywhere, outputs, out_space, scratch, limit=VMEM_LIMIT):
    spaces = [pltpu.SMEM] * len(smem) + [pltpu.VMEM] * len(vmem) + [pl.ANY] * len(anywhere)
    return pl.pallas_call(
        kernel,
        out_shape=outputs,
        in_specs=[pl.BlockSpec(memory_space=space) for space in spaces],
        out_specs=[pl.BlockSpec(memory_space=out_space)] * len(outputs),
        scratch_shapes=scratch,
        compiler_params=pltpu.CompilerParams(vmem_limit_bytes=limit),
        cost_estimate=pl.CostEstimate(flops=0, bytes_accessed=0, transcendentals=0),
    )(*smem, *vmem, *anywhere)


def prepare(own, energies, rows, width):
    size = rows // CHUNKS
    cut = size * width // LANES
    share = width // HALVES

    def kernel(energy_ref, own_ref, high_out, low_out, *refs):
        integral_outs, refs = refs[:HALVES], refs[HALVES:]
        sent_refs = refs[: CHUNKS - 1]
        block_ref, turned_ref, integrals_ref, semaphores = refs[CHUNKS - 1 :]
        copies = Copies(semaphores)
        coming = [copies.start(own_ref.at[pl.ds(at * cut, cut)], block_ref.at[at]) for at in range(CHUNKS)]
        leaving = [copies.start(energy_ref, ref.at[pl.ds(cut, SUBLANES)]) for ref in sent_refs]
        for at in range(CHUNKS):
            coming[at].wait()
            if at:
                leaving.append(copies.start(block_ref.at[at], sent_refs[at - 1].at[pl.ds(0, cut)]))
            block = rows_of(block_ref.at[at], 0, size, width)
            high, low = split(block.T)
            turned_ref[0, at] = high
            turned_ref[1, at] = low
            leaving.append(copies.start(turned_ref.at[0, at], high_out.at[at]))
            leaving.append(copies.start(turned_ref.at[1, at], low_out.at[at]))
            value = dot(jnp.concatenate([high, low, high], axis=1), deep_right(block))
            integrals_ref[...] = integrals_ref[...] + value if at else value
        for at, out_ref in enumerate(integral_outs):
            leaving.append(copies.start(integrals_ref.at[pl.ds(at * share, share)], out_ref))
        for copy in leaving:
            copy.wait()

    turned = jax.ShapeDtypeStruct((CHUNKS, width, size), jnp.bfloat16)
    square = jax.ShapeDtypeStruct((share, width), jnp.float32)
    sent = jax.ShapeDtypeStruct((cut + SUBLANES, LANES), jnp.float32)
    scratch = [
        pltpu.VMEM((CHUNKS, cut, LANES), jnp.float32),
        pltpu.VMEM((2, CHUNKS, width, size), jnp.bfloat16),
        pltpu.VMEM((width, width), jnp.float32),
        pltpu.SemaphoreType.DMA((5 * CHUNKS + HALVES,)),
    ]
    outs = [turned, turned] + [square] * HALVES + [sent] * (CHUNKS - 1)
    return call(kernel, [], [energies], [own], outs, pl.ANY, scratch)


def arrays_of(pieces):
    return distinct([array for piece in pieces for array, _ in piece.places])


def integrate(turned, slots, first, flags, size, width, before=(), limit=VMEM_LIMIT):
    cut = size * width // LANES
    count = len(slots)
    pieces = [piece for slot in slots for piece in slot]
    arrays = arrays_of(pieces)
    numbers = [list(range(start, start + len(slot))) for slot, start in zip(slots, first)]
    needed = sorted({number for some in numbers for number in some})
    before = [part for parts in before for part in parts]
    share = width // HALVES

    def kernel(flag_ref, *refs):
        given = iter(refs)
        high_ref, low_ref = next(given), next(given)
        before_refs = [next(given) for _ in before]
        ref_of = {id(array): next(given) for array in arrays}
        outs = [[next(given) for _ in range(HALVES)] for _ in range(count)]
        turned_ref, block_ref, before_ref, semaphores = given
        copies = Copies(semaphores)
        coming, turning = [], {}

        def turn(number):
            if number not in turning:
                at = needed.index(number)
                turning[number] = [
                    copies.start(high_ref.at[number], turned_ref.at[at, 0]),
                    copies.start(low_ref.at[number], turned_ref.at[at, 1]),
                ]

        at = 0
        for slot in range(count):
            for number, piece in zip(numbers[slot], slots[slot]):
                turn(number)
                coming.append(copies.start_piece(piece, ref_of, flag_ref, cut, block_ref.at[at]))
                at += 1
        adding = [
            copies.start(ref, before_ref.at[at // HALVES, pl.ds(at % HALVES * share, share)])
            for at, ref in enumerate(before_refs)
        ]
        at = 0
        for slot in range(count):
            total = None
            for place, number in enumerate(numbers[slot]):
                for copy in turning.pop(number, []):
                    copy.wait()
                coming[at].wait()
                there = needed.index(number)
                high, low = turned_ref[there, 0], turned_ref[there, 1]
                left = jnp.concatenate([high, low, high], axis=1)
                value = dot(left, deep_right(rows_of(block_ref.at[at], 0, size, width)))
                total = total + value if place else value
                at += 1
            if before:
                for number in range(HALVES):
                    adding[slot * HALVES + number].wait()
                total = total + before_ref[slot]
            for number, out_ref in enumerate(outs[slot]):
                out_ref[...] = total[number * share : (number + 1) * share]

    out = [jax.ShapeDtypeStruct((share, width), jnp.float32)] * (HALVES * count)
    scratch = [
        pltpu.VMEM((len(needed), 2, width, size), jnp.bfloat16),
        pltpu.VMEM((len(pieces), cut, LANES), jnp.float32),
        pltpu.VMEM((max(len(before) // HALVES, 1), width, width), jnp.float32),
        pltpu.SemaphoreType.DMA((2 * len(needed) + len(pieces) + len(before),)),
    ]
    made = call(kernel, [flags], [], [*turned, *before, *arrays], out, pltpu.VMEM, scratch, limit)
    return [made[slot * HALVES : (slot + 1) * HALVES] for slot in range(count)]


def contract(partials, slots, signs, first_sign, energies, flags, eps_virt, size, before=None, limit=VMEM_LIMIT):
    count = len(slots)
    chunks = len(slots[0])
    virt = eps_virt.shape[1]
    width = partials[0][0][0].shape[1]
    share = width // HALVES
    occ_rows = width // virt
    lines = width // LANES
    cut = size * lines
    sums = [part for slot in partials for term in slot for part in term]
    pieces = [piece for slot in slots for piece in slot]
    arrays = arrays_of([*pieces, *energies])
    last = [before] if before is not None else []

    def kernel(*refs):
        given = iter(refs)
        sign_ref, flag_ref, virt_ref = next(given), next(given), next(given)
        sum_refs = [next(given) for _ in sums]
        before_refs = [next(given) for _ in last]
        ref_of = {id(array): next(given) for array in arrays}
        out_ref, energy_ref, sum_ref, block_ref, result_ref, right_ref, semaphores = given
        copies = Copies(semaphores)
        arriving = [
            copies.start_piece(piece, ref_of, flag_ref, SUBLANES, energy_ref.at[at])
            for at, piece in enumerate(energies)
        ]
        arriving += [
            copies.start(ref, sum_ref.at[at // HALVES, pl.ds(at % HALVES * share, share)])
            for at, ref in enumerate(sum_refs)
        ]
        coming = [
            [
                copies.start_piece(slots[slot][at], ref_of, flag_ref, cut, block_ref.at[slot, at])
                for slot in range(count)
            ]
            for at in range(chunks)
        ]
        adding = [
            [copies.start(ref.at[pl.ds(at * cut, cut)], result_ref.at[at]) for ref in before_refs]
            for at in range(chunks)
        ]
        for copy in arriving:
            copy.wait()

        def line(at):
            virtual = virt_ref[...]
            energy = energy_ref[at]
            return jnp.concatenate([virtual - energy[:1, i : i + 1] for i in range(occ_rows)], axis=1)

        row = jnp.broadcast_to(line(0), (SUBLANES, width)).T[:, :1]
        at = 0
        for slot in range(count):
            total = sum_ref[at]
            for extra in range(1, len(partials[slot])):
                total = total + sum_ref[at + extra]
            at += len(partials[slot])
            amplitude = (sign_ref[first_sign + slot] * total) / (row + line(slot + 1))
            right_ref[:, pl.ds(slot * 3 * width, 3 * width)] = deep_right(amplitude, 1)
        leaving = []
        for at in range(chunks):
            for copy in coming[at] + adding[at]:
                copy.wait()
            left = [deep_left(rows_of(block_ref.at[slot, at], 0, size, width)) for slot in range(count)]
            value = dot(jnp.concatenate(left, axis=1), right_ref[...], 1)
            for column in range(lines):
                lanes = value[:, column * LANES : (column + 1) * LANES]
                where = pl.ds(column, size, stride=lines)
                if last:
                    lanes = lanes + result_ref[at, where, :]
                result_ref[at, where, :] = lanes
            leaving.append(copies.start(result_ref.at[at], out_ref.at[pl.ds(at * cut, cut)]))
        for copy in leaving:
            copy.wait()

    rows = chunks * size
    out = jax.ShapeDtypeStruct((rows * lines, LANES), jnp.float32)
    scratch = [
        pltpu.VMEM((len(energies), SUBLANES, LANES), jnp.float32),
        pltpu.VMEM((len(sums) // HALVES, width, width), jnp.float32),
        pltpu.VMEM((count, chunks, cut, LANES), jnp.float32),
        pltpu.VMEM((chunks, cut, LANES), jnp.float32),
        pltpu.VMEM((width, count * 3 * width), jnp.bfloat16),
        pltpu.SemaphoreType.DMA((len(energies) + len(sums) + len(pieces) + 2 * chunks,)),
    ]
    return call(kernel, [signs, flags], [eps_virt], [*sums, *last, *arrays], [out], pl.ANY, scratch, limit)[0]


def after(block, *others):
    return lax.optimization_barrier((block, *others))[0]


def on_device(factors, eps_occ, eps_virt, pair_mask):
    rows, occ_rows, virt = factors.shape
    width = occ_rows * virt
    lines = width // LANES
    groups = lax.axis_size("occ")
    shares = lax.axis_size("aux")
    size = rows // CHUNKS
    cut = size * lines
    last = CHUNKS - 1
    group = lax.axis_index("occ")
    place = group % PLANE
    odd_x = place % 2 == 1
    odd_y = place // 2 == 1

    own = factors.reshape(rows * lines, LANES)
    energies = jnp.zeros((SUBLANES * LANES,), jnp.float32).at[:occ_rows].set(eps_occ)
    energies = energies.reshape(SUBLANES, LANES)

    def part(whole, at):
        return whole[at * cut : (at + 1) * cut]

    def within(block, moves):
        planes = range(0, groups, PLANE)
        return lax.ppermute(block, "occ", [(g + a, g + b) for g in planes for a, b in moves])

    def up(block):
        return lax.ppermute(block, "occ", [(g, g + PLANE) for g in range(groups - PLANE)])

    def totals(parts):
        if shares == 2:
            return [parts, [lax.ppermute(part, "aux", [(0, 1), (1, 0)]) for part in parts]]
        return [[lax.psum(part, "aux") for part in parts]]

    first_sent = jnp.concatenate([part(own, 0), energies])
    def choices(sent):
        group_then, mask_row, _ = lax.optimization_barrier((group, pair_mask[0], sent))
        place_then = group_then % PLANE

        def sign(offset):
            flag = jnp.sum(jnp.where(jnp.arange(1, PLANE + 1) == offset, mask_row, 0))
            return jnp.where((group_then >= offset) & (flag > 0), -1.0, 0.0).astype(jnp.float32)

        near = jnp.where(place_then % 2 == 1, 1, PLANE - 1)
        signs = [jnp.float32(-1.0), sign(PLANE), sign(near), sign(PLANE // 2), sign(PLANE - near)]
        up_then = place_then // 2 == 1
        flags = [
            1 - place_then % 2,
            1 - place_then // 2,
            jnp.where(up_then, 0, 1 + place_then),
            jnp.where(up_then, place_then - 1, 0),
        ]
        return jnp.stack(signs), jnp.stack(flags).astype(jnp.int32)

    def add(first_sign, partials, slots, carriers, before=None, limit=VMEM_LIMIT):
        return contract(
            partials, slots, signs, first_sign, carriers, flags, eps_virt[None, :], size, before, limit
        )

    from_own = [first_sent]
    from_z = [up(first_sent)]
    up_x = within(first_sent, [(0, 1), (2, 3), (1, 0)])
    up_y = within(first_sent, [(0, 2), (1, 3)])
    high, low, *made = prepare(own, energies, rows, width)
    partial_own = made[:HALVES]
    from_own += made[HALVES:]
    turned = (high, low)
    sums_own = totals(partial_own)
    swap_x, swap_y = [], []
    passed = [partial_own[0]]
    for at in range(CHUNKS):
        came = after(from_z[at], *passed)
        if at < last:
            from_z.append(up(after(from_own[at + 1], came)))
            up_part = after(from_own[at + 1], came)
            send_x, send_y = jnp.where(odd_x, came, up_part), jnp.where(odd_y, came, up_part)
            send_x = after(send_x, swap_x[at - 1] if at else up_x)
            send_y = after(send_y, swap_y[at - 1] if at else up_y)
            if at == 0:
                signs, flags = choices((send_x, send_y))
            swap_x.append(within(send_x, [(0, 1), (1, 0), (2, 3), (3, 2)]))
            swap_y.append(within(send_y, [(0, 2), (2, 0), (1, 3), (3, 1)]))
        else:
            cycle = within(after(turning, came, swap_x[last - 1]), [(0, 1), (1, 3), (3, 2), (2, 0)])
            send_x = after(jnp.where(odd_x, came, swap_y[0]), swap_x[last - 1])
            send_y = after(jnp.where(odd_y, came, up_x), swap_y[last - 1])
            swap_x.append(within(send_x, [(0, 1), (1, 0), (2, 3), (3, 2)]))
            swap_y.append(within(send_y, [(0, 2), (2, 0), (1, 3), (3, 1)]))
        passed = []
        if at == 1:
            passed = [signs, flags]
            middle = (place == 1) | (place == 2)
            turning = jnp.where(middle, swap_x[1], swap_y[1])
        if at == 2:
            passed.append(turning)

    cross = within(jnp.where(place == 2, swap_x[0], swap_y[0]), [(2, 0), (3, 2)])
    swap_d = within(swap_y[2], [(0, 1), (1, 0), (2, 3), (3, 2)])
    last_d = within(swap_y[3], [(0, 1), (1, 0)])

    def pieces_of(first, swaps, choice, base):
        arrays = [first, *swaps]
        return [Piece(((arrays[at], base), (arrays[at + 1], base)), choice) for at in range(CHUNKS)]

    def whole(array, base):
        return Piece(((array, base),))

    slot_own = [whole(own, at * cut) for at in range(CHUNKS)]
    slot_z = [whole(block, 0) for block in from_z]
    slot_x = pieces_of(up_x, swap_x, 0, 0)
    slot_y = pieces_of(up_y, swap_y, 1, 0)
    slot_d = [
        Piece(((swap_y[last], 0), (cross, 0), (swap_x[last], 0)), 2),
        Piece(((cycle, 0), (cross, 0), (swap_x[last], 0)), 3),
        Piece(((cycle, 0), (swap_d, 0)), 1),
        Piece(((swap_d, 0), (last_d, 0)), 1),
    ]
    eps_x = pieces_of(up_x, swap_x, 0, cut)[0]
    eps_y = pieces_of(up_y, swap_y, 1, cut)[0]
    eps_d = Piece(((swap_y[last], cut), (cross, cut), (swap_x[last], cut)), 2)

    partial_z, *early = integrate(
        turned, [slot_z, slot_x[:last], slot_y[:last]], [0, 0, 0], flags, size, width
    )
    own_eps = whole(first_sent, cut)
    partial_x, partial_y = integrate(
        turned, [slot_x[last:], slot_y[last:]], [last, last], flags, size, width, early
    )
    gradient = add(
        0,
        [after(sums_own, cycle), totals(partial_z), totals(partial_x), totals(partial_y)],
        [slot_own, slot_z, slot_x, slot_y],
        [own_eps, own_eps, whole(from_z[0], cut), eps_x, eps_y],
    )
    turned = after(turned, gradient)
    half = CHUNKS // 2
    partial_d = integrate(turned, [slot_d[:half]], [0], flags, size, width)
    (partial_d,) = integrate(turned, [slot_d[half:]], [half], flags, size, width, partial_d, LAST_LIMIT)
    gradient = add(4, [totals(partial_d)], [slot_d], [own_eps, eps_d], gradient, LAST_LIMIT)
    return gradient.reshape(rows, occ_rows, virt)


def solution(mesh):
    if mesh.shape["occ"] % PLANE:
        raise ValueError("incomplete plane")
    in_specs = (P("aux", "occ", None), P("occ"), P(), P("occ", None))
    out_specs = P("aux", "occ", None)
    return jax.shard_map(
        on_device, mesh=mesh, in_specs=in_specs, out_specs=out_specs, check_vma=False
    )
```

```python
import dataclasses
import functools

import jax
import jax.numpy as jnp
from jax import lax
from jax.experimental import pallas as pl
from jax.experimental.pallas import tpu as pltpu
from jax.sharding import PartitionSpec as P

LANES = 128
SUBLANES = 8
PLANE = 4
CHUNKS = 4
VMEM_LIMIT = 60 * 1024 * 1024
LAST_LIMIT = 24 * 1024 * 1024
HALVES = 2


def split(value):
    high = value.astype(jnp.bfloat16)
    low = (value - high.astype(jnp.float32)).astype(jnp.bfloat16)
    return high, low


def deep_left(value):
    high, low = split(value)
    return jnp.concatenate([high, low, high], axis=1)


def deep_right(value, axis=0):
    high, low = split(value)
    return jnp.concatenate([high, high, low], axis=axis)


def dot(left, right, axis=0):
    numbers = (((1,), (axis,)), ((), ()))
    return lax.dot_general(left, right, numbers, preferred_element_type=jnp.float32)


def rows_of(ref, start, count, width):
    lines = width // LANES
    columns = [ref[pl.ds(start * lines + at, count, stride=lines), :] for at in range(lines)]
    return jnp.concatenate(columns, axis=1)


def distinct(arrays):
    return list({id(array): array for array in arrays}.values())


class Copies:
    def __init__(self, semaphores):
        self.semaphores = semaphores
        self.used = 0

    def start(self, source, target):
        copy = pltpu.make_async_copy(source, target, self.semaphores.at[self.used])
        self.used += 1
        copy.start()
        return copy

    def start_piece(self, piece, ref_of, choices, count, target):
        made = []
        for array, base in piece.places:
            source = ref_of[id(array)].at[pl.ds(base, count)]
            made.append(pltpu.make_async_copy(source, target, self.semaphores.at[self.used]))
        self.used += 1
        if len(made) == 1:
            made[0].start()
        else:
            for at, copy in enumerate(made):
                pl.when(choices[piece.choice] == at)(copy.start)
        return made[0]


@dataclasses.dataclass(frozen=True)
class Piece:
    places: tuple
    choice: int = 0


def call(kernel, smem, vmem, anywhere, outputs, out_space, scratch, limit=VMEM_LIMIT):
    spaces = [pltpu.SMEM] * len(smem) + [pltpu.VMEM] * len(vmem) + [pl.ANY] * len(anywhere)
    return pl.pallas_call(
        kernel,
        out_shape=outputs,
        in_specs=[pl.BlockSpec(memory_space=space) for space in spaces],
        out_specs=[pl.BlockSpec(memory_space=out_space)] * len(outputs),
        scratch_shapes=scratch,
        compiler_params=pltpu.CompilerParams(vmem_limit_bytes=limit),
        cost_estimate=pl.CostEstimate(flops=0, bytes_accessed=0, transcendentals=0),
    )(*smem, *vmem, *anywhere)


def prepare(own, energies, rows, width):
    size = rows // CHUNKS
    cut = size * width // LANES
    share = width // HALVES

    def kernel(energy_ref, own_ref, high_out, low_out, *refs):
        integral_outs, refs = refs[:HALVES], refs[HALVES:]
        sent_refs = refs[: CHUNKS - 1]
        block_ref, turned_ref, integrals_ref, semaphores = refs[CHUNKS - 1 :]
        copies = Copies(semaphores)
        coming = [copies.start(own_ref.at[pl.ds(at * cut, cut)], block_ref.at[at]) for at in range(CHUNKS)]
        leaving = [copies.start(energy_ref, ref.at[pl.ds(cut, SUBLANES)]) for ref in sent_refs]
        for at in range(CHUNKS):
            coming[at].wait()
            if at:
                leaving.append(copies.start(block_ref.at[at], sent_refs[at - 1].at[pl.ds(0, cut)]))
            block = rows_of(block_ref.at[at], 0, size, width)
            high, low = split(block.T)
            turned_ref[0, at] = high
            turned_ref[1, at] = low
            leaving.append(copies.start(turned_ref.at[0, at], high_out.at[at]))
            leaving.append(copies.start(turned_ref.at[1, at], low_out.at[at]))
            value = dot(jnp.concatenate([high, low, high], axis=1), deep_right(block))
            integrals_ref[...] = integrals_ref[...] + value if at else value
        for at, out_ref in enumerate(integral_outs):
            leaving.append(copies.start(integrals_ref.at[pl.ds(at * share, share)], out_ref))
        for copy in leaving:
            copy.wait()

    turned = jax.ShapeDtypeStruct((CHUNKS, width, size), jnp.bfloat16)
    square = jax.ShapeDtypeStruct((share, width), jnp.float32)
    sent = jax.ShapeDtypeStruct((cut + SUBLANES, LANES), jnp.float32)
    scratch = [
        pltpu.VMEM((CHUNKS, cut, LANES), jnp.float32),
        pltpu.VMEM((2, CHUNKS, width, size), jnp.bfloat16),
        pltpu.VMEM((width, width), jnp.float32),
        pltpu.SemaphoreType.DMA((5 * CHUNKS + HALVES,)),
    ]
    outs = [turned, turned] + [square] * HALVES + [sent] * (CHUNKS - 1)
    return call(kernel, [], [energies], [own], outs, pl.ANY, scratch)


def arrays_of(pieces):
    return distinct([array for piece in pieces for array, _ in piece.places])


def integrate(turned, slots, first, flags, size, width, before=(), limit=VMEM_LIMIT):
    cut = size * width // LANES
    count = len(slots)
    pieces = [piece for slot in slots for piece in slot]
    arrays = arrays_of(pieces)
    numbers = [list(range(start, start + len(slot))) for slot, start in zip(slots, first)]
    needed = sorted({number for some in numbers for number in some})
    before = [part for parts in before for part in parts]
    share = width // HALVES

    def kernel(flag_ref, *refs):
        given = iter(refs)
        high_ref, low_ref = next(given), next(given)
        before_refs = [next(given) for _ in before]
        ref_of = {id(array): next(given) for array in arrays}
        outs = [[next(given) for _ in range(HALVES)] for _ in range(count)]
        turned_ref, block_ref, before_ref, semaphores = given
        copies = Copies(semaphores)
        coming, turning = [], {}

        def turn(number):
            if number not in turning:
                at = needed.index(number)
                turning[number] = [
                    copies.start(high_ref.at[number], turned_ref.at[at, 0]),
                    copies.start(low_ref.at[number], turned_ref.at[at, 1]),
                ]

        at = 0
        for slot in range(count):
            for number, piece in zip(numbers[slot], slots[slot]):
                turn(number)
                coming.append(copies.start_piece(piece, ref_of, flag_ref, cut, block_ref.at[at]))
                at += 1
        adding = [
            copies.start(ref, before_ref.at[at // HALVES, pl.ds(at % HALVES * share, share)])
            for at, ref in enumerate(before_refs)
        ]
        at = 0
        for slot in range(count):
            total = None
            for place, number in enumerate(numbers[slot]):
                for copy in turning.pop(number, []):
                    copy.wait()
                coming[at].wait()
                there = needed.index(number)
                high, low = turned_ref[there, 0], turned_ref[there, 1]
                left = jnp.concatenate([high, low, high], axis=1)
                value = dot(left, deep_right(rows_of(block_ref.at[at], 0, size, width)))
                total = total + value if place else value
                at += 1
            if before:
                for number in range(HALVES):
                    adding[slot * HALVES + number].wait()
                total = total + before_ref[slot]
            for number, out_ref in enumerate(outs[slot]):
                out_ref[...] = total[number * share : (number + 1) * share]

    out = [jax.ShapeDtypeStruct((share, width), jnp.float32)] * (HALVES * count)
    scratch = [
        pltpu.VMEM((len(needed), 2, width, size), jnp.bfloat16),
        pltpu.VMEM((len(pieces), cut, LANES), jnp.float32),
        pltpu.VMEM((max(len(before) // HALVES, 1), width, width), jnp.float32),
        pltpu.SemaphoreType.DMA((2 * len(needed) + len(pieces) + len(before),)),
    ]
    made = call(kernel, [flags], [], [*turned, *before, *arrays], out, pltpu.VMEM, scratch, limit)
    return [made[slot * HALVES : (slot + 1) * HALVES] for slot in range(count)]


def contract(partials, slots, signs, first_sign, energies, flags, eps_virt, size, before=None, limit=VMEM_LIMIT):
    count = len(slots)
    chunks = len(slots[0])
    virt = eps_virt.shape[1]
    width = partials[0][0][0].shape[1]
    share = width // HALVES
    occ_rows = width // virt
    lines = width // LANES
    cut = size * lines
    sums = [part for slot in partials for term in slot for part in term]
    pieces = [piece for slot in slots for piece in slot]
    arrays = arrays_of([*pieces, *energies])
    last = [before] if before is not None else []

    def kernel(*refs):
        given = iter(refs)
        sign_ref, flag_ref, virt_ref = next(given), next(given), next(given)
        sum_refs = [next(given) for _ in sums]
        before_refs = [next(given) for _ in last]
        ref_of = {id(array): next(given) for array in arrays}
        out_ref, energy_ref, sum_ref, block_ref, result_ref, right_ref, semaphores = given
        copies = Copies(semaphores)
        arriving = [
            copies.start_piece(piece, ref_of, flag_ref, SUBLANES, energy_ref.at[at])
            for at, piece in enumerate(energies)
        ]
        arriving += [
            copies.start(ref, sum_ref.at[at // HALVES, pl.ds(at % HALVES * share, share)])
            for at, ref in enumerate(sum_refs)
        ]
        coming = [
            [
                copies.start_piece(slots[slot][at], ref_of, flag_ref, cut, block_ref.at[slot, at])
                for slot in range(count)
            ]
            for at in range(chunks)
        ]
        adding = [
            [copies.start(ref.at[pl.ds(at * cut, cut)], result_ref.at[at]) for ref in before_refs]
            for at in range(chunks)
        ]
        for copy in arriving:
            copy.wait()

        def line(at):
            virtual = virt_ref[...]
            energy = energy_ref[at]
            return jnp.concatenate([virtual - energy[:1, i : i + 1] for i in range(occ_rows)], axis=1)

        row = jnp.broadcast_to(line(0), (SUBLANES, width)).T[:, :1]
        at = 0
        for slot in range(count):
            total = sum_ref[at]
            for extra in range(1, len(partials[slot])):
                total = total + sum_ref[at + extra]
            at += len(partials[slot])
            amplitude = (sign_ref[first_sign + slot] * total) / (row + line(slot + 1))
            right_ref[:, pl.ds(slot * 3 * width, 3 * width)] = deep_right(amplitude, 1)
        leaving = []
        for at in range(chunks):
            for copy in coming[at] + adding[at]:
                copy.wait()
            left = [deep_left(rows_of(block_ref.at[slot, at], 0, size, width)) for slot in range(count)]
            value = dot(jnp.concatenate(left, axis=1), right_ref[...], 1)
            for column in range(lines):
                lanes = value[:, column * LANES : (column + 1) * LANES]
                where = pl.ds(column, size, stride=lines)
                if last:
                    lanes = lanes + result_ref[at, where, :]
                result_ref[at, where, :] = lanes
            leaving.append(copies.start(result_ref.at[at], out_ref.at[pl.ds(at * cut, cut)]))
        for copy in leaving:
            copy.wait()

    rows = chunks * size
    out = jax.ShapeDtypeStruct((rows * lines, LANES), jnp.float32)
    scratch = [
        pltpu.VMEM((len(energies), SUBLANES, LANES), jnp.float32),
        pltpu.VMEM((len(sums) // HALVES, width, width), jnp.float32),
        pltpu.VMEM((count, chunks, cut, LANES), jnp.float32),
        pltpu.VMEM((chunks, cut, LANES), jnp.float32),
        pltpu.VMEM((width, count * 3 * width), jnp.bfloat16),
        pltpu.SemaphoreType.DMA((len(energies) + len(sums) + len(pieces) + 2 * chunks,)),
    ]
    return call(kernel, [signs, flags], [eps_virt], [*sums, *last, *arrays], [out], pl.ANY, scratch, limit)[0]


def after(block, *others):
    return lax.optimization_barrier((block, *others))[0]


def on_device(factors, eps_occ, eps_virt, pair_mask):
    rows, occ_rows, virt = factors.shape
    width = occ_rows * virt
    lines = width // LANES
    groups = lax.axis_size("occ")
    shares = lax.axis_size("aux")
    size = rows // CHUNKS
    cut = size * lines
    last = CHUNKS - 1
    group = lax.axis_index("occ")
    place = group % PLANE
    odd_x = place % 2 == 1
    odd_y = place // 2 == 1

    own = factors.reshape(rows * lines, LANES)
    energies = jnp.zeros((SUBLANES * LANES,), jnp.float32).at[:occ_rows].set(eps_occ)
    energies = energies.reshape(SUBLANES, LANES)

    def part(whole, at):
        return whole[at * cut : (at + 1) * cut]

    def within(block, moves):
        planes = range(0, groups, PLANE)
        return lax.ppermute(block, "occ", [(g + a, g + b) for g in planes for a, b in moves])

    def up(block):
        return lax.ppermute(block, "occ", [(g, g + PLANE) for g in range(groups - PLANE)])

    def totals(parts):
        if shares == 2:
            return [parts, [lax.ppermute(part, "aux", [(0, 1), (1, 0)]) for part in parts]]
        return [[lax.psum(part, "aux") for part in parts]]

    first_sent = jnp.concatenate([part(own, 0), energies])
    def choices(sent):
        group_then, mask_row, _ = lax.optimization_barrier((group, pair_mask[0], sent))
        place_then = group_then % PLANE

        def sign(offset):
            flag = jnp.sum(jnp.where(jnp.arange(1, PLANE + 1) == offset, mask_row, 0))
            return jnp.where((group_then >= offset) & (flag > 0), -1.0, 0.0).astype(jnp.float32)

        near = jnp.where(place_then % 2 == 1, 1, PLANE - 1)
        signs = [jnp.float32(-1.0), sign(PLANE), sign(near), sign(PLANE // 2), sign(PLANE - near)]
        up_then = place_then // 2 == 1
        flags = [
            1 - place_then % 2,
            1 - place_then // 2,
            jnp.where(up_then, 0, 1 + place_then),
            jnp.where(up_then, place_then - 1, 0),
        ]
        return jnp.stack(signs), jnp.stack(flags).astype(jnp.int32)

    def add(first_sign, partials, slots, carriers, before=None, limit=VMEM_LIMIT):
        return contract(
            partials, slots, signs, first_sign, carriers, flags, eps_virt[None, :], size, before, limit
        )

    from_own = [first_sent]
    from_z = [up(first_sent)]
    up_x = within(first_sent, [(0, 1), (2, 3), (1, 0)])
    up_y = within(first_sent, [(0, 2), (1, 3)])
    high, low, *made = prepare(own, energies, rows, width)
    partial_own = made[:HALVES]
    from_own += made[HALVES:]
    turned = (high, low)
    sums_own = totals(partial_own)
    swap_x, swap_y = [], []
    passed = [partial_own[0]]
    for at in range(CHUNKS):
        came = after(from_z[at], *passed)
        if at < last:
            from_z.append(up(after(from_own[at + 1], came)))
            up_part = after(from_own[at + 1], came)
            send_x, send_y = jnp.where(odd_x, came, up_part), jnp.where(odd_y, came, up_part)
            send_x = after(send_x, swap_x[at - 1] if at else up_x)
            send_y = after(send_y, swap_y[at - 1] if at else up_y)
            if at == 0:
                signs, flags = choices((send_x, send_y))
            swap_x.append(within(send_x, [(0, 1), (1, 0), (2, 3), (3, 2)]))
            swap_y.append(within(send_y, [(0, 2), (2, 0), (1, 3), (3, 1)]))
        else:
            cycle = within(after(turning, came, swap_x[last - 1]), [(0, 1), (1, 3), (3, 2), (2, 0)])
            send_x = after(jnp.where(odd_x, came, swap_y[0]), swap_x[last - 1])
            send_y = after(jnp.where(odd_y, came, up_x), swap_y[last - 1])
            swap_x.append(within(send_x, [(0, 1), (1, 0), (2, 3), (3, 2)]))
            swap_y.append(within(send_y, [(0, 2), (2, 0), (1, 3), (3, 1)]))
        passed = []
        if at == 0:
            own_eps = Piece(((first_sent, cut),))
            slot_own = [Piece(((own, number * cut),)) for number in range(CHUNKS)]
            gradient = add(0, [after(sums_own, swap_x[0])], [slot_own], [own_eps, own_eps])
        if at == 1:
            passed = [signs, flags, gradient]
            middle = (place == 1) | (place == 2)
            turning = jnp.where(middle, swap_x[1], swap_y[1])
        if at == 2:
            passed.append(turning)

    cross = within(jnp.where(place == 2, swap_x[0], swap_y[0]), [(2, 0), (3, 2)])
    swap_d = within(swap_y[2], [(0, 1), (1, 0), (2, 3), (3, 2)])
    last_d = within(swap_y[3], [(0, 1), (1, 0)])

    def pieces_of(first, swaps, choice, base):
        arrays = [first, *swaps]
        return [Piece(((arrays[at], base), (arrays[at + 1], base)), choice) for at in range(CHUNKS)]

    def whole(array, base):
        return Piece(((array, base),))

    slot_z = [whole(block, 0) for block in from_z]
    slot_x = pieces_of(up_x, swap_x, 0, 0)
    slot_y = pieces_of(up_y, swap_y, 1, 0)
    slot_d = [
        Piece(((swap_y[last], 0), (cross, 0), (swap_x[last], 0)), 2),
        Piece(((cycle, 0), (cross, 0), (swap_x[last], 0)), 3),
        Piece(((cycle, 0), (swap_d, 0)), 1),
        Piece(((swap_d, 0), (last_d, 0)), 1),
    ]
    eps_x = pieces_of(up_x, swap_x, 0, cut)[0]
    eps_y = pieces_of(up_y, swap_y, 1, cut)[0]
    eps_d = Piece(((swap_y[last], cut), (cross, cut), (swap_x[last], cut)), 2)

    partial_z, *early = integrate(
        turned, [slot_z, slot_x[:last], slot_y[:last]], [0, 0, 0], flags, size, width
    )
    partial_x, partial_y = integrate(
        turned, [slot_x[last:], slot_y[last:]], [last, last], flags, size, width, early
    )
    gradient = add(
        1,
        [after(totals(partial_z), cycle), totals(partial_x), totals(partial_y)],
        [slot_z, slot_x, slot_y],
        [own_eps, whole(from_z[0], cut), eps_x, eps_y],
        gradient,
    )
    turned = after(turned, gradient)
    half = CHUNKS // 2
    partial_d = integrate(turned, [slot_d[:half]], [0], flags, size, width)
    (partial_d,) = integrate(turned, [slot_d[half:]], [half], flags, size, width, partial_d, LAST_LIMIT)
    gradient = add(4, [totals(partial_d)], [slot_d], [own_eps, eps_d], gradient, LAST_LIMIT)
    return gradient.reshape(rows, occ_rows, virt)


def solution(mesh):
    if mesh.shape["occ"] % PLANE:
        raise ValueError("incomplete plane")
    in_specs = (P("aux", "occ", None), P("occ"), P(), P("occ", None))
    out_specs = P("aux", "occ", None)
    return jax.shard_map(
        on_device, mesh=mesh, in_specs=in_specs, out_specs=out_specs, check_vma=False
    )
```

```python
import dataclasses
import functools

import jax
import jax.numpy as jnp
from jax import lax
from jax.experimental import pallas as pl
from jax.experimental.pallas import tpu as pltpu
from jax.sharding import PartitionSpec as P

LANES = 128
SUBLANES = 8
PLANE = 4
CHUNKS = 4
VMEM_LIMIT = 32 * 1024 * 1024
LAST_LIMIT = 24 * 1024 * 1024
HALVES = 2


def split(value):
    high = value.astype(jnp.bfloat16)
    low = (value - high.astype(jnp.float32)).astype(jnp.bfloat16)
    return high, low


def deep_left(value):
    high, low = split(value)
    return jnp.concatenate([high, low, high], axis=1)


def deep_right(value, axis=0):
    high, low = split(value)
    return jnp.concatenate([high, high, low], axis=axis)


def dot(left, right, axis=0):
    numbers = (((1,), (axis,)), ((), ()))
    return lax.dot_general(left, right, numbers, preferred_element_type=jnp.float32)


def rows_of(ref, start, count, width):
    lines = width // LANES
    columns = [ref[pl.ds(start * lines + at, count, stride=lines), :] for at in range(lines)]
    return jnp.concatenate(columns, axis=1)


def distinct(arrays):
    return list({id(array): array for array in arrays}.values())


class Copies:
    def __init__(self, semaphores):
        self.semaphores = semaphores
        self.used = 0

    def start(self, source, target):
        copy = pltpu.make_async_copy(source, target, self.semaphores.at[self.used])
        self.used += 1
        copy.start()
        return copy

    def start_piece(self, piece, ref_of, choices, count, target):
        made = []
        for array, base in piece.places:
            source = ref_of[id(array)].at[pl.ds(base, count)]
            made.append(pltpu.make_async_copy(source, target, self.semaphores.at[self.used]))
        self.used += 1
        if len(made) == 1:
            made[0].start()
        else:
            for at, copy in enumerate(made):
                pl.when(choices[piece.choice] == at)(copy.start)
        return made[0]


@dataclasses.dataclass(frozen=True)
class Piece:
    places: tuple
    choice: int = 0


def call(kernel, smem, vmem, anywhere, outputs, out_space, scratch, limit=VMEM_LIMIT):
    spaces = [pltpu.SMEM] * len(smem) + [pltpu.VMEM] * len(vmem) + [pl.ANY] * len(anywhere)
    return pl.pallas_call(
        kernel,
        out_shape=outputs,
        in_specs=[pl.BlockSpec(memory_space=space) for space in spaces],
        out_specs=[pl.BlockSpec(memory_space=out_space)] * len(outputs),
        scratch_shapes=scratch,
        compiler_params=pltpu.CompilerParams(vmem_limit_bytes=limit),
        cost_estimate=pl.CostEstimate(flops=0, bytes_accessed=0, transcendentals=0),
    )(*smem, *vmem, *anywhere)


def prepare(own, energies, rows, width):
    size = rows // CHUNKS
    cut = size * width // LANES
    share = width // HALVES

    def kernel(energy_ref, own_ref, high_out, low_out, *refs):
        integral_outs, refs = refs[:HALVES], refs[HALVES:]
        sent_refs = refs[: CHUNKS - 1]
        block_ref, turned_ref, integrals_ref, semaphores = refs[CHUNKS - 1 :]
        copies = Copies(semaphores)
        coming = [copies.start(own_ref.at[pl.ds(at * cut, cut)], block_ref.at[at]) for at in range(CHUNKS)]
        leaving = [copies.start(energy_ref, ref.at[pl.ds(cut, SUBLANES)]) for ref in sent_refs]
        for at in range(CHUNKS):
            coming[at].wait()
            if at:
                leaving.append(copies.start(block_ref.at[at], sent_refs[at - 1].at[pl.ds(0, cut)]))
            block = rows_of(block_ref.at[at], 0, size, width)
            high, low = split(block.T)
            turned_ref[0, at] = high
            turned_ref[1, at] = low
            leaving.append(copies.start(turned_ref.at[0, at], high_out.at[at]))
            leaving.append(copies.start(turned_ref.at[1, at], low_out.at[at]))
            value = dot(jnp.concatenate([high, low, high], axis=1), deep_right(block))
            integrals_ref[...] = integrals_ref[...] + value if at else value
        for at, out_ref in enumerate(integral_outs):
            leaving.append(copies.start(integrals_ref.at[pl.ds(at * share, share)], out_ref))
        for copy in leaving:
            copy.wait()

    turned = jax.ShapeDtypeStruct((CHUNKS, width, size), jnp.bfloat16)
    square = jax.ShapeDtypeStruct((share, width), jnp.float32)
    sent = jax.ShapeDtypeStruct((cut + SUBLANES, LANES), jnp.float32)
    scratch = [
        pltpu.VMEM((CHUNKS, cut, LANES), jnp.float32),
        pltpu.VMEM((2, CHUNKS, width, size), jnp.bfloat16),
        pltpu.VMEM((width, width), jnp.float32),
        pltpu.SemaphoreType.DMA((5 * CHUNKS + HALVES,)),
    ]
    outs = [turned, turned] + [square] * HALVES + [sent] * (CHUNKS - 1)
    return call(kernel, [], [energies], [own], outs, pl.ANY, scratch)


def arrays_of(pieces):
    return distinct([array for piece in pieces for array, _ in piece.places])


def integrate(turned, slots, first, flags, size, width, before=(), limit=VMEM_LIMIT):
    cut = size * width // LANES
    count = len(slots)
    pieces = [piece for slot in slots for piece in slot]
    arrays = arrays_of(pieces)
    numbers = [list(range(start, start + len(slot))) for slot, start in zip(slots, first)]
    needed = sorted({number for some in numbers for number in some})
    before = [part for parts in before for part in parts]
    share = width // HALVES

    def kernel(flag_ref, *refs):
        given = iter(refs)
        high_ref, low_ref = next(given), next(given)
        before_refs = [next(given) for _ in before]
        ref_of = {id(array): next(given) for array in arrays}
        outs = [[next(given) for _ in range(HALVES)] for _ in range(count)]
        turned_ref, block_ref, before_ref, semaphores = given
        copies = Copies(semaphores)
        coming, turning = [], {}

        def turn(number):
            if number not in turning:
                at = needed.index(number)
                turning[number] = [
                    copies.start(high_ref.at[number], turned_ref.at[at, 0]),
                    copies.start(low_ref.at[number], turned_ref.at[at, 1]),
                ]

        at = 0
        for slot in range(count):
            for number, piece in zip(numbers[slot], slots[slot]):
                turn(number)
                coming.append(copies.start_piece(piece, ref_of, flag_ref, cut, block_ref.at[at]))
                at += 1
        adding = [
            copies.start(ref, before_ref.at[at // HALVES, pl.ds(at % HALVES * share, share)])
            for at, ref in enumerate(before_refs)
        ]
        at = 0
        for slot in range(count):
            total = None
            for place, number in enumerate(numbers[slot]):
                for copy in turning.pop(number, []):
                    copy.wait()
                coming[at].wait()
                there = needed.index(number)
                high, low = turned_ref[there, 0], turned_ref[there, 1]
                left = jnp.concatenate([high, low, high], axis=1)
                value = dot(left, deep_right(rows_of(block_ref.at[at], 0, size, width)))
                total = total + value if place else value
                at += 1
            if before:
                for number in range(HALVES):
                    adding[slot * HALVES + number].wait()
                total = total + before_ref[slot]
            for number, out_ref in enumerate(outs[slot]):
                out_ref[...] = total[number * share : (number + 1) * share]

    out = [jax.ShapeDtypeStruct((share, width), jnp.float32)] * (HALVES * count)
    scratch = [
        pltpu.VMEM((len(needed), 2, width, size), jnp.bfloat16),
        pltpu.VMEM((len(pieces), cut, LANES), jnp.float32),
        pltpu.VMEM((max(len(before) // HALVES, 1), width, width), jnp.float32),
        pltpu.SemaphoreType.DMA((2 * len(needed) + len(pieces) + len(before),)),
    ]
    made = call(kernel, [flags], [], [*turned, *before, *arrays], out, pltpu.VMEM, scratch, limit)
    return [made[slot * HALVES : (slot + 1) * HALVES] for slot in range(count)]


def contract(partials, slots, signs, first_sign, energies, flags, eps_virt, size, before=None, limit=VMEM_LIMIT):
    count = len(slots)
    chunks = len(slots[0])
    virt = eps_virt.shape[1]
    width = partials[0][0][0].shape[1]
    share = width // HALVES
    occ_rows = width // virt
    lines = width // LANES
    cut = size * lines
    sums = [part for slot in partials for term in slot for part in term]
    pieces = [piece for slot in slots for piece in slot]
    arrays = arrays_of([*pieces, *energies])
    last = [before] if before is not None else []

    def kernel(*refs):
        given = iter(refs)
        sign_ref, flag_ref, virt_ref = next(given), next(given), next(given)
        sum_refs = [next(given) for _ in sums]
        before_refs = [next(given) for _ in last]
        ref_of = {id(array): next(given) for array in arrays}
        out_ref, energy_ref, sum_ref, block_ref, result_ref, right_ref, semaphores = given
        copies = Copies(semaphores)
        arriving = [
            copies.start_piece(piece, ref_of, flag_ref, SUBLANES, energy_ref.at[at])
            for at, piece in enumerate(energies)
        ]
        arriving += [
            copies.start(ref, sum_ref.at[at // HALVES, pl.ds(at % HALVES * share, share)])
            for at, ref in enumerate(sum_refs)
        ]
        coming = [
            [
                copies.start_piece(slots[slot][at], ref_of, flag_ref, cut, block_ref.at[slot, at])
                for slot in range(count)
            ]
            for at in range(chunks)
        ]
        adding = [
            [copies.start(ref.at[pl.ds(at * cut, cut)], result_ref.at[at]) for ref in before_refs]
            for at in range(chunks)
        ]
        for copy in arriving:
            copy.wait()

        def line(at):
            virtual = virt_ref[...]
            energy = energy_ref[at]
            return jnp.concatenate([virtual - energy[:1, i : i + 1] for i in range(occ_rows)], axis=1)

        row = jnp.broadcast_to(line(0), (SUBLANES, width)).T[:, :1]
        at = 0
        for slot in range(count):
            total = sum_ref[at]
            for extra in range(1, len(partials[slot])):
                total = total + sum_ref[at + extra]
            at += len(partials[slot])
            amplitude = (sign_ref[first_sign + slot] * total) / (row + line(slot + 1))
            right_ref[:, pl.ds(slot * 3 * width, 3 * width)] = deep_right(amplitude, 1)
        leaving = []
        for at in range(chunks):
            for copy in coming[at] + adding[at]:
                copy.wait()
            left = [deep_left(rows_of(block_ref.at[slot, at], 0, size, width)) for slot in range(count)]
            value = dot(jnp.concatenate(left, axis=1), right_ref[...], 1)
            for column in range(lines):
                lanes = value[:, column * LANES : (column + 1) * LANES]
                where = pl.ds(column, size, stride=lines)
                if last:
                    lanes = lanes + result_ref[at, where, :]
                result_ref[at, where, :] = lanes
            leaving.append(copies.start(result_ref.at[at], out_ref.at[pl.ds(at * cut, cut)]))
        for copy in leaving:
            copy.wait()

    rows = chunks * size
    out = jax.ShapeDtypeStruct((rows * lines, LANES), jnp.float32)
    scratch = [
        pltpu.VMEM((len(energies), SUBLANES, LANES), jnp.float32),
        pltpu.VMEM((len(sums) // HALVES, width, width), jnp.float32),
        pltpu.VMEM((count, chunks, cut, LANES), jnp.float32),
        pltpu.VMEM((chunks, cut, LANES), jnp.float32),
        pltpu.VMEM((width, count * 3 * width), jnp.bfloat16),
        pltpu.SemaphoreType.DMA((len(energies) + len(sums) + len(pieces) + 2 * chunks,)),
    ]
    return call(kernel, [signs, flags], [eps_virt], [*sums, *last, *arrays], [out], pl.ANY, scratch, limit)[0]


def after(block, *others):
    return lax.optimization_barrier((block, *others))[0]


def on_device(factors, eps_occ, eps_virt, pair_mask):
    rows, occ_rows, virt = factors.shape
    width = occ_rows * virt
    lines = width // LANES
    groups = lax.axis_size("occ")
    shares = lax.axis_size("aux")
    size = rows // CHUNKS
    cut = size * lines
    last = CHUNKS - 1
    group = lax.axis_index("occ")
    place = group % PLANE
    odd_x = place % 2 == 1
    odd_y = place // 2 == 1

    own = factors.reshape(rows * lines, LANES)
    energies = jnp.zeros((SUBLANES * LANES,), jnp.float32).at[:occ_rows].set(eps_occ)
    energies = energies.reshape(SUBLANES, LANES)

    def part(whole, at):
        return whole[at * cut : (at + 1) * cut]

    def within(block, moves):
        planes = range(0, groups, PLANE)
        return lax.ppermute(block, "occ", [(g + a, g + b) for g in planes for a, b in moves])

    def up(block):
        return lax.ppermute(block, "occ", [(g, g + PLANE) for g in range(groups - PLANE)])

    def totals(parts):
        if shares == 2:
            return [parts, [lax.ppermute(part, "aux", [(0, 1), (1, 0)]) for part in parts]]
        return [[lax.psum(part, "aux") for part in parts]]

    first_sent = jnp.concatenate([part(own, 0), energies])
    def choices(sent):
        group_then, mask_row, _ = lax.optimization_barrier((group, pair_mask[0], sent))
        place_then = group_then % PLANE

        def sign(offset):
            flag = jnp.sum(jnp.where(jnp.arange(1, PLANE + 1) == offset, mask_row, 0))
            return jnp.where((group_then >= offset) & (flag > 0), -1.0, 0.0).astype(jnp.float32)

        near = jnp.where(place_then % 2 == 1, 1, PLANE - 1)
        signs = [jnp.float32(-1.0), sign(PLANE), sign(near), sign(PLANE // 2), sign(PLANE - near)]
        up_then = place_then // 2 == 1
        flags = [
            1 - place_then % 2,
            1 - place_then // 2,
            jnp.where(up_then, 0, 1 + place_then),
            jnp.where(up_then, place_then - 1, 0),
        ]
        return jnp.stack(signs), jnp.stack(flags).astype(jnp.int32)

    def add(first_sign, partials, slots, carriers, before=None, limit=VMEM_LIMIT):
        return contract(
            partials, slots, signs, first_sign, carriers, flags, eps_virt[None, :], size, before, limit
        )

    from_own = [first_sent]
    from_z = [up(first_sent)]
    up_x = within(first_sent, [(0, 1), (2, 3), (1, 0)])
    up_y = within(first_sent, [(0, 2), (1, 3)])
    high, low, *made = prepare(own, energies, rows, width)
    partial_own = made[:HALVES]
    from_own += made[HALVES:]
    turned = (high, low)
    sums_own = totals(partial_own)
    swap_x, swap_y = [], []
    passed = [partial_own[0]]
    for at in range(CHUNKS):
        came = after(from_z[at], *passed)
        if at < last:
            from_z.append(up(after(from_own[at + 1], came)))
            up_part = after(from_own[at + 1], came)
            send_x, send_y = jnp.where(odd_x, came, up_part), jnp.where(odd_y, came, up_part)
            send_x = after(send_x, swap_x[at - 1] if at else up_x)
            send_y = after(send_y, swap_y[at - 1] if at else up_y)
            if at == 0:
                signs, flags = choices((send_x, send_y))
            swap_x.append(within(send_x, [(0, 1), (1, 0), (2, 3), (3, 2)]))
            swap_y.append(within(send_y, [(0, 2), (2, 0), (1, 3), (3, 1)]))
        else:
            cycle = within(after(turning, came, swap_x[last - 1]), [(0, 1), (1, 3), (3, 2), (2, 0)])
            send_x = after(jnp.where(odd_x, came, swap_y[0]), swap_x[last - 1])
            send_y = after(jnp.where(odd_y, came, up_x), swap_y[last - 1])
            swap_x.append(within(send_x, [(0, 1), (1, 0), (2, 3), (3, 2)]))
            swap_y.append(within(send_y, [(0, 2), (2, 0), (1, 3), (3, 1)]))
        passed = []
        if at == 1:
            passed = [signs, flags]
            middle = (place == 1) | (place == 2)
            turning = jnp.where(middle, swap_x[1], swap_y[1])
        if at == 2:
            passed.append(turning)

    cross = within(jnp.where(place == 2, swap_x[0], swap_y[0]), [(2, 0), (3, 2)])
    swap_d = within(swap_y[2], [(0, 1), (1, 0), (2, 3), (3, 2)])
    last_d = within(swap_y[3], [(0, 1), (1, 0)])

    def pieces_of(first, swaps, choice, base):
        arrays = [first, *swaps]
        return [Piece(((arrays[at], base), (arrays[at + 1], base)), choice) for at in range(CHUNKS)]

    def whole(array, base):
        return Piece(((array, base),))

    slot_own = [whole(own, at * cut) for at in range(CHUNKS)]
    slot_z = [whole(block, 0) for block in from_z]
    slot_x = pieces_of(up_x, swap_x, 0, 0)
    slot_y = pieces_of(up_y, swap_y, 1, 0)
    slot_d = [
        Piece(((swap_y[last], 0), (cross, 0), (swap_x[last], 0)), 2),
        Piece(((cycle, 0), (cross, 0), (swap_x[last], 0)), 3),
        Piece(((cycle, 0), (swap_d, 0)), 1),
        Piece(((swap_d, 0), (last_d, 0)), 1),
    ]
    eps_x = pieces_of(up_x, swap_x, 0, cut)[0]
    eps_y = pieces_of(up_y, swap_y, 1, cut)[0]
    eps_d = Piece(((swap_y[last], cut), (cross, cut), (swap_x[last], cut)), 2)

    partial_z, *early = integrate(
        turned, [slot_z, slot_x[:last], slot_y[:last]], [0, 0, 0], flags, size, width
    )
    own_eps = whole(first_sent, cut)
    partial_x, partial_y = integrate(
        turned, [slot_x[last:], slot_y[last:]], [last, last], flags, size, width, early
    )
    gradient = add(
        0,
        [after(sums_own, cycle), totals(partial_z), totals(partial_x), totals(partial_y)],
        [slot_own, slot_z, slot_x, slot_y],
        [own_eps, own_eps, whole(from_z[0], cut), eps_x, eps_y],
    )
    turned = after(turned, gradient)
    half = CHUNKS // 2
    partial_d = integrate(turned, [slot_d[:half]], [0], flags, size, width)
    (partial_d,) = integrate(turned, [slot_d[half:]], [half], flags, size, width, partial_d, LAST_LIMIT)
    gradient = add(4, [totals(partial_d)], [slot_d], [own_eps, eps_d], gradient, LAST_LIMIT)
    return gradient.reshape(rows, occ_rows, virt)


def solution(mesh):
    if mesh.shape["occ"] % PLANE:
        raise ValueError("incomplete plane")
    in_specs = (P("aux", "occ", None), P("occ"), P(), P("occ", None))
    out_specs = P("aux", "occ", None)
    return jax.shard_map(
        on_device, mesh=mesh, in_specs=in_specs, out_specs=out_specs, check_vma=False
    )
```

```python
import dataclasses
import functools

import jax
import jax.numpy as jnp
from jax import lax
from jax.experimental import pallas as pl
from jax.experimental.pallas import tpu as pltpu
from jax.sharding import PartitionSpec as P

LANES = 128
SUBLANES = 8
PLANE = 4
CHUNKS = 4
VMEM_LIMIT = 32 * 1024 * 1024
FIRST_LIMIT = 60 * 1024 * 1024
LAST_LIMIT = 24 * 1024 * 1024
HALVES = 2


def split(value):
    high = value.astype(jnp.bfloat16)
    low = (value - high.astype(jnp.float32)).astype(jnp.bfloat16)
    return high, low


def deep_left(value):
    high, low = split(value)
    return jnp.concatenate([high, low, high], axis=1)


def deep_right(value, axis=0):
    high, low = split(value)
    return jnp.concatenate([high, high, low], axis=axis)


def dot(left, right, axis=0):
    numbers = (((1,), (axis,)), ((), ()))
    return lax.dot_general(left, right, numbers, preferred_element_type=jnp.float32)


def rows_of(ref, start, count, width):
    lines = width // LANES
    columns = [ref[pl.ds(start * lines + at, count, stride=lines), :] for at in range(lines)]
    return jnp.concatenate(columns, axis=1)


def distinct(arrays):
    return list({id(array): array for array in arrays}.values())


class Copies:
    def __init__(self, semaphores):
        self.semaphores = semaphores
        self.used = 0

    def start(self, source, target):
        copy = pltpu.make_async_copy(source, target, self.semaphores.at[self.used])
        self.used += 1
        copy.start()
        return copy

    def start_piece(self, piece, ref_of, choices, count, target):
        made = []
        for array, base in piece.places:
            source = ref_of[id(array)].at[pl.ds(base, count)]
            made.append(pltpu.make_async_copy(source, target, self.semaphores.at[self.used]))
        self.used += 1
        if len(made) == 1:
            made[0].start()
        else:
            for at, copy in enumerate(made):
                pl.when(choices[piece.choice] == at)(copy.start)
        return made[0]


@dataclasses.dataclass(frozen=True)
class Piece:
    places: tuple
    choice: int = 0


def call(kernel, smem, vmem, anywhere, outputs, out_space, scratch, limit=VMEM_LIMIT):
    spaces = [pltpu.SMEM] * len(smem) + [pltpu.VMEM] * len(vmem) + [pl.ANY] * len(anywhere)
    return pl.pallas_call(
        kernel,
        out_shape=outputs,
        in_specs=[pl.BlockSpec(memory_space=space) for space in spaces],
        out_specs=[pl.BlockSpec(memory_space=out_space)] * len(outputs),
        scratch_shapes=scratch,
        compiler_params=pltpu.CompilerParams(vmem_limit_bytes=limit),
        cost_estimate=pl.CostEstimate(flops=0, bytes_accessed=0, transcendentals=0),
    )(*smem, *vmem, *anywhere)


def prepare(own, energies, rows, width):
    size = rows // CHUNKS
    cut = size * width // LANES
    share = width // HALVES

    def kernel(energy_ref, own_ref, high_out, low_out, *refs):
        integral_outs, refs = refs[:HALVES], refs[HALVES:]
        sent_refs = refs[: CHUNKS - 1]
        block_ref, turned_ref, integrals_ref, semaphores = refs[CHUNKS - 1 :]
        copies = Copies(semaphores)
        coming = [copies.start(own_ref.at[pl.ds(at * cut, cut)], block_ref.at[at]) for at in range(CHUNKS)]
        leaving = [copies.start(energy_ref, ref.at[pl.ds(cut, SUBLANES)]) for ref in sent_refs]
        for at in range(CHUNKS):
            coming[at].wait()
            if at:
                leaving.append(copies.start(block_ref.at[at], sent_refs[at - 1].at[pl.ds(0, cut)]))
            block = rows_of(block_ref.at[at], 0, size, width)
            high, low = split(block.T)
            turned_ref[0, at] = high
            turned_ref[1, at] = low
            leaving.append(copies.start(turned_ref.at[0, at], high_out.at[at]))
            leaving.append(copies.start(turned_ref.at[1, at], low_out.at[at]))
            value = dot(jnp.concatenate([high, low, high], axis=1), deep_right(block))
            integrals_ref[...] = integrals_ref[...] + value if at else value
        for at, out_ref in enumerate(integral_outs):
            leaving.append(copies.start(integrals_ref.at[pl.ds(at * share, share)], out_ref))
        for copy in leaving:
            copy.wait()

    turned = jax.ShapeDtypeStruct((CHUNKS, width, size), jnp.bfloat16)
    square = jax.ShapeDtypeStruct((share, width), jnp.float32)
    sent = jax.ShapeDtypeStruct((cut + SUBLANES, LANES), jnp.float32)
    scratch = [
        pltpu.VMEM((CHUNKS, cut, LANES), jnp.float32),
        pltpu.VMEM((2, CHUNKS, width, size), jnp.bfloat16),
        pltpu.VMEM((width, width), jnp.float32),
        pltpu.SemaphoreType.DMA((5 * CHUNKS + HALVES,)),
    ]
    outs = [turned, turned] + [square] * HALVES + [sent] * (CHUNKS - 1)
    return call(kernel, [], [energies], [own], outs, pl.ANY, scratch, FIRST_LIMIT)


def arrays_of(pieces):
    return distinct([array for piece in pieces for array, _ in piece.places])


def integrate(turned, slots, first, flags, size, width, before=(), limit=VMEM_LIMIT):
    cut = size * width // LANES
    count = len(slots)
    pieces = [piece for slot in slots for piece in slot]
    arrays = arrays_of(pieces)
    numbers = [list(range(start, start + len(slot))) for slot, start in zip(slots, first)]
    needed = sorted({number for some in numbers for number in some})
    before = [part for parts in before for part in parts]
    share = width // HALVES

    def kernel(flag_ref, *refs):
        given = iter(refs)
        high_ref, low_ref = next(given), next(given)
        before_refs = [next(given) for _ in before]
        ref_of = {id(array): next(given) for array in arrays}
        outs = [[next(given) for _ in range(HALVES)] for _ in range(count)]
        turned_ref, block_ref, before_ref, semaphores = given
        copies = Copies(semaphores)
        coming, turning = [], {}

        def turn(number):
            if number not in turning:
                at = needed.index(number)
                turning[number] = [
                    copies.start(high_ref.at[number], turned_ref.at[at, 0]),
                    copies.start(low_ref.at[number], turned_ref.at[at, 1]),
                ]

        at = 0
        for slot in range(count):
            for number, piece in zip(numbers[slot], slots[slot]):
                turn(number)
                coming.append(copies.start_piece(piece, ref_of, flag_ref, cut, block_ref.at[at]))
                at += 1
        adding = [
            copies.start(ref, before_ref.at[at // HALVES, pl.ds(at % HALVES * share, share)])
            for at, ref in enumerate(before_refs)
        ]
        at = 0
        for slot in range(count):
            total = None
            for place, number in enumerate(numbers[slot]):
                for copy in turning.pop(number, []):
                    copy.wait()
                coming[at].wait()
                there = needed.index(number)
                high, low = turned_ref[there, 0], turned_ref[there, 1]
                left = jnp.concatenate([high, low, high], axis=1)
                value = dot(left, deep_right(rows_of(block_ref.at[at], 0, size, width)))
                total = total + value if place else value
                at += 1
            if before:
                for number in range(HALVES):
                    adding[slot * HALVES + number].wait()
                total = total + before_ref[slot]
            for number, out_ref in enumerate(outs[slot]):
                out_ref[...] = total[number * share : (number + 1) * share]

    out = [jax.ShapeDtypeStruct((share, width), jnp.float32)] * (HALVES * count)
    scratch = [
        pltpu.VMEM((len(needed), 2, width, size), jnp.bfloat16),
        pltpu.VMEM((len(pieces), cut, LANES), jnp.float32),
        pltpu.VMEM((max(len(before) // HALVES, 1), width, width), jnp.float32),
        pltpu.SemaphoreType.DMA((2 * len(needed) + len(pieces) + len(before),)),
    ]
    made = call(kernel, [flags], [], [*turned, *before, *arrays], out, pltpu.VMEM, scratch, limit)
    return [made[slot * HALVES : (slot + 1) * HALVES] for slot in range(count)]


def contract(partials, slots, signs, first_sign, energies, flags, eps_virt, size, before=None, limit=VMEM_LIMIT):
    count = len(slots)
    chunks = len(slots[0])
    virt = eps_virt.shape[1]
    width = partials[0][0][0].shape[1]
    share = width // HALVES
    occ_rows = width // virt
    lines = width // LANES
    cut = size * lines
    sums = [part for slot in partials for term in slot for part in term]
    pieces = [piece for slot in slots for piece in slot]
    arrays = arrays_of([*pieces, *energies])
    last = [before] if before is not None else []

    def kernel(*refs):
        given = iter(refs)
        sign_ref, flag_ref, virt_ref = next(given), next(given), next(given)
        sum_refs = [next(given) for _ in sums]
        before_refs = [next(given) for _ in last]
        ref_of = {id(array): next(given) for array in arrays}
        out_ref, energy_ref, sum_ref, block_ref, result_ref, right_ref, semaphores = given
        copies = Copies(semaphores)
        arriving = [
            copies.start_piece(piece, ref_of, flag_ref, SUBLANES, energy_ref.at[at])
            for at, piece in enumerate(energies)
        ]
        arriving += [
            copies.start(ref, sum_ref.at[at // HALVES, pl.ds(at % HALVES * share, share)])
            for at, ref in enumerate(sum_refs)
        ]
        coming = [
            [
                copies.start_piece(slots[slot][at], ref_of, flag_ref, cut, block_ref.at[slot, at])
                for slot in range(count)
            ]
            for at in range(chunks)
        ]
        adding = [
            [copies.start(ref.at[pl.ds(at * cut, cut)], result_ref.at[at]) for ref in before_refs]
            for at in range(chunks)
        ]
        for copy in arriving:
            copy.wait()

        def line(at):
            virtual = virt_ref[...]
            energy = energy_ref[at]
            return jnp.concatenate([virtual - energy[:1, i : i + 1] for i in range(occ_rows)], axis=1)

        row = jnp.broadcast_to(line(0), (SUBLANES, width)).T[:, :1]
        at = 0
        for slot in range(count):
            total = sum_ref[at]
            for extra in range(1, len(partials[slot])):
                total = total + sum_ref[at + extra]
            at += len(partials[slot])
            amplitude = (sign_ref[first_sign + slot] * total) / (row + line(slot + 1))
            right_ref[:, pl.ds(slot * 3 * width, 3 * width)] = deep_right(amplitude, 1)
        leaving = []
        for at in range(chunks):
            for copy in coming[at] + adding[at]:
                copy.wait()
            left = [deep_left(rows_of(block_ref.at[slot, at], 0, size, width)) for slot in range(count)]
            value = dot(jnp.concatenate(left, axis=1), right_ref[...], 1)
            for column in range(lines):
                lanes = value[:, column * LANES : (column + 1) * LANES]
                where = pl.ds(column, size, stride=lines)
                if last:
                    lanes = lanes + result_ref[at, where, :]
                result_ref[at, where, :] = lanes
            leaving.append(copies.start(result_ref.at[at], out_ref.at[pl.ds(at * cut, cut)]))
        for copy in leaving:
            copy.wait()

    rows = chunks * size
    out = jax.ShapeDtypeStruct((rows * lines, LANES), jnp.float32)
    scratch = [
        pltpu.VMEM((len(energies), SUBLANES, LANES), jnp.float32),
        pltpu.VMEM((len(sums) // HALVES, width, width), jnp.float32),
        pltpu.VMEM((count, chunks, cut, LANES), jnp.float32),
        pltpu.VMEM((chunks, cut, LANES), jnp.float32),
        pltpu.VMEM((width, count * 3 * width), jnp.bfloat16),
        pltpu.SemaphoreType.DMA((len(energies) + len(sums) + len(pieces) + 2 * chunks,)),
    ]
    return call(kernel, [signs, flags], [eps_virt], [*sums, *last, *arrays], [out], pl.ANY, scratch, limit)[0]


def after(block, *others):
    return lax.optimization_barrier((block, *others))[0]


def on_device(factors, eps_occ, eps_virt, pair_mask):
    rows, occ_rows, virt = factors.shape
    width = occ_rows * virt
    lines = width // LANES
    groups = lax.axis_size("occ")
    shares = lax.axis_size("aux")
    size = rows // CHUNKS
    cut = size * lines
    last = CHUNKS - 1
    group = lax.axis_index("occ")
    place = group % PLANE
    odd_x = place % 2 == 1
    odd_y = place // 2 == 1

    own = factors.reshape(rows * lines, LANES)
    energies = jnp.zeros((SUBLANES * LANES,), jnp.float32).at[:occ_rows].set(eps_occ)
    energies = energies.reshape(SUBLANES, LANES)

    def part(whole, at):
        return whole[at * cut : (at + 1) * cut]

    def within(block, moves):
        planes = range(0, groups, PLANE)
        return lax.ppermute(block, "occ", [(g + a, g + b) for g in planes for a, b in moves])

    def up(block):
        return lax.ppermute(block, "occ", [(g, g + PLANE) for g in range(groups - PLANE)])

    def totals(parts):
        if shares == 2:
            return [parts, [lax.ppermute(part, "aux", [(0, 1), (1, 0)]) for part in parts]]
        return [[lax.psum(part, "aux") for part in parts]]

    first_sent = jnp.concatenate([part(own, 0), energies])
    def choices(sent):
        group_then, mask_row, _ = lax.optimization_barrier((group, pair_mask[0], sent))
        place_then = group_then % PLANE

        def sign(offset):
            flag = jnp.sum(jnp.where(jnp.arange(1, PLANE + 1) == offset, mask_row, 0))
            return jnp.where((group_then >= offset) & (flag > 0), -1.0, 0.0).astype(jnp.float32)

        near = jnp.where(place_then % 2 == 1, 1, PLANE - 1)
        signs = [jnp.float32(-1.0), sign(PLANE), sign(near), sign(PLANE // 2), sign(PLANE - near)]
        up_then = place_then // 2 == 1
        flags = [
            1 - place_then % 2,
            1 - place_then // 2,
            jnp.where(up_then, 0, 1 + place_then),
            jnp.where(up_then, place_then - 1, 0),
        ]
        return jnp.stack(signs), jnp.stack(flags).astype(jnp.int32)

    def add(first_sign, partials, slots, carriers, before=None, limit=VMEM_LIMIT):
        return contract(
            partials, slots, signs, first_sign, carriers, flags, eps_virt[None, :], size, before, limit
        )

    from_own = [first_sent]
    from_z = [up(first_sent)]
    up_x = within(first_sent, [(0, 1), (2, 3), (1, 0)])
    up_y = within(first_sent, [(0, 2), (1, 3)])
    high, low, *made = prepare(own, energies, rows, width)
    partial_own = made[:HALVES]
    from_own += made[HALVES:]
    turned = (high, low)
    sums_own = totals(partial_own)
    swap_x, swap_y = [], []
    passed = [partial_own[0]]
    for at in range(CHUNKS):
        came = after(from_z[at], *passed)
        if at < last:
            from_z.append(up(after(from_own[at + 1], came)))
            up_part = after(from_own[at + 1], came)
            send_x, send_y = jnp.where(odd_x, came, up_part), jnp.where(odd_y, came, up_part)
            send_x = after(send_x, swap_x[at - 1] if at else up_x)
            send_y = after(send_y, swap_y[at - 1] if at else up_y)
            if at == 0:
                signs, flags = choices((send_x, send_y))
            swap_x.append(within(send_x, [(0, 1), (1, 0), (2, 3), (3, 2)]))
            swap_y.append(within(send_y, [(0, 2), (2, 0), (1, 3), (3, 1)]))
        else:
            cycle = within(after(turning, came, swap_x[last - 1]), [(0, 1), (1, 3), (3, 2), (2, 0)])
            send_x = after(jnp.where(odd_x, came, swap_y[0]), swap_x[last - 1])
            send_y = after(jnp.where(odd_y, came, up_x), swap_y[last - 1])
            swap_x.append(within(send_x, [(0, 1), (1, 0), (2, 3), (3, 2)]))
            swap_y.append(within(send_y, [(0, 2), (2, 0), (1, 3), (3, 1)]))
        passed = []
        if at == 1:
            passed = [signs, flags]
            middle = (place == 1) | (place == 2)
            turning = jnp.where(middle, swap_x[1], swap_y[1])
        if at == 2:
            passed.append(turning)

    cross = within(jnp.where(place == 2, swap_x[0], swap_y[0]), [(2, 0), (3, 2)])
    swap_d = within(swap_y[2], [(0, 1), (1, 0), (2, 3), (3, 2)])
    last_d = within(swap_y[3], [(0, 1), (1, 0)])

    def pieces_of(first, swaps, choice, base):
        arrays = [first, *swaps]
        return [Piece(((arrays[at], base), (arrays[at + 1], base)), choice) for at in range(CHUNKS)]

    def whole(array, base):
        return Piece(((array, base),))

    slot_own = [whole(own, at * cut) for at in range(CHUNKS)]
    slot_z = [whole(block, 0) for block in from_z]
    slot_x = pieces_of(up_x, swap_x, 0, 0)
    slot_y = pieces_of(up_y, swap_y, 1, 0)
    slot_d = [
        Piece(((swap_y[last], 0), (cross, 0), (swap_x[last], 0)), 2),
        Piece(((cycle, 0), (cross, 0), (swap_x[last], 0)), 3),
        Piece(((cycle, 0), (swap_d, 0)), 1),
        Piece(((swap_d, 0), (last_d, 0)), 1),
    ]
    eps_x = pieces_of(up_x, swap_x, 0, cut)[0]
    eps_y = pieces_of(up_y, swap_y, 1, cut)[0]
    eps_d = Piece(((swap_y[last], cut), (cross, cut), (swap_x[last], cut)), 2)

    partial_z, *early = integrate(
        turned, [slot_z, slot_x[:last], slot_y[:last]], [0, 0, 0], flags, size, width
    )
    own_eps = whole(first_sent, cut)
    partial_x, partial_y = integrate(
        turned, [slot_x[last:], slot_y[last:]], [last, last], flags, size, width, early
    )
    gradient = add(
        0,
        [after(sums_own, cycle), totals(partial_z), totals(partial_x), totals(partial_y)],
        [slot_own, slot_z, slot_x, slot_y],
        [own_eps, own_eps, whole(from_z[0], cut), eps_x, eps_y],
    )
    turned = after(turned, gradient)
    half = CHUNKS // 2
    partial_d = integrate(turned, [slot_d[:half]], [0], flags, size, width)
    (partial_d,) = integrate(turned, [slot_d[half:]], [half], flags, size, width, partial_d, LAST_LIMIT)
    gradient = add(4, [totals(partial_d)], [slot_d], [own_eps, eps_d], gradient, LAST_LIMIT)
    return gradient.reshape(rows, occ_rows, virt)


def solution(mesh):
    if mesh.shape["occ"] % PLANE:
        raise ValueError("incomplete plane")
    in_specs = (P("aux", "occ", None), P("occ"), P(), P("occ", None))
    out_specs = P("aux", "occ", None)
    return jax.shard_map(
        on_device, mesh=mesh, in_specs=in_specs, out_specs=out_specs, check_vma=False
    )
```

```python
import dataclasses
import functools

import jax
import jax.numpy as jnp
from jax import lax
from jax.experimental import pallas as pl
from jax.experimental.pallas import tpu as pltpu
from jax.sharding import PartitionSpec as P

LANES = 128
SUBLANES = 8
PLANE = 4
CHUNKS = 4
VMEM_LIMIT = 32 * 1024 * 1024
FIRST_LIMIT = 60 * 1024 * 1024
LAST_LIMIT = 24 * 1024 * 1024
HALVES = 2


def split(value):
    high = value.astype(jnp.bfloat16)
    low = (value - high.astype(jnp.float32)).astype(jnp.bfloat16)
    return high, low


def deep_left(value):
    high, low = split(value)
    return jnp.concatenate([high, low, high], axis=1)


def deep_right(value, axis=0):
    high, low = split(value)
    return jnp.concatenate([high, high, low], axis=axis)


def dot(left, right, axis=0):
    numbers = (((1,), (axis,)), ((), ()))
    return lax.dot_general(left, right, numbers, preferred_element_type=jnp.float32)


def rows_of(ref, start, count, width):
    lines = width // LANES
    columns = [ref[pl.ds(start * lines + at, count, stride=lines), :] for at in range(lines)]
    return jnp.concatenate(columns, axis=1)


def distinct(arrays):
    return list({id(array): array for array in arrays}.values())


class Copies:
    def __init__(self, semaphores):
        self.semaphores = semaphores
        self.used = 0

    def start(self, source, target):
        copy = pltpu.make_async_copy(source, target, self.semaphores.at[self.used])
        self.used += 1
        copy.start()
        return copy

    def start_piece(self, piece, ref_of, choices, count, target):
        made = []
        for array, base in piece.places:
            source = ref_of[id(array)].at[pl.ds(base, count)]
            made.append(pltpu.make_async_copy(source, target, self.semaphores.at[self.used]))
        self.used += 1
        if len(made) == 1:
            made[0].start()
        else:
            for at, copy in enumerate(made):
                pl.when(choices[piece.choice] == at)(copy.start)
        return made[0]


@dataclasses.dataclass(frozen=True)
class Piece:
    places: tuple
    choice: int = 0


def call(kernel, smem, vmem, anywhere, outputs, out_space, scratch, limit=VMEM_LIMIT):
    spaces = [pltpu.SMEM] * len(smem) + [pltpu.VMEM] * len(vmem) + [pl.ANY] * len(anywhere)
    return pl.pallas_call(
        kernel,
        out_shape=outputs,
        in_specs=[pl.BlockSpec(memory_space=space) for space in spaces],
        out_specs=[pl.BlockSpec(memory_space=out_space)] * len(outputs),
        scratch_shapes=scratch,
        compiler_params=pltpu.CompilerParams(vmem_limit_bytes=limit),
        cost_estimate=pl.CostEstimate(flops=0, bytes_accessed=0, transcendentals=0),
    )(*smem, *vmem, *anywhere)


def prepare(own, energies, rows, width):
    size = rows // CHUNKS
    cut = size * width // LANES
    share = width // HALVES

    def kernel(energy_ref, own_ref, high_out, low_out, *refs):
        integral_outs, refs = refs[:HALVES], refs[HALVES:]
        sent_refs = refs[: CHUNKS - 1]
        block_ref, turned_ref, integrals_ref, semaphores = refs[CHUNKS - 1 :]
        copies = Copies(semaphores)
        coming = [copies.start(own_ref.at[pl.ds(at * cut, cut)], block_ref.at[at]) for at in range(CHUNKS)]
        leaving = [copies.start(energy_ref, ref.at[pl.ds(cut, SUBLANES)]) for ref in sent_refs]
        for at in range(CHUNKS):
            coming[at].wait()
            if at:
                leaving.append(copies.start(block_ref.at[at], sent_refs[at - 1].at[pl.ds(0, cut)]))
            block = rows_of(block_ref.at[at], 0, size, width)
            high, low = split(block.T)
            turned_ref[0, at] = high
            turned_ref[1, at] = low
            leaving.append(copies.start(turned_ref.at[0, at], high_out.at[at]))
            leaving.append(copies.start(turned_ref.at[1, at], low_out.at[at]))
            value = dot(jnp.concatenate([high, low, high], axis=1), deep_right(block))
            integrals_ref[...] = integrals_ref[...] + value if at else value
        for at, out_ref in enumerate(integral_outs):
            leaving.append(copies.start(integrals_ref.at[pl.ds(at * share, share)], out_ref))
        for copy in leaving:
            copy.wait()

    turned = jax.ShapeDtypeStruct((CHUNKS, width, size), jnp.bfloat16)
    square = jax.ShapeDtypeStruct((share, width), jnp.float32)
    sent = jax.ShapeDtypeStruct((cut + SUBLANES, LANES), jnp.float32)
    scratch = [
        pltpu.VMEM((CHUNKS, cut, LANES), jnp.float32),
        pltpu.VMEM((2, CHUNKS, width, size), jnp.bfloat16),
        pltpu.VMEM((width, width), jnp.float32),
        pltpu.SemaphoreType.DMA((5 * CHUNKS + HALVES,)),
    ]
    outs = [turned, turned] + [square] * HALVES + [sent] * (CHUNKS - 1)
    return call(kernel, [], [energies], [own], outs, pl.ANY, scratch, FIRST_LIMIT)


def arrays_of(pieces):
    return distinct([array for piece in pieces for array, _ in piece.places])


def integrate(turned, slots, first, flags, size, width, before=(), limit=VMEM_LIMIT):
    cut = size * width // LANES
    count = len(slots)
    pieces = [piece for slot in slots for piece in slot]
    arrays = arrays_of(pieces)
    numbers = [list(range(start, start + len(slot))) for slot, start in zip(slots, first)]
    needed = sorted({number for some in numbers for number in some})
    before = [part for parts in before for part in parts]
    share = width // HALVES

    def kernel(flag_ref, *refs):
        given = iter(refs)
        high_ref, low_ref = next(given), next(given)
        before_refs = [next(given) for _ in before]
        ref_of = {id(array): next(given) for array in arrays}
        outs = [[next(given) for _ in range(HALVES)] for _ in range(count)]
        turned_ref, block_ref, before_ref, semaphores = given
        copies = Copies(semaphores)
        coming, turning = [], {}

        def turn(number):
            if number not in turning:
                at = needed.index(number)
                turning[number] = [
                    copies.start(high_ref.at[number], turned_ref.at[at, 0]),
                    copies.start(low_ref.at[number], turned_ref.at[at, 1]),
                ]

        at = 0
        for slot in range(count):
            for number, piece in zip(numbers[slot], slots[slot]):
                turn(number)
                coming.append(copies.start_piece(piece, ref_of, flag_ref, cut, block_ref.at[at]))
                at += 1
        adding = [
            copies.start(ref, before_ref.at[at // HALVES, pl.ds(at % HALVES * share, share)])
            for at, ref in enumerate(before_refs)
        ]
        at = 0
        for slot in range(count):
            total = None
            for place, number in enumerate(numbers[slot]):
                for copy in turning.pop(number, []):
                    copy.wait()
                coming[at].wait()
                there = needed.index(number)
                high, low = turned_ref[there, 0], turned_ref[there, 1]
                left = jnp.concatenate([high, low, high], axis=1)
                value = dot(left, deep_right(rows_of(block_ref.at[at], 0, size, width)))
                total = total + value if place else value
                at += 1
            if before:
                for number in range(HALVES):
                    adding[slot * HALVES + number].wait()
                total = total + before_ref[slot]
            for number, out_ref in enumerate(outs[slot]):
                out_ref[...] = total[number * share : (number + 1) * share]

    out = [jax.ShapeDtypeStruct((share, width), jnp.float32)] * (HALVES * count)
    scratch = [
        pltpu.VMEM((len(needed), 2, width, size), jnp.bfloat16),
        pltpu.VMEM((len(pieces), cut, LANES), jnp.float32),
        pltpu.VMEM((max(len(before) // HALVES, 1), width, width), jnp.float32),
        pltpu.SemaphoreType.DMA((2 * len(needed) + len(pieces) + len(before),)),
    ]
    made = call(kernel, [flags], [], [*turned, *before, *arrays], out, pltpu.VMEM, scratch, limit)
    return [made[slot * HALVES : (slot + 1) * HALVES] for slot in range(count)]


def contract(partials, slots, signs, first_sign, energies, flags, eps_virt, size, before=None, limit=VMEM_LIMIT):
    count = len(slots)
    chunks = len(slots[0])
    virt = eps_virt.shape[1]
    width = partials[0][0][0].shape[1]
    share = width // HALVES
    occ_rows = width // virt
    lines = width // LANES
    cut = size * lines
    sums = [part for slot in partials for term in slot for part in term]
    pieces = [piece for slot in slots for piece in slot]
    arrays = arrays_of([*pieces, *energies])
    last = [before] if before is not None else []

    def kernel(*refs):
        given = iter(refs)
        sign_ref, flag_ref, virt_ref = next(given), next(given), next(given)
        sum_refs = [next(given) for _ in sums]
        before_refs = [next(given) for _ in last]
        ref_of = {id(array): next(given) for array in arrays}
        out_ref, energy_ref, sum_ref, block_ref, result_ref, right_ref, semaphores = given
        copies = Copies(semaphores)
        arriving = [
            copies.start_piece(piece, ref_of, flag_ref, SUBLANES, energy_ref.at[at])
            for at, piece in enumerate(energies)
        ]
        arriving += [
            copies.start(ref, sum_ref.at[at // HALVES, pl.ds(at % HALVES * share, share)])
            for at, ref in enumerate(sum_refs)
        ]
        coming = [
            [
                copies.start_piece(slots[slot][at], ref_of, flag_ref, cut, block_ref.at[slot, at])
                for slot in range(count)
            ]
            for at in range(chunks)
        ]
        adding = [
            [copies.start(ref.at[pl.ds(at * cut, cut)], result_ref.at[at]) for ref in before_refs]
            for at in range(chunks)
        ]
        for copy in arriving:
            copy.wait()

        def line(at):
            virtual = virt_ref[...]
            energy = energy_ref[at]
            return jnp.concatenate([virtual - energy[:1, i : i + 1] for i in range(occ_rows)], axis=1)

        row = jnp.broadcast_to(line(0), (SUBLANES, width)).T[:, :1]
        at = 0
        for slot in range(count):
            total = sum_ref[at]
            for extra in range(1, len(partials[slot])):
                total = total + sum_ref[at + extra]
            at += len(partials[slot])
            amplitude = (sign_ref[first_sign + slot] * total) / (row + line(slot + 1))
            right_ref[:, pl.ds(slot * 3 * width, 3 * width)] = deep_right(amplitude, 1)
        leaving = []
        for at in range(chunks):
            for copy in coming[at] + adding[at]:
                copy.wait()
            left = [deep_left(rows_of(block_ref.at[slot, at], 0, size, width)) for slot in range(count)]
            value = dot(jnp.concatenate(left, axis=1), right_ref[...], 1)
            for column in range(lines):
                lanes = value[:, column * LANES : (column + 1) * LANES]
                where = pl.ds(column, size, stride=lines)
                if last:
                    lanes = lanes + result_ref[at, where, :]
                result_ref[at, where, :] = lanes
            leaving.append(copies.start(result_ref.at[at], out_ref.at[pl.ds(at * cut, cut)]))
        for copy in leaving:
            copy.wait()

    rows = chunks * size
    out = jax.ShapeDtypeStruct((rows * lines, LANES), jnp.float32)
    scratch = [
        pltpu.VMEM((len(energies), SUBLANES, LANES), jnp.float32),
        pltpu.VMEM((len(sums) // HALVES, width, width), jnp.float32),
        pltpu.VMEM((count, chunks, cut, LANES), jnp.float32),
        pltpu.VMEM((chunks, cut, LANES), jnp.float32),
        pltpu.VMEM((width, count * 3 * width), jnp.bfloat16),
        pltpu.SemaphoreType.DMA((len(energies) + len(sums) + len(pieces) + 2 * chunks,)),
    ]
    return call(kernel, [signs, flags], [eps_virt], [*sums, *last, *arrays], [out], pl.ANY, scratch, limit)[0]


def after(block, *others):
    return lax.optimization_barrier((block, *others))[0]


def on_device(factors, eps_occ, eps_virt, pair_mask):
    rows, occ_rows, virt = factors.shape
    width = occ_rows * virt
    lines = width // LANES
    groups = lax.axis_size("occ")
    shares = lax.axis_size("aux")
    size = rows // CHUNKS
    cut = size * lines
    last = CHUNKS - 1
    group = lax.axis_index("occ")
    place = group % PLANE
    odd_x = place % 2 == 1
    odd_y = place // 2 == 1

    own = factors.reshape(rows * lines, LANES)
    energies = jnp.zeros((SUBLANES * LANES,), jnp.float32).at[:occ_rows].set(eps_occ)
    energies = energies.reshape(SUBLANES, LANES)

    def part(whole, at):
        return whole[at * cut : (at + 1) * cut]

    def within(block, moves):
        planes = range(0, groups, PLANE)
        return lax.ppermute(block, "occ", [(g + a, g + b) for g in planes for a, b in moves])

    def up(block):
        return lax.ppermute(block, "occ", [(g, g + PLANE) for g in range(groups - PLANE)])

    def totals(parts):
        if shares == 2:
            return [parts, [lax.ppermute(part, "aux", [(0, 1), (1, 0)]) for part in parts]]
        return [[lax.psum(part, "aux") for part in parts]]

    first_sent = jnp.concatenate([part(own, 0), energies])
    def choices(sent):
        group_then, mask_row, _ = lax.optimization_barrier((group, pair_mask[0], sent))
        place_then = group_then % PLANE

        def sign(offset):
            flag = jnp.sum(jnp.where(jnp.arange(1, PLANE + 1) == offset, mask_row, 0))
            return jnp.where((group_then >= offset) & (flag > 0), -1.0, 0.0).astype(jnp.float32)

        near = jnp.where(place_then % 2 == 1, 1, PLANE - 1)
        signs = [jnp.float32(-1.0), sign(PLANE), sign(near), sign(PLANE // 2), sign(PLANE - near)]
        up_then = place_then // 2 == 1
        flags = [
            1 - place_then % 2,
            1 - place_then // 2,
            jnp.where(up_then, 0, 1 + place_then),
            jnp.where(up_then, place_then - 1, 0),
        ]
        return jnp.stack(signs), jnp.stack(flags).astype(jnp.int32)

    def add(first_sign, partials, slots, carriers, before=None, limit=VMEM_LIMIT):
        return contract(
            partials, slots, signs, first_sign, carriers, flags, eps_virt[None, :], size, before, limit
        )

    from_own = [first_sent]
    from_z = [up(first_sent)]
    up_x = within(first_sent, [(0, 1), (2, 3), (1, 0)])
    up_y = within(first_sent, [(0, 2), (1, 3)])
    high, low, *made = prepare(own, energies, rows, width)
    partial_own = made[:HALVES]
    from_own += made[HALVES:]
    turned = (high, low)
    sums_own = totals(partial_own)
    swap_x, swap_y = [], []
    passed = [partial_own[0]]
    for at in range(CHUNKS):
        came = after(from_z[at], *passed)
        if at < last:
            from_z.append(up(after(from_own[at + 1], came)))
            up_part = after(from_own[at + 1], came)
            send_x = after(jnp.where(odd_x, came, up_part), swap_x[at - 1] if at else up_x)
            came, up_part, _ = lax.optimization_barrier((came, up_part, send_x))
            send_y = after(jnp.where(odd_y, came, up_part), swap_y[at - 1] if at else up_y)
            if at == 0:
                signs, flags = choices((send_x, send_y))
            swap_x.append(within(send_x, [(0, 1), (1, 0), (2, 3), (3, 2)]))
            swap_y.append(within(send_y, [(0, 2), (2, 0), (1, 3), (3, 1)]))
        else:
            cycle = within(after(turning, came, swap_x[last - 1]), [(0, 1), (1, 3), (3, 2), (2, 0)])
            send_x = after(jnp.where(odd_x, came, swap_y[0]), swap_x[last - 1])
            send_y = after(jnp.where(odd_y, after(came, send_x), up_x), swap_y[last - 1])
            swap_x.append(within(send_x, [(0, 1), (1, 0), (2, 3), (3, 2)]))
            swap_y.append(within(send_y, [(0, 2), (2, 0), (1, 3), (3, 1)]))
        passed = []
        if at == 1:
            passed = [signs, flags]
            middle = (place == 1) | (place == 2)
            turning = jnp.where(middle, swap_x[1], swap_y[1])
        if at == 2:
            passed.append(turning)

    cross = within(jnp.where(place == 2, swap_x[0], swap_y[0]), [(2, 0), (3, 2)])
    swap_d = within(swap_y[2], [(0, 1), (1, 0), (2, 3), (3, 2)])
    last_d = within(swap_y[3], [(0, 1), (1, 0)])

    def pieces_of(first, swaps, choice, base):
        arrays = [first, *swaps]
        return [Piece(((arrays[at], base), (arrays[at + 1], base)), choice) for at in range(CHUNKS)]

    def whole(array, base):
        return Piece(((array, base),))

    slot_own = [whole(own, at * cut) for at in range(CHUNKS)]
    slot_z = [whole(block, 0) for block in from_z]
    slot_x = pieces_of(up_x, swap_x, 0, 0)
    slot_y = pieces_of(up_y, swap_y, 1, 0)
    slot_d = [
        Piece(((swap_y[last], 0), (cross, 0), (swap_x[last], 0)), 2),
        Piece(((cycle, 0), (cross, 0), (swap_x[last], 0)), 3),
        Piece(((cycle, 0), (swap_d, 0)), 1),
        Piece(((swap_d, 0), (last_d, 0)), 1),
    ]
    eps_x = pieces_of(up_x, swap_x, 0, cut)[0]
    eps_y = pieces_of(up_y, swap_y, 1, cut)[0]
    eps_d = Piece(((swap_y[last], cut), (cross, cut), (swap_x[last], cut)), 2)

    partial_z, *early = integrate(
        turned, [slot_z, slot_x[:last], slot_y[:last]], [0, 0, 0], flags, size, width
    )
    own_eps = whole(first_sent, cut)
    partial_x, partial_y = integrate(
        turned, [slot_x[last:], slot_y[last:]], [last, last], flags, size, width, early
    )
    gradient = add(
        0,
        [after(sums_own, cycle), totals(partial_z), totals(partial_x), totals(partial_y)],
        [slot_own, slot_z, slot_x, slot_y],
        [own_eps, own_eps, whole(from_z[0], cut), eps_x, eps_y],
    )
    turned = after(turned, gradient)
    half = CHUNKS // 2
    partial_d = integrate(turned, [slot_d[:half]], [0], flags, size, width)
    (partial_d,) = integrate(turned, [slot_d[half:]], [half], flags, size, width, partial_d, LAST_LIMIT)
    gradient = add(4, [totals(partial_d)], [slot_d], [own_eps, eps_d], gradient, LAST_LIMIT)
    return gradient.reshape(rows, occ_rows, virt)


def solution(mesh):
    if mesh.shape["occ"] % PLANE:
        raise ValueError("incomplete plane")
    in_specs = (P("aux", "occ", None), P("occ"), P(), P("occ", None))
    out_specs = P("aux", "occ", None)
    return jax.shard_map(
        on_device, mesh=mesh, in_specs=in_specs, out_specs=out_specs, check_vma=False
    )
```

```python
import dataclasses
import functools

import jax
import jax.numpy as jnp
from jax import lax
from jax.experimental import pallas as pl
from jax.experimental.pallas import tpu as pltpu
from jax.sharding import PartitionSpec as P

LANES = 128
SUBLANES = 8
PLANE = 4
CHUNKS = 4
VMEM_LIMIT = 32 * 1024 * 1024
FIRST_LIMIT = 60 * 1024 * 1024
LAST_LIMIT = 24 * 1024 * 1024
HALVES = 2


def split(value):
    high = value.astype(jnp.bfloat16)
    low = (value - high.astype(jnp.float32)).astype(jnp.bfloat16)
    return high, low


def deep_left(value):
    high, low = split(value)
    return jnp.concatenate([high, low, high], axis=1)


def deep_right(value, axis=0):
    high, low = split(value)
    return jnp.concatenate([high, high, low], axis=axis)


def dot(left, right, axis=0):
    numbers = (((1,), (axis,)), ((), ()))
    return lax.dot_general(left, right, numbers, preferred_element_type=jnp.float32)


def rows_of(ref, start, count, width):
    lines = width // LANES
    columns = [ref[pl.ds(start * lines + at, count, stride=lines), :] for at in range(lines)]
    return jnp.concatenate(columns, axis=1)


def distinct(arrays):
    return list({id(array): array for array in arrays}.values())


class Copies:
    def __init__(self, semaphores):
        self.semaphores = semaphores
        self.used = 0

    def start(self, source, target):
        copy = pltpu.make_async_copy(source, target, self.semaphores.at[self.used])
        self.used += 1
        copy.start()
        return copy

    def start_piece(self, piece, ref_of, choices, count, target):
        made = []
        for array, base in piece.places:
            source = ref_of[id(array)].at[pl.ds(base, count)]
            made.append(pltpu.make_async_copy(source, target, self.semaphores.at[self.used]))
        self.used += 1
        if len(made) == 1:
            made[0].start()
        else:
            for at, copy in enumerate(made):
                pl.when(choices[piece.choice] == at)(copy.start)
        return made[0]


@dataclasses.dataclass(frozen=True)
class Piece:
    places: tuple
    choice: int = 0


def call(kernel, smem, vmem, anywhere, outputs, out_space, scratch, limit=VMEM_LIMIT):
    spaces = [pltpu.SMEM] * len(smem) + [pltpu.VMEM] * len(vmem) + [pl.ANY] * len(anywhere)
    return pl.pallas_call(
        kernel,
        out_shape=outputs,
        in_specs=[pl.BlockSpec(memory_space=space) for space in spaces],
        out_specs=[pl.BlockSpec(memory_space=out_space)] * len(outputs),
        scratch_shapes=scratch,
        compiler_params=pltpu.CompilerParams(vmem_limit_bytes=limit),
        cost_estimate=pl.CostEstimate(flops=0, bytes_accessed=0, transcendentals=0),
    )(*smem, *vmem, *anywhere)


def prepare(own, energies, rows, width):
    size = rows // CHUNKS
    cut = size * width // LANES
    share = width // HALVES

    def kernel(energy_ref, own_ref, high_out, low_out, *refs):
        integral_outs, refs = refs[:HALVES], refs[HALVES:]
        sent_refs = refs[: CHUNKS - 1]
        block_ref, turned_ref, integrals_ref, semaphores = refs[CHUNKS - 1 :]
        copies = Copies(semaphores)
        coming = [copies.start(own_ref.at[pl.ds(at * cut, cut)], block_ref.at[at]) for at in range(CHUNKS)]
        leaving = [copies.start(energy_ref, ref.at[pl.ds(cut, SUBLANES)]) for ref in sent_refs]
        for at in range(CHUNKS):
            coming[at].wait()
            if at:
                leaving.append(copies.start(block_ref.at[at], sent_refs[at - 1].at[pl.ds(0, cut)]))
            block = rows_of(block_ref.at[at], 0, size, width)
            high, low = split(block.T)
            turned_ref[0, at] = high
            turned_ref[1, at] = low
            leaving.append(copies.start(turned_ref.at[0, at], high_out.at[at]))
            leaving.append(copies.start(turned_ref.at[1, at], low_out.at[at]))
            value = dot(jnp.concatenate([high, low, high], axis=1), deep_right(block))
            integrals_ref[...] = integrals_ref[...] + value if at else value
        for at, out_ref in enumerate(integral_outs):
            leaving.append(copies.start(integrals_ref.at[pl.ds(at * share, share)], out_ref))
        for copy in leaving:
            copy.wait()

    turned = jax.ShapeDtypeStruct((CHUNKS, width, size), jnp.bfloat16)
    square = jax.ShapeDtypeStruct((share, width), jnp.float32)
    sent = jax.ShapeDtypeStruct((cut + SUBLANES, LANES), jnp.float32)
    scratch = [
        pltpu.VMEM((CHUNKS, cut, LANES), jnp.float32),
        pltpu.VMEM((2, CHUNKS, width, size), jnp.bfloat16),
        pltpu.VMEM((width, width), jnp.float32),
        pltpu.SemaphoreType.DMA((5 * CHUNKS + HALVES,)),
    ]
    outs = [turned, turned] + [square] * HALVES + [sent] * (CHUNKS - 1)
    return call(kernel, [], [energies], [own], outs, pl.ANY, scratch, FIRST_LIMIT)


def arrays_of(pieces):
    return distinct([array for piece in pieces for array, _ in piece.places])


def integrate(turned, slots, first, flags, size, width, before=(), limit=VMEM_LIMIT):
    cut = size * width // LANES
    count = len(slots)
    pieces = [piece for slot in slots for piece in slot]
    arrays = arrays_of(pieces)
    numbers = [list(range(start, start + len(slot))) for slot, start in zip(slots, first)]
    needed = sorted({number for some in numbers for number in some})
    before = [part for parts in before for part in parts]
    share = width // HALVES

    def kernel(flag_ref, *refs):
        given = iter(refs)
        high_ref, low_ref = next(given), next(given)
        before_refs = [next(given) for _ in before]
        ref_of = {id(array): next(given) for array in arrays}
        outs = [[next(given) for _ in range(HALVES)] for _ in range(count)]
        turned_ref, block_ref, before_ref, semaphores = given
        copies = Copies(semaphores)
        coming, turning = [], {}

        def turn(number):
            if number not in turning:
                at = needed.index(number)
                turning[number] = [
                    copies.start(high_ref.at[number], turned_ref.at[at, 0]),
                    copies.start(low_ref.at[number], turned_ref.at[at, 1]),
                ]

        at = 0
        for slot in range(count):
            for number, piece in zip(numbers[slot], slots[slot]):
                turn(number)
                coming.append(copies.start_piece(piece, ref_of, flag_ref, cut, block_ref.at[at]))
                at += 1
        adding = [
            copies.start(ref, before_ref.at[at // HALVES, pl.ds(at % HALVES * share, share)])
            for at, ref in enumerate(before_refs)
        ]
        at = 0
        for slot in range(count):
            total = None
            for place, number in enumerate(numbers[slot]):
                for copy in turning.pop(number, []):
                    copy.wait()
                coming[at].wait()
                there = needed.index(number)
                high, low = turned_ref[there, 0], turned_ref[there, 1]
                left = jnp.concatenate([high, low, high], axis=1)
                value = dot(left, deep_right(rows_of(block_ref.at[at], 0, size, width)))
                total = total + value if place else value
                at += 1
            if before:
                for number in range(HALVES):
                    adding[slot * HALVES + number].wait()
                total = total + before_ref[slot]
            for number, out_ref in enumerate(outs[slot]):
                out_ref[...] = total[number * share : (number + 1) * share]

    out = [jax.ShapeDtypeStruct((share, width), jnp.float32)] * (HALVES * count)
    scratch = [
        pltpu.VMEM((len(needed), 2, width, size), jnp.bfloat16),
        pltpu.VMEM((len(pieces), cut, LANES), jnp.float32),
        pltpu.VMEM((max(len(before) // HALVES, 1), width, width), jnp.float32),
        pltpu.SemaphoreType.DMA((2 * len(needed) + len(pieces) + len(before),)),
    ]
    made = call(kernel, [flags], [], [*turned, *before, *arrays], out, pltpu.VMEM, scratch, limit)
    return [made[slot * HALVES : (slot + 1) * HALVES] for slot in range(count)]


def contract(partials, slots, signs, first_sign, energies, flags, eps_virt, size, before=None, limit=VMEM_LIMIT, space=pltpu.VMEM):
    count = len(slots)
    chunks = len(slots[0])
    virt = eps_virt.shape[1]
    width = partials[0][0][0].shape[1]
    share = width // HALVES
    occ_rows = width // virt
    lines = width // LANES
    cut = size * lines
    sums = [part for slot in partials for term in slot for part in term]
    pieces = [piece for slot in slots for piece in slot]
    arrays = arrays_of([*pieces, *energies])
    last = [before] if before is not None else []

    def kernel(*refs):
        given = iter(refs)
        sign_ref, flag_ref, virt_ref = next(given), next(given), next(given)
        sum_refs = [next(given) for _ in sums]
        before_refs = [next(given) for _ in last]
        ref_of = {id(array): next(given) for array in arrays}
        out_ref, energy_ref, sum_ref, block_ref, result_ref, right_ref, semaphores = given
        copies = Copies(semaphores)
        arriving = [
            copies.start_piece(piece, ref_of, flag_ref, SUBLANES, energy_ref.at[at])
            for at, piece in enumerate(energies)
        ]
        arriving += [
            copies.start(ref, sum_ref.at[at // HALVES, pl.ds(at % HALVES * share, share)])
            for at, ref in enumerate(sum_refs)
        ]
        coming = [
            [
                copies.start_piece(slots[slot][at], ref_of, flag_ref, cut, block_ref.at[slot, at])
                for slot in range(count)
            ]
            for at in range(chunks)
        ]
        adding = [
            [copies.start(ref.at[pl.ds(at * cut, cut)], result_ref.at[at]) for ref in before_refs]
            for at in range(chunks)
        ]
        for copy in arriving:
            copy.wait()

        def line(at):
            virtual = virt_ref[...]
            energy = energy_ref[at]
            return jnp.concatenate([virtual - energy[:1, i : i + 1] for i in range(occ_rows)], axis=1)

        row = jnp.broadcast_to(line(0), (SUBLANES, width)).T[:, :1]
        at = 0
        for slot in range(count):
            total = sum_ref[at]
            for extra in range(1, len(partials[slot])):
                total = total + sum_ref[at + extra]
            at += len(partials[slot])
            amplitude = (sign_ref[first_sign + slot] * total) / (row + line(slot + 1))
            right_ref[:, pl.ds(slot * 3 * width, 3 * width)] = deep_right(amplitude, 1)
        leaving = []
        for at in range(chunks):
            for copy in coming[at] + adding[at]:
                copy.wait()
            left = [deep_left(rows_of(block_ref.at[slot, at], 0, size, width)) for slot in range(count)]
            value = dot(jnp.concatenate(left, axis=1), right_ref[...], 1)
            for column in range(lines):
                lanes = value[:, column * LANES : (column + 1) * LANES]
                where = pl.ds(column, size, stride=lines)
                if last:
                    lanes = lanes + result_ref[at, where, :]
                result_ref[at, where, :] = lanes
            leaving.append(copies.start(result_ref.at[at], out_ref.at[pl.ds(at * cut, cut)]))
        for copy in leaving:
            copy.wait()

    rows = chunks * size
    out = jax.ShapeDtypeStruct((rows * lines, LANES), jnp.float32)
    scratch = [
        pltpu.VMEM((len(energies), SUBLANES, LANES), jnp.float32),
        pltpu.VMEM((len(sums) // HALVES, width, width), jnp.float32),
        pltpu.VMEM((count, chunks, cut, LANES), jnp.float32),
        pltpu.VMEM((chunks, cut, LANES), jnp.float32),
        pltpu.VMEM((width, count * 3 * width), jnp.bfloat16),
        pltpu.SemaphoreType.DMA((len(energies) + len(sums) + len(pieces) + 2 * chunks,)),
    ]
    return call(kernel, [signs, flags], [eps_virt], [*sums, *last, *arrays], [out], space, scratch, limit)[0]


def after(block, *others):
    return lax.optimization_barrier((block, *others))[0]


def on_device(factors, eps_occ, eps_virt, pair_mask):
    rows, occ_rows, virt = factors.shape
    width = occ_rows * virt
    lines = width // LANES
    groups = lax.axis_size("occ")
    shares = lax.axis_size("aux")
    size = rows // CHUNKS
    cut = size * lines
    last = CHUNKS - 1
    group = lax.axis_index("occ")
    place = group % PLANE
    odd_x = place % 2 == 1
    odd_y = place // 2 == 1

    own = factors.reshape(rows * lines, LANES)
    energies = jnp.zeros((SUBLANES * LANES,), jnp.float32).at[:occ_rows].set(eps_occ)
    energies = energies.reshape(SUBLANES, LANES)

    def part(whole, at):
        return whole[at * cut : (at + 1) * cut]

    def within(block, moves):
        planes = range(0, groups, PLANE)
        return lax.ppermute(block, "occ", [(g + a, g + b) for g in planes for a, b in moves])

    def up(block):
        return lax.ppermute(block, "occ", [(g, g + PLANE) for g in range(groups - PLANE)])

    def totals(parts):
        if shares == 2:
            return [parts, [lax.ppermute(part, "aux", [(0, 1), (1, 0)]) for part in parts]]
        return [[lax.psum(part, "aux") for part in parts]]

    first_sent = jnp.concatenate([part(own, 0), energies])
    def choices(sent):
        group_then, mask_row, _ = lax.optimization_barrier((group, pair_mask[0], sent))
        place_then = group_then % PLANE

        def sign(offset):
            flag = jnp.sum(jnp.where(jnp.arange(1, PLANE + 1) == offset, mask_row, 0))
            return jnp.where((group_then >= offset) & (flag > 0), -1.0, 0.0).astype(jnp.float32)

        near = jnp.where(place_then % 2 == 1, 1, PLANE - 1)
        signs = [jnp.float32(-1.0), sign(PLANE), sign(near), sign(PLANE // 2), sign(PLANE - near)]
        up_then = place_then // 2 == 1
        flags = [
            1 - place_then % 2,
            1 - place_then // 2,
            jnp.where(up_then, 0, 1 + place_then),
            jnp.where(up_then, place_then - 1, 0),
        ]
        return jnp.stack(signs), jnp.stack(flags).astype(jnp.int32)

    def add(first_sign, partials, slots, carriers, before=None, limit=VMEM_LIMIT, space=pltpu.VMEM):
        return contract(
            partials, slots, signs, first_sign, carriers, flags, eps_virt[None, :], size, before, limit, space
        )

    from_own = [first_sent]
    from_z = [up(first_sent)]
    up_x = within(first_sent, [(0, 1), (2, 3), (1, 0)])
    up_y = within(first_sent, [(0, 2), (1, 3)])
    high, low, *made = prepare(own, energies, rows, width)
    partial_own = made[:HALVES]
    from_own += made[HALVES:]
    turned = (high, low)
    sums_own = totals(partial_own)
    swap_x, swap_y = [], []
    passed = [partial_own[0]]
    for at in range(CHUNKS):
        came = after(from_z[at], *passed)
        if at < last:
            from_z.append(up(after(from_own[at + 1], came)))
            up_part = after(from_own[at + 1], came)
            send_x, send_y = jnp.where(odd_x, came, up_part), jnp.where(odd_y, came, up_part)
            send_x = after(send_x, swap_x[at - 1] if at else up_x)
            send_y = after(send_y, swap_y[at - 1] if at else up_y)
            if at == 0:
                signs, flags = choices((send_x, send_y))
            swap_x.append(within(send_x, [(0, 1), (1, 0), (2, 3), (3, 2)]))
            swap_y.append(within(send_y, [(0, 2), (2, 0), (1, 3), (3, 1)]))
        else:
            cycle = within(after(turning, came, swap_x[last - 1]), [(0, 1), (1, 3), (3, 2), (2, 0)])
            send_x = after(jnp.where(odd_x, came, swap_y[0]), swap_x[last - 1])
            send_y = after(jnp.where(odd_y, came, up_x), swap_y[last - 1])
            swap_x.append(within(send_x, [(0, 1), (1, 0), (2, 3), (3, 2)]))
            swap_y.append(within(send_y, [(0, 2), (2, 0), (1, 3), (3, 1)]))
        passed = []
        if at == 1:
            passed = [signs, flags]
            middle = (place == 1) | (place == 2)
            turning = jnp.where(middle, swap_x[1], swap_y[1])
        if at == 2:
            passed.append(turning)

    cross = within(jnp.where(place == 2, swap_x[0], swap_y[0]), [(2, 0), (3, 2)])
    swap_d = within(swap_y[2], [(0, 1), (1, 0), (2, 3), (3, 2)])
    last_d = within(swap_y[3], [(0, 1), (1, 0)])

    def pieces_of(first, swaps, choice, base):
        arrays = [first, *swaps]
        return [Piece(((arrays[at], base), (arrays[at + 1], base)), choice) for at in range(CHUNKS)]

    def whole(array, base):
        return Piece(((array, base),))

    slot_own = [whole(own, at * cut) for at in range(CHUNKS)]
    slot_z = [whole(block, 0) for block in from_z]
    slot_x = pieces_of(up_x, swap_x, 0, 0)
    slot_y = pieces_of(up_y, swap_y, 1, 0)
    slot_d = [
        Piece(((swap_y[last], 0), (cross, 0), (swap_x[last], 0)), 2),
        Piece(((cycle, 0), (cross, 0), (swap_x[last], 0)), 3),
        Piece(((cycle, 0), (swap_d, 0)), 1),
        Piece(((swap_d, 0), (last_d, 0)), 1),
    ]
    eps_x = pieces_of(up_x, swap_x, 0, cut)[0]
    eps_y = pieces_of(up_y, swap_y, 1, cut)[0]
    eps_d = Piece(((swap_y[last], cut), (cross, cut), (swap_x[last], cut)), 2)

    partial_z, *early = integrate(
        turned, [slot_z, slot_x[:last], slot_y[:last]], [0, 0, 0], flags, size, width
    )
    own_eps = whole(first_sent, cut)
    partial_x, partial_y = integrate(
        turned, [slot_x[last:], slot_y[last:]], [last, last], flags, size, width, early
    )
    gradient = add(
        0,
        [after(sums_own, cycle), totals(partial_z), totals(partial_x), totals(partial_y)],
        [slot_own, slot_z, slot_x, slot_y],
        [own_eps, own_eps, whole(from_z[0], cut), eps_x, eps_y],
    )
    turned = after(turned, gradient)
    half = CHUNKS // 2
    partial_d = integrate(turned, [slot_d[:half]], [0], flags, size, width)
    (partial_d,) = integrate(turned, [slot_d[half:]], [half], flags, size, width, partial_d, LAST_LIMIT)
    gradient = add(4, [totals(partial_d)], [slot_d], [own_eps, eps_d], gradient, LAST_LIMIT, pl.ANY)
    return gradient.reshape(rows, occ_rows, virt)


def solution(mesh):
    if mesh.shape["occ"] % PLANE:
        raise ValueError("incomplete plane")
    in_specs = (P("aux", "occ", None), P("occ"), P(), P("occ", None))
    out_specs = P("aux", "occ", None)
    return jax.shard_map(
        on_device, mesh=mesh, in_specs=in_specs, out_specs=out_specs, check_vma=False
    )
```

```python
import dataclasses
import functools

import jax
import jax.numpy as jnp
from jax import lax
from jax.experimental import pallas as pl
from jax.experimental.pallas import tpu as pltpu
from jax.sharding import PartitionSpec as P

LANES = 128
SUBLANES = 8
PLANE = 4
CHUNKS = 4
VMEM_LIMIT = 32 * 1024 * 1024
FIRST_LIMIT = 60 * 1024 * 1024
LAST_LIMIT = 24 * 1024 * 1024
HALVES = 2


def split(value):
    high = value.astype(jnp.bfloat16)
    low = (value - high.astype(jnp.float32)).astype(jnp.bfloat16)
    return high, low


def deep_left(value):
    high, low = split(value)
    return jnp.concatenate([high, low, high], axis=1)


def deep_right(value, axis=0):
    high, low = split(value)
    return jnp.concatenate([high, high, low], axis=axis)


def dot(left, right, axis=0):
    numbers = (((1,), (axis,)), ((), ()))
    return lax.dot_general(left, right, numbers, preferred_element_type=jnp.float32)


def rows_of(ref, start, count, width):
    lines = width // LANES
    columns = [ref[pl.ds(start * lines + at, count, stride=lines), :] for at in range(lines)]
    return jnp.concatenate(columns, axis=1)


def distinct(arrays):
    return list({id(array): array for array in arrays}.values())


class Copies:
    def __init__(self, semaphores):
        self.semaphores = semaphores
        self.used = 0

    def start(self, source, target):
        copy = pltpu.make_async_copy(source, target, self.semaphores.at[self.used])
        self.used += 1
        copy.start()
        return copy

    def start_piece(self, piece, ref_of, choices, count, target):
        made = []
        for array, base in piece.places:
            source = ref_of[id(array)].at[pl.ds(base, count)]
            made.append(pltpu.make_async_copy(source, target, self.semaphores.at[self.used]))
        self.used += 1
        if len(made) == 1:
            made[0].start()
        else:
            for at, copy in enumerate(made):
                pl.when(choices[piece.choice] == at)(copy.start)
        return made[0]


@dataclasses.dataclass(frozen=True)
class Piece:
    places: tuple
    choice: int = 0


def call(kernel, smem, vmem, anywhere, outputs, out_space, scratch, limit=VMEM_LIMIT):
    spaces = [pltpu.SMEM] * len(smem) + [pltpu.VMEM] * len(vmem) + [pl.ANY] * len(anywhere)
    return pl.pallas_call(
        kernel,
        out_shape=outputs,
        in_specs=[pl.BlockSpec(memory_space=space) for space in spaces],
        out_specs=[pl.BlockSpec(memory_space=out_space)] * len(outputs),
        scratch_shapes=scratch,
        compiler_params=pltpu.CompilerParams(vmem_limit_bytes=limit),
        cost_estimate=pl.CostEstimate(flops=0, bytes_accessed=0, transcendentals=0),
    )(*smem, *vmem, *anywhere)


def prepare(own, energies, rows, width):
    size = rows // CHUNKS
    cut = size * width // LANES
    share = width // HALVES

    def kernel(energy_ref, own_ref, high_out, low_out, *refs):
        integral_outs, refs = refs[:HALVES], refs[HALVES:]
        sent_refs = refs[: CHUNKS - 1]
        block_ref, turned_ref, integrals_ref, semaphores = refs[CHUNKS - 1 :]
        copies = Copies(semaphores)
        coming = [copies.start(own_ref.at[pl.ds(at * cut, cut)], block_ref.at[at]) for at in range(CHUNKS)]
        leaving = [copies.start(energy_ref, ref.at[pl.ds(cut, SUBLANES)]) for ref in sent_refs]
        for at in range(CHUNKS):
            coming[at].wait()
            if at:
                leaving.append(copies.start(block_ref.at[at], sent_refs[at - 1].at[pl.ds(0, cut)]))
            block = rows_of(block_ref.at[at], 0, size, width)
            high, low = split(block.T)
            turned_ref[0, at] = high
            turned_ref[1, at] = low
            leaving.append(copies.start(turned_ref.at[0, at], high_out.at[at]))
            leaving.append(copies.start(turned_ref.at[1, at], low_out.at[at]))
            value = dot(jnp.concatenate([high, low, high], axis=1), deep_right(block))
            integrals_ref[...] = integrals_ref[...] + value if at else value
        for at, out_ref in enumerate(integral_outs):
            leaving.append(copies.start(integrals_ref.at[pl.ds(at * share, share)], out_ref))
        for copy in leaving:
            copy.wait()

    turned = jax.ShapeDtypeStruct((CHUNKS, width, size), jnp.bfloat16)
    square = jax.ShapeDtypeStruct((share, width), jnp.float32)
    sent = jax.ShapeDtypeStruct((cut + SUBLANES, LANES), jnp.float32)
    scratch = [
        pltpu.VMEM((CHUNKS, cut, LANES), jnp.float32),
        pltpu.VMEM((2, CHUNKS, width, size), jnp.bfloat16),
        pltpu.VMEM((width, width), jnp.float32),
        pltpu.SemaphoreType.DMA((5 * CHUNKS + HALVES,)),
    ]
    outs = [turned, turned] + [square] * HALVES + [sent] * (CHUNKS - 1)
    return call(kernel, [], [energies], [own], outs, pl.ANY, scratch, FIRST_LIMIT)


def arrays_of(pieces):
    return distinct([array for piece in pieces for array, _ in piece.places])


def integrate(turned, slots, first, flags, size, width, before=(), limit=VMEM_LIMIT):
    cut = size * width // LANES
    count = len(slots)
    pieces = [piece for slot in slots for piece in slot]
    arrays = arrays_of(pieces)
    numbers = [list(range(start, start + len(slot))) for slot, start in zip(slots, first)]
    needed = sorted({number for some in numbers for number in some})
    before = [part for parts in before for part in parts]
    share = width // HALVES

    def kernel(flag_ref, *refs):
        given = iter(refs)
        high_ref, low_ref = next(given), next(given)
        before_refs = [next(given) for _ in before]
        ref_of = {id(array): next(given) for array in arrays}
        outs = [[next(given) for _ in range(HALVES)] for _ in range(count)]
        turned_ref, block_ref, before_ref, semaphores = given
        copies = Copies(semaphores)
        coming, turning = [], {}

        def turn(number):
            if number not in turning:
                at = needed.index(number)
                turning[number] = [
                    copies.start(high_ref.at[number], turned_ref.at[at, 0]),
                    copies.start(low_ref.at[number], turned_ref.at[at, 1]),
                ]

        at = 0
        for slot in range(count):
            for number, piece in zip(numbers[slot], slots[slot]):
                turn(number)
                coming.append(copies.start_piece(piece, ref_of, flag_ref, cut, block_ref.at[at]))
                at += 1
        adding = [
            copies.start(ref, before_ref.at[at // HALVES, pl.ds(at % HALVES * share, share)])
            for at, ref in enumerate(before_refs)
        ]
        at = 0
        for slot in range(count):
            total = None
            for place, number in enumerate(numbers[slot]):
                for copy in turning.pop(number, []):
                    copy.wait()
                coming[at].wait()
                there = needed.index(number)
                high, low = turned_ref[there, 0], turned_ref[there, 1]
                left = jnp.concatenate([high, low, high], axis=1)
                value = dot(left, deep_right(rows_of(block_ref.at[at], 0, size, width)))
                total = total + value if place else value
                at += 1
            if before:
                for number in range(HALVES):
                    adding[slot * HALVES + number].wait()
                total = total + before_ref[slot]
            for number, out_ref in enumerate(outs[slot]):
                out_ref[...] = total[number * share : (number + 1) * share]

    out = [jax.ShapeDtypeStruct((share, width), jnp.float32)] * (HALVES * count)
    scratch = [
        pltpu.VMEM((len(needed), 2, width, size), jnp.bfloat16),
        pltpu.VMEM((len(pieces), cut, LANES), jnp.float32),
        pltpu.VMEM((max(len(before) // HALVES, 1), width, width), jnp.float32),
        pltpu.SemaphoreType.DMA((2 * len(needed) + len(pieces) + len(before),)),
    ]
    made = call(kernel, [flags], [], [*turned, *before, *arrays], out, pltpu.VMEM, scratch, limit)
    return [made[slot * HALVES : (slot + 1) * HALVES] for slot in range(count)]


def contract(partials, slots, signs, first_sign, energies, flags, eps_virt, size, before=None, limit=VMEM_LIMIT):
    count = len(slots)
    chunks = len(slots[0])
    virt = eps_virt.shape[1]
    width = partials[0][0][0].shape[1]
    share = width // HALVES
    occ_rows = width // virt
    lines = width // LANES
    cut = size * lines
    sums = [part for slot in partials for term in slot for part in term]
    pieces = [piece for slot in slots for piece in slot]
    arrays = arrays_of([*pieces, *energies])
    last = [before] if before is not None else []
    ahead = count == 1

    def kernel(*refs):
        given = iter(refs)
        sign_ref, flag_ref, virt_ref = next(given), next(given), next(given)
        sum_refs = [next(given) for _ in sums]
        before_refs = [next(given) for _ in last]
        ref_of = {id(array): next(given) for array in arrays}
        out_ref, energy_ref, sum_ref, block_ref, result_ref, right_ref, left_ref, semaphores = given
        copies = Copies(semaphores)
        arriving = [
            copies.start_piece(piece, ref_of, flag_ref, SUBLANES, energy_ref.at[at])
            for at, piece in enumerate(energies)
        ]
        arriving += [
            copies.start(ref, sum_ref.at[at // HALVES, pl.ds(at % HALVES * share, share)])
            for at, ref in enumerate(sum_refs)
        ]
        coming = [
            [
                copies.start_piece(slots[slot][at], ref_of, flag_ref, cut, block_ref.at[slot, at])
                for slot in range(count)
            ]
            for at in range(chunks)
        ]
        adding = [
            [copies.start(ref.at[pl.ds(at * cut, cut)], result_ref.at[at]) for ref in before_refs]
            for at in range(chunks)
        ]
        if ahead:
            for at in range(chunks):
                coming[at][0].wait()
                left_ref[at] = deep_left(rows_of(block_ref.at[0, at], 0, size, width))
        for copy in arriving:
            copy.wait()

        def line(at):
            virtual = virt_ref[...]
            energy = energy_ref[at]
            return jnp.concatenate([virtual - energy[:1, i : i + 1] for i in range(occ_rows)], axis=1)

        row = jnp.broadcast_to(line(0), (SUBLANES, width)).T[:, :1]
        at = 0
        for slot in range(count):
            total = sum_ref[at]
            for extra in range(1, len(partials[slot])):
                total = total + sum_ref[at + extra]
            at += len(partials[slot])
            amplitude = (sign_ref[first_sign + slot] * total) / (row + line(slot + 1))
            right_ref[:, pl.ds(slot * 3 * width, 3 * width)] = deep_right(amplitude, 1)
        leaving = []
        for at in range(chunks):
            for copy in adding[at] if ahead else coming[at] + adding[at]:
                copy.wait()
            if ahead:
                left = left_ref[at]
            else:
                left = [deep_left(rows_of(block_ref.at[slot, at], 0, size, width)) for slot in range(count)]
                left = jnp.concatenate(left, axis=1)
            value = dot(left, right_ref[...], 1)
            for column in range(lines):
                lanes = value[:, column * LANES : (column + 1) * LANES]
                where = pl.ds(column, size, stride=lines)
                if last:
                    lanes = lanes + result_ref[at, where, :]
                result_ref[at, where, :] = lanes
            leaving.append(copies.start(result_ref.at[at], out_ref.at[pl.ds(at * cut, cut)]))
        for copy in leaving:
            copy.wait()

    rows = chunks * size
    out = jax.ShapeDtypeStruct((rows * lines, LANES), jnp.float32)
    scratch = [
        pltpu.VMEM((len(energies), SUBLANES, LANES), jnp.float32),
        pltpu.VMEM((len(sums) // HALVES, width, width), jnp.float32),
        pltpu.VMEM((count, chunks, cut, LANES), jnp.float32),
        pltpu.VMEM((chunks, cut, LANES), jnp.float32),
        pltpu.VMEM((width, count * 3 * width), jnp.bfloat16),
        pltpu.VMEM((chunks, size, 3 * width) if ahead else (2 * SUBLANES, LANES), jnp.bfloat16),
        pltpu.SemaphoreType.DMA((len(energies) + len(sums) + len(pieces) + 2 * chunks,)),
    ]
    return call(kernel, [signs, flags], [eps_virt], [*sums, *last, *arrays], [out], pl.ANY, scratch, limit)[0]


def after(block, *others):
    return lax.optimization_barrier((block, *others))[0]


def on_device(factors, eps_occ, eps_virt, pair_mask):
    rows, occ_rows, virt = factors.shape
    width = occ_rows * virt
    lines = width // LANES
    groups = lax.axis_size("occ")
    shares = lax.axis_size("aux")
    size = rows // CHUNKS
    cut = size * lines
    last = CHUNKS - 1
    group = lax.axis_index("occ")
    place = group % PLANE
    odd_x = place % 2 == 1
    odd_y = place // 2 == 1

    own = factors.reshape(rows * lines, LANES)
    energies = jnp.zeros((SUBLANES * LANES,), jnp.float32).at[:occ_rows].set(eps_occ)
    energies = energies.reshape(SUBLANES, LANES)

    def part(whole, at):
        return whole[at * cut : (at + 1) * cut]

    def within(block, moves):
        planes = range(0, groups, PLANE)
        return lax.ppermute(block, "occ", [(g + a, g + b) for g in planes for a, b in moves])

    def up(block):
        return lax.ppermute(block, "occ", [(g, g + PLANE) for g in range(groups - PLANE)])

    def totals(parts):
        if shares == 2:
            return [parts, [lax.ppermute(part, "aux", [(0, 1), (1, 0)]) for part in parts]]
        return [[lax.psum(part, "aux") for part in parts]]

    first_sent = jnp.concatenate([part(own, 0), energies])
    def choices(sent):
        group_then, mask_row, _ = lax.optimization_barrier((group, pair_mask[0], sent))
        place_then = group_then % PLANE

        def sign(offset):
            flag = jnp.sum(jnp.where(jnp.arange(1, PLANE + 1) == offset, mask_row, 0))
            return jnp.where((group_then >= offset) & (flag > 0), -1.0, 0.0).astype(jnp.float32)

        near = jnp.where(place_then % 2 == 1, 1, PLANE - 1)
        signs = [jnp.float32(-1.0), sign(PLANE), sign(near), sign(PLANE // 2), sign(PLANE - near)]
        up_then = place_then // 2 == 1
        flags = [
            1 - place_then % 2,
            1 - place_then // 2,
            jnp.where(up_then, 0, 1 + place_then),
            jnp.where(up_then, place_then - 1, 0),
        ]
        return jnp.stack(signs), jnp.stack(flags).astype(jnp.int32)

    def add(first_sign, partials, slots, carriers, before=None, limit=VMEM_LIMIT):
        return contract(
            partials, slots, signs, first_sign, carriers, flags, eps_virt[None, :], size, before, limit
        )

    from_own = [first_sent]
    from_z = [up(first_sent)]
    up_x = within(first_sent, [(0, 1), (2, 3), (1, 0)])
    up_y = within(first_sent, [(0, 2), (1, 3)])
    high, low, *made = prepare(own, energies, rows, width)
    partial_own = made[:HALVES]
    from_own += made[HALVES:]
    turned = (high, low)
    sums_own = totals(partial_own)
    swap_x, swap_y = [], []
    passed = [partial_own[0]]
    for at in range(CHUNKS):
        came = after(from_z[at], *passed)
        if at < last:
            from_z.append(up(after(from_own[at + 1], came)))
            up_part = after(from_own[at + 1], came)
            send_x, send_y = jnp.where(odd_x, came, up_part), jnp.where(odd_y, came, up_part)
            send_x = after(send_x, swap_x[at - 1] if at else up_x)
            send_y = after(send_y, swap_y[at - 1] if at else up_y)
            if at == 0:
                signs, flags = choices((send_x, send_y))
            swap_x.append(within(send_x, [(0, 1), (1, 0), (2, 3), (3, 2)]))
            swap_y.append(within(send_y, [(0, 2), (2, 0), (1, 3), (3, 1)]))
        else:
            cycle = within(after(turning, came, swap_x[last - 1]), [(0, 1), (1, 3), (3, 2), (2, 0)])
            send_x = after(jnp.where(odd_x, came, swap_y[0]), swap_x[last - 1])
            send_y = after(jnp.where(odd_y, came, up_x), swap_y[last - 1])
            swap_x.append(within(send_x, [(0, 1), (1, 0), (2, 3), (3, 2)]))
            swap_y.append(within(send_y, [(0, 2), (2, 0), (1, 3), (3, 1)]))
        passed = []
        if at == 1:
            passed = [signs, flags]
            middle = (place == 1) | (place == 2)
            turning = jnp.where(middle, swap_x[1], swap_y[1])
        if at == 2:
            passed.append(turning)

    cross = within(jnp.where(place == 2, swap_x[0], swap_y[0]), [(2, 0), (3, 2)])
    swap_d = within(swap_y[2], [(0, 1), (1, 0), (2, 3), (3, 2)])
    last_d = within(swap_y[3], [(0, 1), (1, 0)])

    def pieces_of(first, swaps, choice, base):
        arrays = [first, *swaps]
        return [Piece(((arrays[at], base), (arrays[at + 1], base)), choice) for at in range(CHUNKS)]

    def whole(array, base):
        return Piece(((array, base),))

    slot_own = [whole(own, at * cut) for at in range(CHUNKS)]
    slot_z = [whole(block, 0) for block in from_z]
    slot_x = pieces_of(up_x, swap_x, 0, 0)
    slot_y = pieces_of(up_y, swap_y, 1, 0)
    slot_d = [
        Piece(((swap_y[last], 0), (cross, 0), (swap_x[last], 0)), 2),
        Piece(((cycle, 0), (cross, 0), (swap_x[last], 0)), 3),
        Piece(((cycle, 0), (swap_d, 0)), 1),
        Piece(((swap_d, 0), (last_d, 0)), 1),
    ]
    eps_x = pieces_of(up_x, swap_x, 0, cut)[0]
    eps_y = pieces_of(up_y, swap_y, 1, cut)[0]
    eps_d = Piece(((swap_y[last], cut), (cross, cut), (swap_x[last], cut)), 2)

    partial_z, *early = integrate(
        turned, [slot_z, slot_x[:last], slot_y[:last]], [0, 0, 0], flags, size, width
    )
    own_eps = whole(first_sent, cut)
    partial_x, partial_y = integrate(
        turned, [slot_x[last:], slot_y[last:]], [last, last], flags, size, width, early
    )
    gradient = add(
        0,
        [after(sums_own, cycle), totals(partial_z), totals(partial_x), totals(partial_y)],
        [slot_own, slot_z, slot_x, slot_y],
        [own_eps, own_eps, whole(from_z[0], cut), eps_x, eps_y],
    )
    turned = after(turned, gradient)
    half = CHUNKS // 2
    partial_d = integrate(turned, [slot_d[:half]], [0], flags, size, width)
    (partial_d,) = integrate(turned, [slot_d[half:]], [half], flags, size, width, partial_d, LAST_LIMIT)
    gradient = add(4, [totals(partial_d)], [slot_d], [own_eps, eps_d], gradient, LAST_LIMIT)
    return gradient.reshape(rows, occ_rows, virt)


def solution(mesh):
    if mesh.shape["occ"] % PLANE:
        raise ValueError("incomplete plane")
    in_specs = (P("aux", "occ", None), P("occ"), P(), P("occ", None))
    out_specs = P("aux", "occ", None)
    return jax.shard_map(
        on_device, mesh=mesh, in_specs=in_specs, out_specs=out_specs, check_vma=False
    )
```

```python
import dataclasses
import functools

import jax
import jax.numpy as jnp
from jax import lax
from jax.experimental import pallas as pl
from jax.experimental.pallas import tpu as pltpu
from jax.sharding import PartitionSpec as P

LANES = 128
SUBLANES = 8
PLANE = 4
CHUNKS = 4
VMEM_LIMIT = 32 * 1024 * 1024
FIRST_LIMIT = 60 * 1024 * 1024
LAST_LIMIT = 16 * 1024 * 1024
HALVES = 2


def split(value):
    high = value.astype(jnp.bfloat16)
    low = (value - high.astype(jnp.float32)).astype(jnp.bfloat16)
    return high, low


def deep_left(value):
    high, low = split(value)
    return jnp.concatenate([high, low, high], axis=1)


def deep_right(value, axis=0):
    high, low = split(value)
    return jnp.concatenate([high, high, low], axis=axis)


def dot(left, right, axis=0):
    numbers = (((1,), (axis,)), ((), ()))
    return lax.dot_general(left, right, numbers, preferred_element_type=jnp.float32)


def rows_of(ref, start, count, width):
    lines = width // LANES
    columns = [ref[pl.ds(start * lines + at, count, stride=lines), :] for at in range(lines)]
    return jnp.concatenate(columns, axis=1)


def distinct(arrays):
    return list({id(array): array for array in arrays}.values())


class Copies:
    def __init__(self, semaphores):
        self.semaphores = semaphores
        self.used = 0

    def start(self, source, target):
        copy = pltpu.make_async_copy(source, target, self.semaphores.at[self.used])
        self.used += 1
        copy.start()
        return copy

    def start_piece(self, piece, ref_of, choices, count, target):
        made = []
        for array, base in piece.places:
            source = ref_of[id(array)].at[pl.ds(base, count)]
            made.append(pltpu.make_async_copy(source, target, self.semaphores.at[self.used]))
        self.used += 1
        if len(made) == 1:
            made[0].start()
        else:
            for at, copy in enumerate(made):
                pl.when(choices[piece.choice] == at)(copy.start)
        return made[0]


@dataclasses.dataclass(frozen=True)
class Piece:
    places: tuple
    choice: int = 0


def call(kernel, smem, vmem, anywhere, outputs, out_space, scratch, limit=VMEM_LIMIT):
    spaces = [pltpu.SMEM] * len(smem) + [pltpu.VMEM] * len(vmem) + [pl.ANY] * len(anywhere)
    return pl.pallas_call(
        kernel,
        out_shape=outputs,
        in_specs=[pl.BlockSpec(memory_space=space) for space in spaces],
        out_specs=[pl.BlockSpec(memory_space=out_space)] * len(outputs),
        scratch_shapes=scratch,
        compiler_params=pltpu.CompilerParams(vmem_limit_bytes=limit),
        cost_estimate=pl.CostEstimate(flops=0, bytes_accessed=0, transcendentals=0),
    )(*smem, *vmem, *anywhere)


def prepare(own, energies, rows, width):
    size = rows // CHUNKS
    cut = size * width // LANES
    share = width // HALVES

    def kernel(energy_ref, own_ref, high_out, low_out, *refs):
        integral_outs, refs = refs[:HALVES], refs[HALVES:]
        sent_refs = refs[: CHUNKS - 1]
        block_ref, turned_ref, integrals_ref, semaphores = refs[CHUNKS - 1 :]
        copies = Copies(semaphores)
        coming = [copies.start(own_ref.at[pl.ds(at * cut, cut)], block_ref.at[at]) for at in range(CHUNKS)]
        leaving = [copies.start(energy_ref, ref.at[pl.ds(cut, SUBLANES)]) for ref in sent_refs]
        for at in range(CHUNKS):
            coming[at].wait()
            if at:
                leaving.append(copies.start(block_ref.at[at], sent_refs[at - 1].at[pl.ds(0, cut)]))
            block = rows_of(block_ref.at[at], 0, size, width)
            high, low = split(block.T)
            turned_ref[0, at] = high
            turned_ref[1, at] = low
            leaving.append(copies.start(turned_ref.at[0, at], high_out.at[at]))
            leaving.append(copies.start(turned_ref.at[1, at], low_out.at[at]))
            value = dot(jnp.concatenate([high, low, high], axis=1), deep_right(block))
            integrals_ref[...] = integrals_ref[...] + value if at else value
        for at, out_ref in enumerate(integral_outs):
            leaving.append(copies.start(integrals_ref.at[pl.ds(at * share, share)], out_ref))
        for copy in leaving:
            copy.wait()

    turned = jax.ShapeDtypeStruct((CHUNKS, width, size), jnp.bfloat16)
    square = jax.ShapeDtypeStruct((share, width), jnp.float32)
    sent = jax.ShapeDtypeStruct((cut + SUBLANES, LANES), jnp.float32)
    scratch = [
        pltpu.VMEM((CHUNKS, cut, LANES), jnp.float32),
        pltpu.VMEM((2, CHUNKS, width, size), jnp.bfloat16),
        pltpu.VMEM((width, width), jnp.float32),
        pltpu.SemaphoreType.DMA((5 * CHUNKS + HALVES,)),
    ]
    outs = [turned, turned] + [square] * HALVES + [sent] * (CHUNKS - 1)
    return call(kernel, [], [energies], [own], outs, pl.ANY, scratch, FIRST_LIMIT)


def arrays_of(pieces):
    return distinct([array for piece in pieces for array, _ in piece.places])


def integrate(turned, slots, first, flags, size, width, before=(), limit=VMEM_LIMIT):
    cut = size * width // LANES
    count = len(slots)
    pieces = [piece for slot in slots for piece in slot]
    arrays = arrays_of(pieces)
    numbers = [list(range(start, start + len(slot))) for slot, start in zip(slots, first)]
    needed = sorted({number for some in numbers for number in some})
    before = [part for parts in before for part in parts]
    share = width // HALVES

    def kernel(flag_ref, *refs):
        given = iter(refs)
        high_ref, low_ref = next(given), next(given)
        before_refs = [next(given) for _ in before]
        ref_of = {id(array): next(given) for array in arrays}
        outs = [[next(given) for _ in range(HALVES)] for _ in range(count)]
        turned_ref, block_ref, before_ref, semaphores = given
        copies = Copies(semaphores)
        coming, turning = [], {}

        def turn(number):
            if number not in turning:
                at = needed.index(number)
                turning[number] = [
                    copies.start(high_ref.at[number], turned_ref.at[at, 0]),
                    copies.start(low_ref.at[number], turned_ref.at[at, 1]),
                ]

        at = 0
        for slot in range(count):
            for number, piece in zip(numbers[slot], slots[slot]):
                turn(number)
                coming.append(copies.start_piece(piece, ref_of, flag_ref, cut, block_ref.at[at]))
                at += 1
        adding = [
            copies.start(ref, before_ref.at[at // HALVES, pl.ds(at % HALVES * share, share)])
            for at, ref in enumerate(before_refs)
        ]
        at = 0
        for slot in range(count):
            total = None
            for place, number in enumerate(numbers[slot]):
                for copy in turning.pop(number, []):
                    copy.wait()
                coming[at].wait()
                there = needed.index(number)
                high, low = turned_ref[there, 0], turned_ref[there, 1]
                left = jnp.concatenate([high, low, high], axis=1)
                value = dot(left, deep_right(rows_of(block_ref.at[at], 0, size, width)))
                total = total + value if place else value
                at += 1
            if before:
                for number in range(HALVES):
                    adding[slot * HALVES + number].wait()
                total = total + before_ref[slot]
            for number, out_ref in enumerate(outs[slot]):
                out_ref[...] = total[number * share : (number + 1) * share]

    out = [jax.ShapeDtypeStruct((share, width), jnp.float32)] * (HALVES * count)
    scratch = [
        pltpu.VMEM((len(needed), 2, width, size), jnp.bfloat16),
        pltpu.VMEM((len(pieces), cut, LANES), jnp.float32),
        pltpu.VMEM((max(len(before) // HALVES, 1), width, width), jnp.float32),
        pltpu.SemaphoreType.DMA((2 * len(needed) + len(pieces) + len(before),)),
    ]
    made = call(kernel, [flags], [], [*turned, *before, *arrays], out, pltpu.VMEM, scratch, limit)
    return [made[slot * HALVES : (slot + 1) * HALVES] for slot in range(count)]


def contract(partials, slots, signs, first_sign, energies, flags, eps_virt, size, before=None, limit=VMEM_LIMIT):
    count = len(slots)
    chunks = len(slots[0])
    virt = eps_virt.shape[1]
    width = partials[0][0][0].shape[1]
    share = width // HALVES
    occ_rows = width // virt
    lines = width // LANES
    cut = size * lines
    sums = [part for slot in partials for term in slot for part in term]
    pieces = [piece for slot in slots for piece in slot]
    arrays = arrays_of([*pieces, *energies])
    last = [before] if before is not None else []
    ahead = count == 1

    def kernel(*refs):
        given = iter(refs)
        sign_ref, flag_ref, virt_ref = next(given), next(given), next(given)
        sum_refs = [next(given) for _ in sums]
        before_refs = [next(given) for _ in last]
        ref_of = {id(array): next(given) for array in arrays}
        out_ref, energy_ref, sum_ref, block_ref, result_ref, right_ref, left_ref, semaphores = given
        copies = Copies(semaphores)
        arriving = [
            copies.start_piece(piece, ref_of, flag_ref, SUBLANES, energy_ref.at[at])
            for at, piece in enumerate(energies)
        ]
        arriving += [
            copies.start(ref, sum_ref.at[at // HALVES, pl.ds(at % HALVES * share, share)])
            for at, ref in enumerate(sum_refs)
        ]
        coming = [
            [
                copies.start_piece(slots[slot][at], ref_of, flag_ref, cut, block_ref.at[slot, at])
                for slot in range(count)
            ]
            for at in range(chunks)
        ]
        adding = [
            [copies.start(ref.at[pl.ds(at * cut, cut)], result_ref.at[at]) for ref in before_refs]
            for at in range(chunks)
        ]
        if ahead:
            for at in range(chunks):
                coming[at][0].wait()
                left_ref[at] = deep_left(rows_of(block_ref.at[0, at], 0, size, width))
        for copy in arriving:
            copy.wait()

        def line(at):
            virtual = virt_ref[...]
            energy = energy_ref[at]
            return jnp.concatenate([virtual - energy[:1, i : i + 1] for i in range(occ_rows)], axis=1)

        row = jnp.broadcast_to(line(0), (SUBLANES, width)).T[:, :1]
        at = 0
        for slot in range(count):
            total = sum_ref[at]
            for extra in range(1, len(partials[slot])):
                total = total + sum_ref[at + extra]
            at += len(partials[slot])
            amplitude = (sign_ref[first_sign + slot] * total) / (row + line(slot + 1))
            right_ref[:, pl.ds(slot * 3 * width, 3 * width)] = deep_right(amplitude, 1)
        leaving = []
        for at in range(chunks):
            for copy in adding[at] if ahead else coming[at] + adding[at]:
                copy.wait()
            if ahead:
                left = left_ref[at]
            else:
                left = [deep_left(rows_of(block_ref.at[slot, at], 0, size, width)) for slot in range(count)]
                left = jnp.concatenate(left, axis=1)
            value = dot(left, right_ref[...], 1)
            for column in range(lines):
                lanes = value[:, column * LANES : (column + 1) * LANES]
                where = pl.ds(column, size, stride=lines)
                if last:
                    lanes = lanes + result_ref[at, where, :]
                result_ref[at, where, :] = lanes
            leaving.append(copies.start(result_ref.at[at], out_ref.at[pl.ds(at * cut, cut)]))
        for copy in leaving:
            copy.wait()

    rows = chunks * size
    out = jax.ShapeDtypeStruct((rows * lines, LANES), jnp.float32)
    scratch = [
        pltpu.VMEM((len(energies), SUBLANES, LANES), jnp.float32),
        pltpu.VMEM((len(sums) // HALVES, width, width), jnp.float32),
        pltpu.VMEM((count, chunks, cut, LANES), jnp.float32),
        pltpu.VMEM((chunks, cut, LANES), jnp.float32),
        pltpu.VMEM((width, count * 3 * width), jnp.bfloat16),
        pltpu.VMEM((chunks, size, 3 * width) if ahead else (2 * SUBLANES, LANES), jnp.bfloat16),
        pltpu.SemaphoreType.DMA((len(energies) + len(sums) + len(pieces) + 2 * chunks,)),
    ]
    return call(kernel, [signs, flags], [eps_virt], [*sums, *last, *arrays], [out], pl.ANY, scratch, limit)[0]


def after(block, *others):
    return lax.optimization_barrier((block, *others))[0]


def on_device(factors, eps_occ, eps_virt, pair_mask):
    rows, occ_rows, virt = factors.shape
    width = occ_rows * virt
    lines = width // LANES
    groups = lax.axis_size("occ")
    shares = lax.axis_size("aux")
    size = rows // CHUNKS
    cut = size * lines
    last = CHUNKS - 1
    group = lax.axis_index("occ")
    place = group % PLANE
    odd_x = place % 2 == 1
    odd_y = place // 2 == 1

    own = factors.reshape(rows * lines, LANES)
    energies = jnp.zeros((SUBLANES * LANES,), jnp.float32).at[:occ_rows].set(eps_occ)
    energies = energies.reshape(SUBLANES, LANES)

    def part(whole, at):
        return whole[at * cut : (at + 1) * cut]

    def within(block, moves):
        planes = range(0, groups, PLANE)
        return lax.ppermute(block, "occ", [(g + a, g + b) for g in planes for a, b in moves])

    def up(block):
        return lax.ppermute(block, "occ", [(g, g + PLANE) for g in range(groups - PLANE)])

    def totals(parts):
        if shares == 2:
            return [parts, [lax.ppermute(part, "aux", [(0, 1), (1, 0)]) for part in parts]]
        return [[lax.psum(part, "aux") for part in parts]]

    first_sent = jnp.concatenate([part(own, 0), energies])
    def choices(sent):
        group_then, mask_row, _ = lax.optimization_barrier((group, pair_mask[0], sent))
        place_then = group_then % PLANE

        def sign(offset):
            flag = jnp.sum(jnp.where(jnp.arange(1, PLANE + 1) == offset, mask_row, 0))
            return jnp.where((group_then >= offset) & (flag > 0), -1.0, 0.0).astype(jnp.float32)

        near = jnp.where(place_then % 2 == 1, 1, PLANE - 1)
        signs = [jnp.float32(-1.0), sign(PLANE), sign(near), sign(PLANE // 2), sign(PLANE - near)]
        up_then = place_then // 2 == 1
        flags = [
            1 - place_then % 2,
            1 - place_then // 2,
            jnp.where(up_then, 0, 1 + place_then),
            jnp.where(up_then, place_then - 1, 0),
        ]
        return jnp.stack(signs), jnp.stack(flags).astype(jnp.int32)

    def add(first_sign, partials, slots, carriers, before=None, limit=VMEM_LIMIT):
        return contract(
            partials, slots, signs, first_sign, carriers, flags, eps_virt[None, :], size, before, limit
        )

    from_own = [first_sent]
    from_z = [up(first_sent)]
    up_x = within(first_sent, [(0, 1), (2, 3), (1, 0)])
    up_y = within(first_sent, [(0, 2), (1, 3)])
    high, low, *made = prepare(own, energies, rows, width)
    partial_own = made[:HALVES]
    from_own += made[HALVES:]
    turned = (high, low)
    sums_own = totals(partial_own)
    swap_x, swap_y = [], []
    passed = [partial_own[0]]
    for at in range(CHUNKS):
        came = after(from_z[at], *passed)
        if at < last:
            from_z.append(up(after(from_own[at + 1], came)))
            up_part = after(from_own[at + 1], came)
            send_x, send_y = jnp.where(odd_x, came, up_part), jnp.where(odd_y, came, up_part)
            send_x = after(send_x, swap_x[at - 1] if at else up_x)
            send_y = after(send_y, swap_y[at - 1] if at else up_y)
            if at == 0:
                signs, flags = choices((send_x, send_y))
            swap_x.append(within(send_x, [(0, 1), (1, 0), (2, 3), (3, 2)]))
            swap_y.append(within(send_y, [(0, 2), (2, 0), (1, 3), (3, 1)]))
        else:
            cycle = within(after(turning, came, swap_x[last - 1]), [(0, 1), (1, 3), (3, 2), (2, 0)])
            send_x = after(jnp.where(odd_x, came, swap_y[0]), swap_x[last - 1])
            send_y = after(jnp.where(odd_y, came, up_x), swap_y[last - 1])
            swap_x.append(within(send_x, [(0, 1), (1, 0), (2, 3), (3, 2)]))
            swap_y.append(within(send_y, [(0, 2), (2, 0), (1, 3), (3, 1)]))
        passed = []
        if at == 1:
            passed = [signs, flags]
            middle = (place == 1) | (place == 2)
            turning = jnp.where(middle, swap_x[1], swap_y[1])
        if at == 2:
            passed.append(turning)

    cross = within(jnp.where(place == 2, swap_x[0], swap_y[0]), [(2, 0), (3, 2)])
    swap_d = within(swap_y[2], [(0, 1), (1, 0), (2, 3), (3, 2)])
    last_d = within(swap_y[3], [(0, 1), (1, 0)])

    def pieces_of(first, swaps, choice, base):
        arrays = [first, *swaps]
        return [Piece(((arrays[at], base), (arrays[at + 1], base)), choice) for at in range(CHUNKS)]

    def whole(array, base):
        return Piece(((array, base),))

    slot_own = [whole(own, at * cut) for at in range(CHUNKS)]
    slot_z = [whole(block, 0) for block in from_z]
    slot_x = pieces_of(up_x, swap_x, 0, 0)
    slot_y = pieces_of(up_y, swap_y, 1, 0)
    slot_d = [
        Piece(((swap_y[last], 0), (cross, 0), (swap_x[last], 0)), 2),
        Piece(((cycle, 0), (cross, 0), (swap_x[last], 0)), 3),
        Piece(((cycle, 0), (swap_d, 0)), 1),
        Piece(((swap_d, 0), (last_d, 0)), 1),
    ]
    eps_x = pieces_of(up_x, swap_x, 0, cut)[0]
    eps_y = pieces_of(up_y, swap_y, 1, cut)[0]
    eps_d = Piece(((swap_y[last], cut), (cross, cut), (swap_x[last], cut)), 2)

    partial_z, *early = integrate(
        turned, [slot_z, slot_x[:last], slot_y[:last]], [0, 0, 0], flags, size, width
    )
    own_eps = whole(first_sent, cut)
    partial_x, partial_y = integrate(
        turned, [slot_x[last:], slot_y[last:]], [last, last], flags, size, width, early
    )
    gradient = add(
        0,
        [after(sums_own, cycle), totals(partial_z), totals(partial_x), totals(partial_y)],
        [slot_own, slot_z, slot_x, slot_y],
        [own_eps, own_eps, whole(from_z[0], cut), eps_x, eps_y],
    )
    turned = after(turned, gradient)
    half = CHUNKS // 2
    partial_d = integrate(turned, [slot_d[:half]], [0], flags, size, width)
    (partial_d,) = integrate(turned, [slot_d[half:]], [half], flags, size, width, partial_d, LAST_LIMIT)
    gradient = add(4, [totals(partial_d)], [slot_d], [own_eps, eps_d], gradient, LAST_LIMIT)
    return gradient.reshape(rows, occ_rows, virt)


def solution(mesh):
    if mesh.shape["occ"] % PLANE:
        raise ValueError("incomplete plane")
    in_specs = (P("aux", "occ", None), P("occ"), P(), P("occ", None))
    out_specs = P("aux", "occ", None)
    return jax.shard_map(
        on_device, mesh=mesh, in_specs=in_specs, out_specs=out_specs, check_vma=False
    )
```
